32 devices in a mesh: tx: 2 (over x), ty: 4 (over y, core), mem: 4 (over z).
Axes of the slice: x: 2, y: 2, z: 4, core: 2. Of those that a mesh axis runs over, the one named last changes fastest.
Arguments:
- alpha: float32 [16, 128, 2560], P('tx', 'ty', 'mem'), may hold values from -6 to 6
- lv_sqrt: float32 [32, 32], replicated, may hold values from -1 to 1
- ens_pert: bfloat16 [80, 32, 64, 512], P('mem', None, 'tx', 'ty'), may hold values from -0.625 to 0.625
- bg_sigma: float32 [32, 64, 512], P(None, 'tx', 'ty'), may hold values from 0.1 to 1
- static_ctrl: float32 [32, 64, 512], P(None, 'tx', 'ty'), may hold values from -6 to 6
- obs_owner: int32 [262144, 1], P(('tx', 'ty', 'mem')), may hold values from 0 to 7; in each aligned block of 8192 rows (0 to 8191, 8192 to 16383, ...) at most 2048 rows name the same one
- obs_column: int32 [262144], P(('tx', 'ty', 'mem')), may hold values from 0 to 3966, as said below
- obs_level: int32 [262144], P(('tx', 'ty', 'mem')), may hold values from 0 to 30
- obs_frac: float32 [3, 262144], P(None, ('tx', 'ty', 'mem')), may hold values from 0 to 1
- innovation: float32 [262144], P(('tx', 'ty', 'mem')), may hold values from -6 to 6
- obs_rinv: float32 [262144], P(('tx', 'ty', 'mem')), may hold values from 0.5 to 8
- obs_count: int32 [32], P(('tx', 'ty', 'mem')), may hold values from 4096 to 8192, as said below
Outputs:
- grad_alpha: float32 [16, 128, 2560], P('tx', 'ty', 'mem')
- grad_static: float32 [32, 64, 512], P(None, 'tx', 'ty')
- departures: float32 [262144], P(('tx', 'ty', 'mem'))
The draws below stay inside these ranges and needn't reach their ends.
Inputs may be any that keep to these rules, and one draw needn't show every extreme that they name: `obs_owner`: tile number (tx index) * 4 + (ty index). Among one device's 8192 rows no tile is named more than 2048 times, a bound that some block reaches. `obs_column`: i * 128 + j with i < 31 and j < 127. `obs_count`: the live slots of a device are its first ones; some device has all 8192 live and some half of them.
All inputs are finite; a program needn't handle non-finite values.
Results may differ from the reference program's by a relative error of at most 0.0003.
Values sent between devices are 32-bit elements; how exact they have to be, the bound alone decides.
No kernel may reach another device: no remote copies, remote signals or barrier semaphores. Data moves between devices by JAX's collectives and lax.ppermute only.
A program may use at most 128 MiB of HBM per device.

```python
import math
import jax
import jax.numpy as jnp
import numpy as np
from jax import lax

MEMBERS = 80
LEV = 32
FX = 32
FY = 128
RATIO = 4
NSTEP = 4
OBS_DEV = 8192
NFX = 64
NFY = 512
NCX = 16
NCY = 128
TILES = 8
NOBS = 262144
CAP = 2048
N_TY = 4
DEVICES = 32


def draw_obs_column(key, part):
    key = jax.random.fold_in(key, 11)
    first, second = jax.random.split(key)
    across = jax.random.randint(first, (NOBS,), 0, FX - 1)
    along = jax.random.randint(second, (NOBS,), 0, FY - 1)
    across = across.at[0].set(FX - 2)
    along = along.at[0].set(FY - 2)
    return (across * FY + along).astype(jnp.int32)


def draw_obs_count(key, part):
    key = jax.random.fold_in(key, 12)
    counts = jax.random.randint(key, (DEVICES,), OBS_DEV // 2, OBS_DEV + 1)
    counts = counts.at[0].set(OBS_DEV).at[1].set(OBS_DEV // 2)
    return counts.astype(jnp.int32)


def touch_ends(values, rng, smallest, largest):
    longest = values.shape.index(max(values.shape))
    spots = []
    for shift in (0, 1):
        where = [jax.random.randint(jax.random.fold_in(rng, axis), (), 0, length) for axis, length in enumerate(values.shape)]
        where[longest] = (where[longest] + shift) % values.shape[longest]
        spots.append(tuple(where))
    return values.at[spots[0]].set(smallest).at[spots[1]].set(largest)


def levels(rng, dims, cuts, smallest, high):
    def one(axis_at, parts):
        heights = jax.random.uniform(jax.random.fold_in(jax.random.fold_in(rng, 6), axis_at), (parts,), jnp.float32, smallest / len(cuts), high / len(cuts))
        return jnp.repeat(jnp.exp(heights), dims[axis_at] // parts).reshape((-1,) + (1,) * (len(dims) - axis_at - 1))

    factor_of = one(*cuts[0])
    for cut in cuts[1:]:
        factor_of = factor_of * one(*cut)
    return factor_of


def deal_out(rng, own, number, rows, amount, top, bound, slope):
    order = jax.random.permutation(rng, amount)
    heavy_load, ordinary = load_shares(amount, rows * top, bound, slope, True), load_shares(amount, rows * top, bound, slope, False)
    places = jnp.arange(amount)

    def named(sizes, turn):
        used = int((sizes > 0).sum())
        fixed = max(1, used // 4)
        moved = fixed + (places - fixed + turn * (used - fixed)) % max(1, amount - fixed)
        return jnp.zeros((amount,), jnp.int32).at[order[jnp.where(places < fixed, places, moved)]].set(jnp.asarray(sizes, jnp.int32))

    sizes = jnp.where(number % 4 == 0, named(heavy_load, number // 4), named(ordinary, number - number // 4 - 1))
    mixed = jax.random.permutation(jax.random.fold_in(own, 3), amount)
    giver, sink = mixed[0:amount // 2 * 2:2], mixed[1:amount // 2 * 2:2]
    slack = jnp.minimum(sizes[giver] - 1, bound - sizes[sink]) // 2
    slack = jnp.where((giver == order[0]) | (sink == order[0]) | (sizes[sink] == 0), 0, jnp.maximum(slack, 0))
    moved = jax.random.randint(jax.random.fold_in(own, 4), (amount // 2,), 0, 1 << 20) % (slack + 1)
    sizes = sizes.at[giver].add(-moved).at[sink].add(moved)
    labels = jnp.searchsorted(jnp.cumsum(sizes), jnp.arange(rows * top), side="right").astype(jnp.int32)
    listing = labels.reshape(top, rows).T
    listing = listing[jax.random.permutation(jax.random.fold_in(own, 1), rows)]
    turn = jax.random.randint(jax.random.fold_in(own, 2), (rows, 1), 0, top)
    return jnp.take_along_axis(listing, (jnp.arange(top)[None, :] + turn) % top, axis=1)


def load_shares(amount, total, most, slope, full):
    weights = [(1 << 20) // math.isqrt(standing ** slope) + 1 for standing in range(1, amount + 1)]
    largest = most if full else min(most, max(-(-total // amount), total * weights[0] // sum(weights)))
    least = 1 if total - largest >= amount - 1 else 0
    given, rest = [largest] + [least] * (amount - 1), total - largest - least * (amount - 1)
    while rest > 0:
        candidates = [i for i in range(1, amount) if given[i] < largest] or [i for i in range(1, amount) if given[i] < most]
        pool, remaining = sum([weights[i] for i in candidates]), rest
        for i in candidates:
            extra = min(most - given[i], max(1, remaining * weights[i] // pool), rest)
            given[i] = given[i] + extra
            rest = rest - extra
    return np.array(given)


def centred(key, dims, scale, reach, shards=(), kind=jnp.bfloat16):
    values = scale * jax.random.normal(key, dims, jnp.float32)
    if shards:
        values = values * levels(key, dims, shards, -0.22, 0.18)
    return jnp.clip(values, -reach, reach).astype(kind)


def setup_inputs(seed: int = 0) -> dict:
    splits = jax.random.split(jax.random.key(seed), 13)
    alpha = centred(splits[0], (NCX, NCY, MEMBERS * LEV), 1.0, 6.0, ((0, 2), (1, 4), (2, 4)), jnp.float32)
    lv_sqrt = centred(splits[1], (LEV, LEV), LEV ** -0.5, 1.0, (), jnp.float32)
    ens_pert = centred(splits[2], (MEMBERS, LEV, NFX, NFY), MEMBERS ** -0.5, 0.625, ((0, 4), (2, 2), (3, 4)))
    bg_sigma = jnp.clip(jnp.exp(math.log(1.0) - 2.3025851 * jax.random.uniform(splits[3], (LEV, NFX, NFY), jnp.float32) ** levels(splits[3], (LEV, NFX, NFY), ((1, 2), (2, 4)), -0.2, 0.2)), 0.1, 1.0)
    static_ctrl = centred(splits[4], (LEV, NFX, NFY), 1.0, 6.0, ((1, 2), (2, 4)), jnp.float32)
    obs_owner_keys = jax.random.split(jax.random.fold_in(splits[5], 1), NOBS // OBS_DEV)
    obs_owner_turns = jax.random.permutation(jax.random.fold_in(splits[5], 3), NOBS // OBS_DEV)
    obs_owner = jax.vmap(lambda own, number: deal_out(jax.random.fold_in(splits[5], 2), own, number, OBS_DEV, TILES, 1, CAP, 1))(obs_owner_keys, obs_owner_turns).reshape((NOBS, 1))
    obs_column = draw_obs_column(jax.random.fold_in(splits[12], 71), 0)
    obs_level = touch_ends(jax.random.randint(splits[7], (NOBS,), 0, LEV - 1), jax.random.fold_in(splits[7], 1), 0, (LEV - 1) - 1).astype(jnp.int32)
    obs_frac = jnp.clip(1.0 * jax.random.uniform(splits[8], (3, NOBS), jnp.float32) ** levels(splits[8], (3, NOBS), ((1, 32),), -0.2, 0.2), 0.0, 1.0)
    innovation = centred(splits[9], (NOBS,), 1.0, 6.0, ((0, 32),), jnp.float32)
    obs_rinv = jnp.clip(jnp.exp(math.log(8.0) - 2.7725887 * jax.random.uniform(splits[10], (NOBS,), jnp.float32) ** levels(splits[10], (NOBS,), ((0, 32),), -0.2, 0.2)), 0.5, 8.0)
    obs_count = draw_obs_count(jax.random.fold_in(splits[12], 71), 0)
    return {"alpha": alpha, "lv_sqrt": lv_sqrt, "ens_pert": ens_pert, "bg_sigma": bg_sigma, "static_ctrl": static_ctrl, "obs_owner": obs_owner, "obs_column": obs_column, "obs_level": obs_level, "obs_frac": obs_frac, "innovation": innovation, "obs_rinv": obs_rinv, "obs_count": obs_count}


NU = 0.2

def diffuse(field):
    for repeat in range(NSTEP):
        near = jnp.roll(field, 1, 0) + jnp.roll(field, -1, 0) + jnp.roll(field, 1, 1) + jnp.roll(field, -1, 1)
        field = field + NU * (near - 4.0 * field)
    return field

def upsample(coarse):
    frac = jnp.arange(RATIO, dtype=jnp.float32) / RATIO
    first = (1.0 - frac)[None, :, None, None] * coarse[:, None] + frac[None, :, None, None] * jnp.roll(coarse, -1, 0)[:, None]
    first = first.reshape(NFX, NCY, LEV)
    second = (1.0 - frac)[None, None, :, None] * first[:, :, None] + frac[None, None, :, None] * jnp.roll(first, -1, 1)[:, :, None]
    second = second.reshape(NFX, NFY, LEV)
    return jnp.transpose(second, (2, 0, 1))

def coarsen_field(fine_grid):
    frac = jnp.arange(RATIO, dtype=jnp.float32) / RATIO
    grid = jnp.transpose(fine_grid, (1, 2, 0))
    grid = grid.reshape(NFX, NCY, RATIO, LEV)
    lower = lax.optimization_barrier(jnp.sum((1.0 - frac)[None, None, :, None] * grid, 2))
    upper = lax.optimization_barrier(jnp.sum(frac[None, None, :, None] * grid, 2))
    grid = lower + jnp.roll(upper, 1, 1)
    grid = grid.reshape(NCX, RATIO, NCY, LEV)
    lower = lax.optimization_barrier(jnp.sum((1.0 - frac)[None, :, None, None] * grid, 1))
    upper = lax.optimization_barrier(jnp.sum(frac[None, :, None, None] * grid, 1))
    return lower + jnp.roll(upper, 1, 0)

def reference(alpha, lv_sqrt, ens_pert, bg_sigma, static_ctrl, obs_owner, obs_column, obs_level, obs_frac, innovation, obs_rinv, obs_count):
    highest = lax.Precision.HIGHEST
    alpha_four = alpha.reshape(NCX, NCY, MEMBERS, LEV)
    vert = jnp.einsum('xykm,lm->xykl', alpha_four, lv_sqrt, precision=highest)
    smooth = jnp.moveaxis(diffuse(vert), 2, 0)

    def forward(total, pair):
        coarse, member_perturbation = pair
        return (total + upsample(coarse) * member_perturbation.astype(jnp.float32), None)
    increment, unused = lax.scan(forward, jnp.zeros((LEV, NFX, NFY), jnp.float32), (smooth, ens_pert))
    increment = increment + bg_sigma * static_ctrl
    grid_position = jnp.arange(NOBS, dtype=jnp.int32)
    device = grid_position // OBS_DEV
    live = grid_position % OBS_DEV < obs_count[device]
    owner = obs_owner[:, 0]
    row_base = owner // N_TY * FX + obs_column // FY
    col_base = owner % N_TY * FY + obs_column % FY
    hx = jnp.zeros((NOBS,), jnp.float32)
    corners = []
    for offset_x in (0, 1):
        for offset_y in (0, 1):
            for offset_l in (0, 1):
                weight_x = obs_frac[0] if offset_x else 1.0 - obs_frac[0]
                weight_y = obs_frac[1] if offset_y else 1.0 - obs_frac[1]
                weight_l = obs_frac[2] if offset_l else 1.0 - obs_frac[2]
                weight = weight_x * weight_y * weight_l
                level = obs_level + offset_l
                across = row_base + offset_x
                along = col_base + offset_y
                hx = hx + weight * increment[level, across, along]
                corners.append((level, across, along, weight))
    departure = hx - innovation
    departures = jnp.where(live, departure, 0.0)
    weighted = jnp.where(live, obs_rinv * departure, 0.0)
    adjoint_grid_values = jnp.zeros((LEV, NFX, NFY), jnp.float32)
    for level, across, along, weight in corners:
        adjoint_grid_values = adjoint_grid_values.at[level, across, along].add(weighted * weight)
    grad_static = static_ctrl + bg_sigma * adjoint_grid_values

    def backward(running_total, member_perturbation):
        return (running_total, coarsen_field(member_perturbation.astype(jnp.float32) * adjoint_grid_values))
    unused, back = lax.scan(backward, jnp.float32(0.0), ens_pert)
    smooth_back = diffuse(jnp.moveaxis(back, 0, 2))
    mixed = jnp.einsum('xykl,lm->xykm', smooth_back, lv_sqrt, precision=highest)
    grad_alpha = alpha + mixed.reshape(NCX, NCY, MEMBERS * LEV)
    return (grad_alpha, grad_static, departures)
```

```python
import functools

import jax
import jax.numpy as jnp
from jax import lax
from jax.experimental import pallas as pl
from jax.experimental.pallas import tpu as pltpu
from jax.sharding import PartitionSpec as P

RATIO = 4
NSTEP = 4


NU = 0.2


def with_halo(value, sides, width):
    for axis, dim in sides:
        count, length = (lax.axis_size(axis), value.shape[dim])
        up = [(i, (i + 1) % count) for i in range(count)]
        down = [(j, i) for i, j in up]
        last = lax.slice_in_dim(value, length - width, length, axis=dim)
        first = lax.slice_in_dim(value, 0, width, axis=dim)
        before = lax.ppermute(last, axis, up)
        after = lax.ppermute(first, axis, down)
        value = jnp.concatenate([before, value, after], axis=dim)
    return value


def passed_along(value, axis, by):
    count = lax.axis_size(axis)
    return lax.ppermute(value, axis, [(i, (i + by) % count) for i in range(count)])


def diffusion_step(padded):
    center = padded[1:-1, 1:-1]
    near = padded[2:, 1:-1] + padded[:-2, 1:-1] + padded[1:-1, 2:] + padded[1:-1, :-2]
    return center + NU * (near - 4.0 * center)


def diffuse(field):
    for repeat in range(NSTEP):
        padded = with_halo(field, (("tx", 0), ("ty", 1)), 1)
        field = diffusion_step(padded)
    return field


def interpolation_matrix(fine_count, coarse_count):
    index = jnp.arange(fine_count, dtype=jnp.int32)
    lower = index // RATIO
    frac = (index % RATIO).astype(jnp.float32) / RATIO
    target = jnp.arange(coarse_count + 1, dtype=jnp.int32)
    low_part = jnp.where(target[None, :] == lower[:, None], 1.0 - frac[:, None], 0.0)
    high_part = jnp.where(target[None, :] == lower[:, None] + 1, frac[:, None], 0.0)
    return low_part + high_part


BLOCK = 256
LANES = 128
WINDOW = 12
HALF = jnp.bfloat16


def split_two(value):
    high = value.astype(HALF)
    return high, (value - high.astype(jnp.float32)).astype(HALF)


def dot_nt(a, b):
    return lax.dot_general(a, b, (((1,), (1,)), ((), ())), preferred_element_type=jnp.float32)


def dot_nn(a, b):
    return jnp.dot(a, b, preferred_element_type=jnp.float32)


def iota(shape, dim):
    return lax.broadcasted_iota(jnp.int32, shape, dim)


def pack_kernel(
    tiles, levels, plane, capacity,
    count_ref, owner_ref, column_ref, level_ref, frac_ref, innov_ref, rinv_ref,
    out_ref, target_ref,
    carry, total, gathered,
):
    blocks = owner_ref.shape[0] * LANES // BLOCK
    keys = tiles * levels
    deep = capacity // BLOCK
    slot_rows = tiles * deep
    group = 4
    count = count_ref[0]

    def row_of(ref, j):
        pair = ref[pl.ds(2 * j, 2), :]
        return jnp.concatenate([pair[0:1], pair[1:2]], 1)

    def onehot(j):
        live = iota((1, BLOCK), 1) + j * BLOCK < count
        key = jnp.where(live, row_of(owner_ref, j) * levels + row_of(level_ref, j), -1)
        return live, iota((keys, BLOCK), 0) == key

    ones = jnp.ones((BLOCK, LANES), HALF)
    total[...] = jnp.zeros_like(total)

    def count_block(j, unused):
        live, mask = onehot(j)
        total[...] += dot_nn(jnp.where(mask, 1.0, 0.0).astype(HALF), ones)
        return unused

    lax.fori_loop(0, blocks, count_block, 0)
    high = jnp.floor(total[...] * (1.0 / LANES))
    low = total[...] - high * LANES
    row_key, col_key = iota((keys, keys), 0), iota((keys, keys), 1)
    before = jnp.where((col_key < row_key) & (col_key // levels == row_key // levels), 1.0, 0.0).astype(HALF)
    start = dot_nn(before, high.astype(HALF)) * LANES + dot_nn(before, low.astype(HALF))
    carry[...] = start + ((iota((keys, LANES), 0) // levels) * capacity).astype(jnp.float32)

    earlier = jnp.where(iota((BLOCK, BLOCK), 0) < iota((BLOCK, BLOCK), 1), 1.0, 0.0).astype(HALF)
    prefix = jnp.concatenate([earlier, ones], 1)
    gathered[...] = jnp.zeros_like(gathered)

    def place(j):
        live, mask = onehot(j)
        ranks = dot_nn(jnp.where(mask, 1.0, 0.0).astype(HALF), prefix)
        now = carry[...]
        here = ranks[:, :BLOCK] + jnp.concatenate([now] * (BLOCK // LANES), 1)
        carry[...] = now + ranks[:, BLOCK:]
        slot = jnp.sum(jnp.where(mask, here, 0.0), 0, keepdims=True)
        target = jnp.where(live, slot.astype(jnp.int32), -1)
        target_ref[pl.ds(2 * j, 2), :] = jnp.concatenate([target[:, :LANES], target[:, LANES:]], 0)
        rows = jnp.where(iota((slot_rows, BLOCK), 0) == (target >> 8), 1.0, 0.0).astype(HALF)
        lanes = jnp.where(iota((BLOCK, BLOCK), 0) == (target & (BLOCK - 1)), 1.0, 0.0).astype(HALF)
        column = row_of(column_ref, j)
        frac = frac_ref[:, pl.ds(pl.multiple_of(j * BLOCK, BLOCK), BLOCK)]
        terms = []
        for value in (frac[0:1], frac[1:2], frac[2:3], row_of(innov_ref, j), row_of(rinv_ref, j)):
            terms.extend(split_two(jnp.broadcast_to(value, (16, BLOCK))))
        for value in (row_of(level_ref, j), column >> 7, column & (LANES - 1)):
            terms.append(jnp.broadcast_to(value.astype(jnp.float32), (16, BLOCK)).astype(HALF))
        spread = [rows * jnp.concatenate([term] * (slot_rows // 16), 0) for term in terms]
        return jnp.concatenate(spread, 0), lanes

    def scatter_group(g, unused):
        placed = [place(g * group + i) for i in range(group)]
        left = jnp.concatenate([a for a, b in placed], 1)
        right = jnp.concatenate([b for a, b in placed], 1)
        gathered[...] += dot_nt(left, right)
        return unused

    lax.fori_loop(0, blocks // group, scatter_group, 0)

    def part(index, tile):
        begin = index * slot_rows + tile * deep
        return gathered[begin:begin + deep, :]

    for tile in range(tiles):
        for p in range(5):
            out_ref[tile, p * deep:(p + 1) * deep, :] = part(2 * p, tile) + part(2 * p + 1, tile)
        base = part(10, tile) * plane + part(11, tile) * LANES + part(12, tile)
        out_ref[tile, 5 * deep:6 * deep, :] = base


def pack(tiles, levels, plane, capacity, count, owner, column, level, frac, innov, rinv):
    slots = owner.shape[0]
    rows = slots // LANES
    deep = capacity // BLOCK
    vmem = pl.BlockSpec(memory_space=pltpu.VMEM)
    return pl.pallas_call(
        functools.partial(pack_kernel, tiles, levels, plane, capacity),
        out_shape=(
            jax.ShapeDtypeStruct((tiles, 6 * deep, BLOCK), jnp.float32),
            jax.ShapeDtypeStruct((rows, LANES), jnp.int32),
        ),
        in_specs=[pl.BlockSpec(memory_space=pltpu.SMEM)] + [vmem] * 6,
        out_specs=(vmem, vmem),
        scratch_shapes=[
            pltpu.VMEM((tiles * levels, LANES), jnp.float32),
            pltpu.VMEM((tiles * levels, LANES), jnp.float32),
            pltpu.VMEM((13 * tiles * deep, BLOCK), jnp.float32),
        ],
        compiler_params=pltpu.CompilerParams(vmem_limit_bytes=40 << 20),
        cost_estimate=pl.CostEstimate(flops=8 << 30, bytes_accessed=1 << 20, transcendentals=0),
        name="pack",
    )(count, *[a.reshape(rows, LANES) for a in (owner, column, level)], frac,
      *[a.reshape(rows, LANES) for a in (innov, rinv)])


def stencil_kernel(field_ref, incoming_ref, dep_ref, adj_ref, field_t, row_hi, row_lo, adjoint):
    levels, fine_x, fine_y = field_ref.shape
    sources, packed_rows, block = incoming_ref.shape
    deep = packed_rows // 6
    plane = fine_x * fine_y
    chunk = LANES // fine_x
    chunks = levels // chunk
    span = WINDOW // chunk
    width = WINDOW * fine_x
    adjoint[...] = jnp.zeros_like(adjoint)
    field_t[...] = jnp.zeros_like(field_t)
    for g in range(chunks):
        turned = field_ref[g * chunk:(g + 1) * chunk].reshape(LANES, fine_y).T
        high, low = split_two(turned)
        field_t[:fine_y, g * LANES:(g + 1) * LANES] = high
        field_t[fine_y:, g * LANES:(g + 1) * LANES] = low

    def one_block(q, unused):
        source, at = q // deep, q % deep

        def row(p):
            return incoming_ref[source, pl.ds(p * deep + at, 1), :]

        rinv = row(4)
        used = rinv > 0.0
        base = row(5)
        level = jnp.floor(base * (1.0 / plane))
        rest = base - level * plane
        across = jnp.floor(rest * (1.0 / fine_y))
        along = rest - across * fine_y
        lowest = jnp.min(jnp.where(used, level, float(levels)))
        highest = jnp.max(jnp.where(used, level, -1.0))

        @pl.when(highest >= 0.0)
        def _():
            frac_x, frac_y, frac_l = row(0), row(1), row(2)
            first = lowest.astype(jnp.int32) // chunk
            last = (highest.astype(jnp.int32) + 1) // chunk
            windows = (last - first) // span + 1
            rows_x = iota((fine_x, block), 0).astype(jnp.float32)
            pick_x = jnp.where(rows_x == across, 1.0 - frac_x, 0.0) + jnp.where(rows_x == across + 1.0, frac_x, 0.0)

            def at_window(w):
                return pl.ds(pl.multiple_of((first + w * span) * LANES, LANES), width)

            def forward(w, acc):
                bottom = ((first + w * span) * chunk).astype(jnp.float32)
                offset = level - bottom
                picks = []
                for g in range(WINDOW):
                    pick_l = jnp.where(offset == float(g), 1.0 - frac_l, 0.0) + jnp.where(offset == float(g - 1), frac_l, 0.0)
                    picks.append(pick_x * pick_l)
                high, low = split_two(jnp.concatenate(picks, 0))
                where = at_window(w)
                row_hi[where, :] = high
                row_lo[where, :] = low
                both = field_t[:, where]
                twice = dot_nn(both, high)
                return acc + (twice[:fine_y] + twice[fine_y:]) + dot_nn(both[:fine_y], low)

            picked = lax.fori_loop(0, windows, forward, jnp.zeros((fine_y, block), jnp.float32))
            rows_y = iota((fine_y, block), 0).astype(jnp.float32)
            pick_y = jnp.where(rows_y == along, 1.0 - frac_y, 0.0) + jnp.where(rows_y == along + 1.0, frac_y, 0.0)
            departure = jnp.sum(picked * pick_y, 0, keepdims=True) - row(3)
            dep_ref[source, pl.ds(at, 1), :] = departure
            high, low = split_two(pick_y * (rinv * departure))
            both = jnp.concatenate([high, low], 0)

            def backward(w, unused):
                where = at_window(w)
                adjoint[where, :] += dot_nt(row_hi[where, :], both)
                adjoint[where, :fine_y] += dot_nt(row_lo[where, :], high)
                return unused

            lax.fori_loop(0, windows, backward, 0)

        return unused

    dep_ref[...] = jnp.zeros_like(dep_ref)
    lax.fori_loop(0, sources * deep, one_block, 0)
    rows = levels * fine_x
    adj_ref[...] = (adjoint[:rows, :fine_y] + adjoint[:rows, fine_y:]).reshape(levels, fine_x, fine_y)


def stencil(field, incoming):
    levels, fine_x, fine_y = field.shape
    sources, packed_rows, block = incoming.shape
    rows = levels * fine_x + WINDOW * fine_x
    vmem = pl.BlockSpec(memory_space=pltpu.VMEM)
    return pl.pallas_call(
        stencil_kernel,
        out_shape=(
            jax.ShapeDtypeStruct((sources, packed_rows // 6, block), jnp.float32),
            jax.ShapeDtypeStruct(field.shape, jnp.float32),
        ),
        in_specs=[vmem, vmem],
        out_specs=(vmem, vmem),
        scratch_shapes=[
            pltpu.VMEM((2 * fine_y, rows), HALF),
            pltpu.VMEM((rows, block), HALF),
            pltpu.VMEM((rows, block), HALF),
            pltpu.VMEM((rows, 2 * fine_y), jnp.float32),
        ],
        compiler_params=pltpu.CompilerParams(vmem_limit_bytes=40 << 20),
        cost_estimate=pl.CostEstimate(flops=16 << 30, bytes_accessed=1 << 20, transcendentals=0),
        name="stencil",
    )(field, incoming)


def unpack_kernel(target_ref, table_ref, out_ref):
    rows = target_ref.shape[0]
    target = target_ref[...]
    wanted, lane = target >> 7, target & (LANES - 1)

    def one_row(r, found):
        pair = table_ref[pl.ds(r, 1), :]
        for h in range(BLOCK // LANES):
            line = jnp.broadcast_to(pair[:, h * LANES:(h + 1) * LANES], (rows, LANES))
            value = jnp.take_along_axis(line, lane, axis=1, mode="promise_in_bounds")
            found = jnp.where(wanted == r * (BLOCK // LANES) + h, value, found)
        return found

    out_ref[...] = lax.fori_loop(0, table_ref.shape[0], one_row, jnp.zeros((rows, LANES), jnp.float32))


def unpack(target, table):
    vmem = pl.BlockSpec(memory_space=pltpu.VMEM)
    return pl.pallas_call(
        unpack_kernel,
        out_shape=jax.ShapeDtypeStruct(target.shape, jnp.float32),
        in_specs=[vmem, vmem],
        out_specs=vmem,
        cost_estimate=pl.CostEstimate(flops=16 << 20, bytes_accessed=1 << 18, transcendentals=0),
        name="unpack",
    )(target, table).reshape(-1)


def per_device(
    alpha,
    lv_sqrt,
    ens_pert,
    bg_sigma,
    static_ctrl,
    obs_owner,
    obs_column,
    obs_level,
    obs_frac,
    innovation,
    obs_rinv,
    obs_count,
):
    highest = lax.Precision.HIGHEST
    coarse_x, coarse_y, channel_count = alpha.shape
    members, levels, fine_x, fine_y = ens_pert.shape
    plane = fine_x * fine_y
    alpha_four = alpha.reshape(coarse_x, coarse_y, members, levels)
    vert = jnp.einsum("xykm,lm->xykl", alpha_four, lv_sqrt, precision=highest).reshape(
        coarse_x, coarse_y, channel_count
    )
    smooth = diffuse(vert)
    row_next = passed_along(smooth[0:1], "tx", -1)
    extended = jnp.concatenate([smooth, row_next], 0)
    col_next = passed_along(extended[:, 0:1], "ty", -1)
    extended = jnp.concatenate([extended, col_next], 1)
    matrix_x = interpolation_matrix(fine_x, coarse_x)
    matrix_y = interpolation_matrix(fine_y, coarse_y)
    partial_x = jnp.einsum("xa,abc->xbc", matrix_x, extended, precision=highest)
    fine_grid = jnp.einsum("yb,xbc->cxy", matrix_y, partial_x, precision=highest)
    fine_grid = fine_grid.reshape(members, levels, fine_x, fine_y)
    partial_sum = jnp.sum(fine_grid * ens_pert.astype(jnp.float32), 0)
    tiles_x = lax.axis_size("tx")
    tiles_y = lax.axis_size("ty")
    tiles = tiles_x * tiles_y
    slots = obs_owner.shape[0]
    capacity = 2 * slots // tiles
    outgoing, target = pack(
        tiles, levels, plane, capacity, obs_count, obs_owner[:, 0], obs_column, obs_level, obs_frac, innovation, obs_rinv
    )
    incoming = lax.all_to_all(outgoing, ("tx", "ty"), split_axis=0, concat_axis=0, tiled=True)
    increment = lax.psum(partial_sum, "mem") + bg_sigma * static_ctrl
    departure, adjoint_part = stencil(increment, incoming)
    returned = lax.all_to_all(departure, ("tx", "ty"), split_axis=0, concat_axis=0, tiled=True)
    departures = unpack(target, returned.reshape(-1, BLOCK))
    adjoint_grid_values = lax.psum(adjoint_part, "mem")
    grad_static = static_ctrl + bg_sigma * adjoint_grid_values
    scaled = (ens_pert.astype(jnp.float32) * adjoint_grid_values[None]).reshape(
        channel_count, fine_x, fine_y
    )
    back_y = jnp.einsum("yb,cxy->xbc", matrix_y, scaled, precision=highest)
    back_ext = jnp.einsum("xa,xbc->abc", matrix_x, back_y, precision=highest)
    row_in = passed_along(back_ext[-1:], "tx", 1)
    folded = back_ext[:-1].at[0:1].add(row_in)
    col_in = passed_along(folded[:, -1:], "ty", 1)
    folded = folded[:, :-1].at[:, 0:1].add(col_in)
    smooth_back = diffuse(folded).reshape(coarse_x, coarse_y, members, levels)
    mixed = jnp.einsum("xykl,lm->xykm", smooth_back, lv_sqrt, precision=highest)
    grad_alpha = alpha + mixed.reshape(coarse_x, coarse_y, channel_count)
    return (grad_alpha, grad_static, departures)


def solution(mesh):
    placed = (
        P("tx", "ty", "mem"),
        P(),
        P("mem", None, "tx", "ty"),
        P(None, "tx", "ty"),
        P(None, "tx", "ty"),
        P(("tx", "ty", "mem"), None),
        P(("tx", "ty", "mem")),
        P(("tx", "ty", "mem")),
        P(None, ("tx", "ty", "mem")),
        P(("tx", "ty", "mem")),
        P(("tx", "ty", "mem")),
        P(("tx", "ty", "mem")),
    )
    return jax.shard_map(
        per_device,
        mesh=mesh,
        in_specs=placed,
        out_specs=(P("tx", "ty", "mem"), P(None, "tx", "ty"), P(("tx", "ty", "mem"))),
        check_vma=False,
    )
```

```python
import functools

import jax
import jax.numpy as jnp
import numpy as np
from jax import lax
from jax.experimental import pallas as pl
from jax.experimental.pallas import tpu as pltpu
from jax.sharding import PartitionSpec as P

RATIO = 4
NSTEP = 4
NU = 0.2
VMEM = pl.BlockSpec(memory_space=pltpu.VMEM)
SMEM = pl.BlockSpec(memory_space=pltpu.SMEM)
ROOM = pltpu.CompilerParams(vmem_limit_bytes=48 << 20)
BLOCK = 256
LANES = 128
WINDOW = 12
HALF = jnp.bfloat16


def split_two(value):
    high = value.astype(HALF)
    return high, (value - high.astype(jnp.float32)).astype(HALF)


def dot_nt(a, b):
    return lax.dot_general(a, b, (((1,), (1,)), ((), ())), preferred_element_type=jnp.float32)


def dot_nn(a, b):
    return jnp.dot(a, b, preferred_element_type=jnp.float32)


def iota(shape, dim):
    return lax.broadcasted_iota(jnp.int32, shape, dim)


def pack_kernel(
    tiles, levels, plane, capacity,
    count_ref, owner_ref, column_ref, level_ref, frac_ref, innov_ref, rinv_ref,
    out_ref, target_ref,
    carry, total, gathered,
):
    blocks = owner_ref.shape[0] * LANES // BLOCK
    keys = tiles * levels
    deep = capacity // BLOCK
    slot_rows = tiles * deep
    group = 4
    count = count_ref[0]

    def row_of(ref, j):
        pair = ref[pl.ds(2 * j, 2), :]
        return jnp.concatenate([pair[0:1], pair[1:2]], 1)

    def onehot(j):
        live = iota((1, BLOCK), 1) + j * BLOCK < count
        key = jnp.where(live, row_of(owner_ref, j) * levels + row_of(level_ref, j), -1)
        return live, iota((keys, BLOCK), 0) == key

    ones = jnp.ones((BLOCK, LANES), HALF)
    total[...] = jnp.zeros_like(total)

    def count_block(j, unused):
        live, mask = onehot(j)
        total[...] += dot_nn(jnp.where(mask, 1.0, 0.0).astype(HALF), ones)
        return unused

    lax.fori_loop(0, blocks, count_block, 0)
    high = jnp.floor(total[...] * (1.0 / LANES))
    low = total[...] - high * LANES
    row_key, col_key = iota((keys, keys), 0), iota((keys, keys), 1)
    before = jnp.where((col_key < row_key) & (col_key // levels == row_key // levels), 1.0, 0.0).astype(HALF)
    start = dot_nn(before, high.astype(HALF)) * LANES + dot_nn(before, low.astype(HALF))
    carry[...] = start + ((iota((keys, LANES), 0) // levels) * capacity).astype(jnp.float32)

    earlier = jnp.where(iota((BLOCK, BLOCK), 0) < iota((BLOCK, BLOCK), 1), 1.0, 0.0).astype(HALF)
    prefix = jnp.concatenate([earlier, ones], 1)
    gathered[...] = jnp.zeros_like(gathered)

    def place(j):
        live, mask = onehot(j)
        ranks = dot_nn(jnp.where(mask, 1.0, 0.0).astype(HALF), prefix)
        now = carry[...]
        here = ranks[:, :BLOCK] + jnp.concatenate([now] * (BLOCK // LANES), 1)
        carry[...] = now + ranks[:, BLOCK:]
        slot = jnp.sum(jnp.where(mask, here, 0.0), 0, keepdims=True)
        target = jnp.where(live, slot.astype(jnp.int32), -1)
        target_ref[pl.ds(2 * j, 2), :] = jnp.concatenate([target[:, :LANES], target[:, LANES:]], 0)
        rows = jnp.where(iota((slot_rows, BLOCK), 0) == (target >> 8), 1.0, 0.0).astype(HALF)
        lanes = jnp.where(iota((BLOCK, BLOCK), 0) == (target & (BLOCK - 1)), 1.0, 0.0).astype(HALF)
        column = row_of(column_ref, j)
        frac = frac_ref[:, pl.ds(pl.multiple_of(j * BLOCK, BLOCK), BLOCK)]
        terms = []
        for value in (frac[0:1], frac[1:2], frac[2:3], row_of(innov_ref, j), row_of(rinv_ref, j)):
            terms.extend(split_two(jnp.broadcast_to(value, (16, BLOCK))))
        for value in (row_of(level_ref, j), column >> 7, column & (LANES - 1)):
            terms.append(jnp.broadcast_to(value.astype(jnp.float32), (16, BLOCK)).astype(HALF))
        spread = [rows * jnp.concatenate([term] * (slot_rows // 16), 0) for term in terms]
        return jnp.concatenate(spread, 0), lanes

    def scatter_group(g, unused):
        placed = [place(g * group + i) for i in range(group)]
        left = jnp.concatenate([a for a, b in placed], 1)
        right = jnp.concatenate([b for a, b in placed], 1)
        gathered[...] += dot_nt(left, right)
        return unused

    lax.fori_loop(0, blocks // group, scatter_group, 0)

    def part(index, tile):
        begin = index * slot_rows + tile * deep
        return gathered[begin:begin + deep, :]

    for tile in range(tiles):
        for p in range(5):
            out_ref[tile, p * deep:(p + 1) * deep, :] = part(2 * p, tile) + part(2 * p + 1, tile)
        base = part(10, tile) * plane + part(11, tile) * LANES + part(12, tile)
        out_ref[tile, 5 * deep:6 * deep, :] = base


def pack(tiles, levels, plane, capacity, count, owner, column, level, frac, innov, rinv):
    slots = owner.shape[0]
    rows = slots // LANES
    deep = capacity // BLOCK
    vmem = pl.BlockSpec(memory_space=pltpu.VMEM)
    return pl.pallas_call(
        functools.partial(pack_kernel, tiles, levels, plane, capacity),
        out_shape=(
            jax.ShapeDtypeStruct((tiles, 6 * deep, BLOCK), jnp.float32),
            jax.ShapeDtypeStruct((rows, LANES), jnp.int32),
        ),
        in_specs=[pl.BlockSpec(memory_space=pltpu.SMEM)] + [vmem] * 6,
        out_specs=(vmem, vmem),
        scratch_shapes=[
            pltpu.VMEM((tiles * levels, LANES), jnp.float32),
            pltpu.VMEM((tiles * levels, LANES), jnp.float32),
            pltpu.VMEM((13 * tiles * deep, BLOCK), jnp.float32),
        ],
        compiler_params=pltpu.CompilerParams(vmem_limit_bytes=40 << 20),
        cost_estimate=pl.CostEstimate(flops=8 << 30, bytes_accessed=1 << 20, transcendentals=0),
        name="pack",
    )(count, *[a.reshape(rows, LANES) for a in (owner, column, level)], frac,
      *[a.reshape(rows, LANES) for a in (innov, rinv)])


def stencil_kernel(
    ahead_ref, behind_ref, first_ref, windows_ref, parts_refs, sigma_ref, static_ref, incoming_ref,
    dep_ref, adj_refs,
    field_t, row_hi, row_lo, adjoint,
):
    levels, fine_x, fine_y = sigma_ref.shape
    sources, packed_rows, block = incoming_ref.shape
    deep = packed_rows // 6
    plane = fine_x * fine_y
    chunk = LANES // fine_x
    share = levels // len(parts_refs)
    span = WINDOW // chunk
    width = WINDOW * fine_x
    adjoint[...] = jnp.zeros_like(adjoint)
    dep_ref[...] = jnp.zeros_like(dep_ref)
    field_t[:, levels * fine_x:] = jnp.zeros((2 * fine_y, width), HALF)
    for slot, part in enumerate(parts_refs):
        start = behind_ref[slot] * share
        static = sigma_ref[pl.ds(start, share)] * static_ref[pl.ds(start, share)]
        turned = (part[...] + static).reshape(share * fine_x, fine_y).T
        high, low = split_two(turned)
        where = pl.ds(pl.multiple_of(start * fine_x, LANES), share * fine_x)
        field_t[:fine_y, where] = high
        field_t[fine_y:, where] = low

    def one_block(q, unused):
        source, at = q // deep, q % deep

        def row(p):
            return incoming_ref[source, pl.ds(p * deep + at, 1), :]

        windows = windows_ref[q]

        @pl.when(windows > 0)
        def _():
            rinv, base = row(4), row(5)
            level = jnp.floor(base * (1.0 / plane))
            rest = base - level * plane
            across = jnp.floor(rest * (1.0 / fine_y))
            along = rest - across * fine_y
            frac_x, frac_y, frac_l = row(0), row(1), row(2)
            first = first_ref[q]
            rows_x = iota((fine_x, block), 0).astype(jnp.float32)
            pick_x = jnp.where(rows_x == across, 1.0 - frac_x, 0.0) + jnp.where(rows_x == across + 1.0, frac_x, 0.0)

            def at_window(w):
                return pl.ds(pl.multiple_of((first + w * span) * LANES, LANES), width)

            def forward(w, acc):
                bottom = ((first + w * span) * chunk).astype(jnp.float32)
                offset = level - bottom
                picks = []
                for g in range(WINDOW):
                    pick_l = jnp.where(offset == float(g), 1.0 - frac_l, 0.0) + jnp.where(offset == float(g - 1), frac_l, 0.0)
                    picks.append(pick_x * pick_l)
                high, low = split_two(jnp.concatenate(picks, 0))
                where = at_window(w)
                row_hi[where, :] = high
                row_lo[where, :] = low
                both = field_t[:, where]
                twice = dot_nn(both, high)
                return acc + (twice[:fine_y] + twice[fine_y:]) + dot_nn(both[:fine_y], low)

            picked = lax.fori_loop(0, windows, forward, jnp.zeros((fine_y, block), jnp.float32))
            rows_y = iota((fine_y, block), 0).astype(jnp.float32)
            pick_y = jnp.where(rows_y == along, 1.0 - frac_y, 0.0) + jnp.where(rows_y == along + 1.0, frac_y, 0.0)
            departure = jnp.sum(picked * pick_y, 0, keepdims=True) - row(3)
            dep_ref[source, pl.ds(at, 1), :] = departure
            high, low = split_two(pick_y * (rinv * departure))
            both = jnp.concatenate([high, low], 0)

            def backward(w, unused):
                where = at_window(w)
                adjoint[where, :] += dot_nt(row_hi[where, :], both)
                adjoint[where, :fine_y] += dot_nt(row_lo[where, :], high)
                return unused

            lax.fori_loop(0, windows, backward, 0)

        return unused

    lax.fori_loop(0, sources * deep, one_block, 0)
    for slot, adj_ref in enumerate(adj_refs):
        rows = pl.ds(pl.multiple_of(ahead_ref[slot] * share * fine_x, LANES), share * fine_x)
        both = adjoint[rows, :]
        adj_ref[...] = (both[:, :fine_y] + both[:, fine_y:]).reshape(share, fine_x, fine_y)


def stencil(parts, incoming, bg_sigma, static_ctrl, ahead, behind):
    levels, fine_x, fine_y = bg_sigma.shape
    sources, packed_rows, block = incoming.shape
    deep, groups = packed_rows // 6, len(parts)
    rows = levels * fine_x + WINDOW * fine_x
    chunk = LANES // fine_x
    level = (incoming[:, 5 * deep:] * (1.0 / (fine_x * fine_y))).astype(jnp.int32)
    used = incoming[:, 4 * deep:5 * deep] > 0.0
    lowest = jnp.min(jnp.where(used, level, levels), 2).reshape(-1)
    highest = jnp.max(jnp.where(used, level, -1), 2).reshape(-1)
    first = lowest // chunk
    windows = jnp.where(highest >= 0, ((highest + 1) // chunk - first) // (WINDOW // chunk) + 1, 0)

    def kernel(*refs):
        parts_end = 4 + groups
        stencil_kernel(
            *refs[:4], refs[4:parts_end], *refs[parts_end:parts_end + 4],
            refs[parts_end + 4:parts_end + 4 + groups], *refs[parts_end + 4 + groups:]
        )

    results = pl.pallas_call(
        kernel,
        out_shape=(jax.ShapeDtypeStruct((sources, deep, block), jnp.float32),)
        + tuple(jax.ShapeDtypeStruct(part.shape, jnp.float32) for part in parts),
        in_specs=[SMEM] * 4 + [VMEM] * (groups + 3),
        out_specs=(VMEM,) * (1 + groups),
        scratch_shapes=[
            pltpu.VMEM((2 * fine_y, rows), HALF),
            pltpu.VMEM((rows, block), HALF),
            pltpu.VMEM((rows, block), HALF),
            pltpu.VMEM((rows, 2 * fine_y), jnp.float32),
        ],
        compiler_params=ROOM,
        cost_estimate=pl.CostEstimate(flops=16 << 30, bytes_accessed=1 << 20, transcendentals=0),
        name="stencil",
    )(ahead, behind, first, windows, *parts, bg_sigma, static_ctrl, incoming)
    return results[0], results[1:]


def unpack_kernel(target_ref, table_ref, out_ref):
    rows = target_ref.shape[0]
    target = target_ref[...]
    wanted, lane = target >> 7, target & (LANES - 1)

    def one_row(r, found):
        pair = table_ref[pl.ds(r, 1), :]
        for h in range(BLOCK // LANES):
            line = jnp.broadcast_to(pair[:, h * LANES:(h + 1) * LANES], (rows, LANES))
            value = jnp.take_along_axis(line, lane, axis=1, mode="promise_in_bounds")
            found = jnp.where(wanted == r * (BLOCK // LANES) + h, value, found)
        return found

    out_ref[...] = lax.fori_loop(0, table_ref.shape[0], one_row, jnp.zeros((rows, LANES), jnp.float32))


def unpack(target, table):
    vmem = pl.BlockSpec(memory_space=pltpu.VMEM)
    return pl.pallas_call(
        unpack_kernel,
        out_shape=jax.ShapeDtypeStruct(target.shape, jnp.float32),
        in_specs=[vmem, vmem],
        out_specs=vmem,
        cost_estimate=pl.CostEstimate(flops=16 << 20, bytes_accessed=1 << 18, transcendentals=0),
        name="unpack",
    )(target, table).reshape(-1)


REACH = NSTEP
EDGE = 8
PAD = 2 * EDGE
SCALE = NU**NSTEP


def interpolation(shape, fine_dim, coarse_dim, shift):
    fine, coarse = iota(shape, fine_dim), iota(shape, coarse_dim) - shift
    frac = (fine % RATIO).astype(jnp.float32) * (1.0 / RATIO)
    low = jnp.where(coarse == fine // RATIO, 1.0 - frac, 0.0)
    return (low + jnp.where(coarse == fine // RATIO + 1, frac, 0.0)).astype(HALF)


def interpolation_rows(fine_x, depth, copies, transposed):
    long, short = EDGE * fine_x, EDGE * depth
    shape = (short, long) if transposed else (long, copies * short)
    fine, coarse = iota(shape, 1 if transposed else 0), iota(shape, 0 if transposed else 1)
    for copy in range(1, copies):
        coarse = jnp.where(coarse >= short, coarse - short, coarse)
    place, target = fine % fine_x, coarse // EDGE
    frac = (place % RATIO).astype(jnp.float32) * (1.0 / RATIO)
    low = jnp.where(target == place // RATIO, 1.0 - frac, 0.0)
    weight = low + jnp.where(target == place // RATIO + 1, frac, 0.0)
    return jnp.where(fine // fine_x == coarse % EDGE, weight, 0.0).astype(HALF)


def neighbours(field):
    width = field.shape[1]
    return pltpu.roll(field, 1, 1) + pltpu.roll(field, width - 1, 1)


def ensemble_kernel(
    coarse_x, coarse_y, offsets,
    order_ref, alpha_ref, above_ref, below_ref,
    left_ref, left_above_ref, left_below_ref, right_ref, right_above_ref, right_below_ref,
    mix_ref, pert_hbm, out_refs, pert_ref, sem, ext, coarse,
):
    members, levels, fine_x, fine_y = pert_ref.shape
    channels = alpha_ref.shape[2]
    fetch = pltpu.make_async_copy(pert_hbm, pert_ref, sem)
    fetch.start()
    ext[:, :EDGE, :] = jnp.zeros((ext.shape[0], EDGE, channels), jnp.float32)
    ext[:, EDGE + coarse_y:, :] = jnp.zeros((ext.shape[0], EDGE, channels), jnp.float32)
    above, below = offsets
    groups = (
        (0, REACH, above, above_ref, left_above_ref, right_above_ref),
        (REACH, coarse_x, 0, alpha_ref, left_ref, right_ref),
        (REACH + coarse_x, REACH + 1, below, below_ref, left_below_ref, right_below_ref),
    )
    for begin, count, offset, middle, left, right in groups:
        ext[begin:begin + count, EDGE:EDGE + coarse_y, :] = middle[offset:offset + count]
        for i in range(count):
            at = offset + i
            ext[begin + i, EDGE - REACH:EDGE, :] = left[at * REACH:(at + 1) * REACH, :]
            ext[begin + i, EDGE + coarse_y:EDGE + coarse_y + REACH + 1, :] = right[
                at * (REACH + 1):(at + 1) * (REACH + 1), :
            ]
    spread_y = interpolation((fine_y, coarse_y + PAD), 0, 1, EDGE)
    spread_y = jnp.concatenate([spread_y.astype(jnp.float32)] * 2, 1).astype(HALF)
    high, low = split_two(mix_ref[...])
    mix = jnp.concatenate([high, high, low], 1)

    def one_group(g, unused):
        lanes = pl.ds(pl.multiple_of(g * LANES, LANES), LANES)
        field = ext[:, :, lanes]
        for step in range(NSTEP):
            inner = field[1:-1]
            field = inner + field[2:] + field[:-2] + neighbours(inner)
        high, low = split_two(field * SCALE)
        for c in range(coarse_x + 1):
            wide = dot_nn(spread_y, jnp.concatenate([high[c], low[c]], 0))
            wide_high, wide_low = split_two(wide)
            coarse[c, lanes, :] = dot_nt(mix, jnp.concatenate([wide_high, wide_low, wide_high], 1))
        return unused

    lax.fori_loop(0, channels // LANES, one_group, 0)
    fetch.wait()
    depth = coarse_x + 2
    spread_x = interpolation_rows(fine_x, depth, 2, False)
    share = levels // len(out_refs)

    for slot, out_ref in enumerate(out_refs):
        for sub in range(share // EDGE):
            first = pl.multiple_of(order_ref[slot] * share + sub * EDGE, EDGE)

            def stacked(k):
                rows = pl.ds(pl.multiple_of(k * levels + first, EDGE), EDGE)
                parts = [coarse[c, rows, :] for c in range(coarse_x + 1)]
                return jnp.concatenate(parts + [jnp.zeros((EDGE, fine_y), jnp.float32)], 0)

            def perturbation(k):
                return pert_ref[k, pl.ds(first, EDGE)].reshape(EDGE * fine_x, fine_y).astype(jnp.float32)

            def pair(p, total):
                high, low = split_two(jnp.concatenate([stacked(2 * p), stacked(2 * p + 1)], 1))
                fine = dot_nn(spread_x, jnp.concatenate([high, low], 0))
                return total + fine[:, :fine_y] * perturbation(2 * p) + fine[:, fine_y:] * perturbation(2 * p + 1)

            total = lax.fori_loop(0, members // 2, pair, jnp.zeros((EDGE * fine_x, fine_y), jnp.float32))
            out_ref[sub * EDGE:(sub + 1) * EDGE] = total.reshape(EDGE, fine_x, fine_y)


def backward_kernel(
    coarse_x, coarse_y, joined,
    order_ref, parts_refs, mix_ref, sigma_ref, static_ref, pert_ref,
    grad_ref, center_ref, middle_refs, left_refs, right_refs,
    adjoint, coarse,
):
    members, levels, fine_x, fine_y = pert_ref.shape
    channels = members * levels
    share = levels // len(parts_refs)
    for slot, part in enumerate(parts_refs):
        first = order_ref[slot] * share
        adjoint[pl.ds(first, share)] = part[...]
    grad_ref[...] = static_ref[...] + sigma_ref[...] * adjoint[...]
    depth = coarse_x + 2
    fold_x = interpolation_rows(fine_x, depth, 1, True)

    for group in range(levels // EDGE):
        field = adjoint[group * EDGE:(group + 1) * EDGE].reshape(EDGE * fine_x, fine_y)

        def member(k, unused):
            scaled = pert_ref[k, group * EDGE:(group + 1) * EDGE].reshape(EDGE * fine_x, fine_y).astype(jnp.float32)
            high, low = split_two(scaled * field)
            both = dot_nn(fold_x, jnp.concatenate([high, low], 1))
            rows = pl.ds(pl.multiple_of(k * levels + group * EDGE, EDGE), EDGE)
            for c in range(coarse_x + 1):
                piece = both[c * EDGE:(c + 1) * EDGE]
                coarse[c, rows, :] = piece[:, :fine_y] + piece[:, fine_y:]
            return unused

        lax.fori_loop(0, members, member, 0)

    fold_y = interpolation((coarse_y + PAD, fine_y), 1, 0, EDGE)
    fold_y = jnp.concatenate([fold_y, fold_y], 1)
    high, low = split_two(mix_ref[...])
    mix = jnp.concatenate([high, high, low], 0)

    def one_group(g, unused):
        lanes = pl.ds(pl.multiple_of(g * LANES, LANES), LANES)
        rows = []
        for c in range(coarse_x + 1):
            high, low = split_two(coarse[c, lanes, :])
            narrow = dot_nt(fold_y, jnp.concatenate([high, low], 1))
            high, low = split_two(narrow)
            rows.append(dot_nn(jnp.concatenate([high, low, high], 1), mix)[None])
        field = jnp.concatenate(rows, 0) * SCALE
        empty = jnp.zeros((1,) + field.shape[1:], jnp.float32)
        for step in range(NSTEP):
            own = field + neighbours(field)
            field = jnp.concatenate([field, empty, empty], 0) + jnp.concatenate([empty, own, empty], 0) + jnp.concatenate(
                [empty, empty, field], 0
            )
        inside = field[REACH:REACH + coarse_x]
        up, down = field[:REACH], field[REACH + coarse_x:]
        if joined:
            none = jnp.zeros((coarse_x - REACH - 1,) + field.shape[1:], jnp.float32)
            outside = [jnp.concatenate([down, none], 0) + jnp.concatenate([none, empty, up], 0)]
        else:
            outside = [up, down]
        center_ref[:, :, lanes] = inside[:, EDGE:EDGE + coarse_y]
        for ref, value in zip(middle_refs, outside):
            ref[:, :, lanes] = value[:, EDGE:EDGE + coarse_y]
        for left, right, value in zip(left_refs, right_refs, [inside] + outside):
            for i in range(value.shape[0]):
                left[i * REACH:(i + 1) * REACH, lanes] = value[i, EDGE - REACH:EDGE]
                right[i * (REACH + 1):(i + 1) * (REACH + 1), lanes] = value[
                    i, EDGE + coarse_y:EDGE + coarse_y + REACH + 1
                ]
        return unused

    lax.fori_loop(0, channels // LANES, one_group, 0)


def fold_kernel(places, alpha_ref, center_ref, *refs):
    part_refs, out_ref = refs[:-1], refs[-1]
    out_ref[...] = alpha_ref[...] + center_ref[...]
    for (row, count, column, width), ref in zip(places, part_refs):
        if width == out_ref.shape[1]:
            out_ref[row:row + count] += ref[...]
        else:
            for i in range(count):
                out_ref[row + i, column:column + width, :] += ref[i * width:(i + 1) * width, :]


def shifted(value, by_x, by_y):
    count_x, count_y = lax.axis_size("tx"), lax.axis_size("ty")
    pairs = [
        (x * count_y + y, (x + by_x) % count_x * count_y + (y + by_y) % count_y)
        for x in range(count_x)
        for y in range(count_y)
    ]
    return lax.ppermute(value, ("tx", "ty"), pairs)


def ensemble(alpha, mix, ens_pert, order):
    coarse_x, coarse_y, channels = alpha.shape
    members, levels, fine_x, fine_y = ens_pert.shape
    joined = lax.axis_size("tx") == 2
    ends = alpha[:, coarse_y - REACH:]
    starts = alpha[:, :REACH + 1]

    def flat(strip):
        return strip.reshape(-1, channels)

    if joined:
        other = shifted(alpha, 1, 0)
        above = below = other
        left_above = left_below = shifted(flat(ends), 1, 1)
        right_above = right_below = shifted(flat(starts), 1, -1)
        offsets = (coarse_x - REACH, 0)
    else:
        last = slice(coarse_x - REACH, coarse_x)
        first = slice(0, REACH + 1)
        above, below = shifted(alpha[last], 1, 0), shifted(alpha[first], -1, 0)
        left_above, left_below = shifted(flat(ends[last]), 1, 1), shifted(flat(ends[first]), -1, 1)
        right_above, right_below = shifted(flat(starts[last]), 1, -1), shifted(flat(starts[first]), -1, -1)
        offsets = (0, 0)
    left, right = shifted(flat(ends), 0, 1), shifted(flat(starts), 0, -1)
    groups = order.shape[0]

    def kernel(*refs):
        ensemble_kernel(coarse_x, coarse_y, offsets, *refs[:12], refs[12:12 + groups], *refs[12 + groups:])

    return pl.pallas_call(
        kernel,
        out_shape=tuple(jax.ShapeDtypeStruct((levels // groups, fine_x, fine_y), jnp.float32) for _ in range(groups)),
        in_specs=[SMEM] + [VMEM] * 10 + [pl.BlockSpec(memory_space=pl.ANY)],
        out_specs=(VMEM,) * groups,
        scratch_shapes=[
            pltpu.VMEM(ens_pert.shape, ens_pert.dtype),
            pltpu.SemaphoreType.DMA,
            pltpu.VMEM((coarse_x + 2 * REACH + 1, coarse_y + PAD, channels), jnp.float32),
            pltpu.VMEM((coarse_x + 1, channels, fine_y), jnp.float32),
        ],
        compiler_params=ROOM,
        cost_estimate=pl.CostEstimate(flops=8 << 30, bytes_accessed=8 << 20, transcendentals=0),
        name="ensemble",
    )(order, alpha, above, below, left, left_above, left_below, right, right_above, right_below, mix, ens_pert)


def backward(alpha, adjoint_parts, mix, bg_sigma, static_ctrl, ens_pert, order):
    coarse_x, coarse_y, channels = alpha.shape
    members, levels, fine_x, fine_y = ens_pert.shape
    joined = lax.axis_size("tx") == 2
    groups = len(adjoint_parts)
    outside = [coarse_x] if joined else [REACH, REACH + 1]
    strips = [coarse_x] + outside
    shapes = [bg_sigma.shape, alpha.shape]
    shapes += [(rows, coarse_y, channels) for rows in outside]
    shapes += [(rows * REACH, channels) for rows in strips]
    shapes += [(rows * (REACH + 1), channels) for rows in strips]
    n_in, n_mid, n_strip = 5 + groups, len(outside), len(strips)

    def kernel(*refs):
        order_ref, parts, rest = refs[0], refs[1:1 + groups], refs[1 + groups:n_in]
        outs = refs[n_in:n_in + len(shapes)]
        middle = outs[2:2 + n_mid]
        left = outs[2 + n_mid:2 + n_mid + n_strip]
        right = outs[2 + n_mid + n_strip:]
        backward_kernel(
            coarse_x, coarse_y, joined, order_ref, parts, *rest,
            outs[0], outs[1], middle, left, right, *refs[n_in + len(shapes):]
        )

    results = pl.pallas_call(
        kernel,
        out_shape=tuple(jax.ShapeDtypeStruct(shape, jnp.float32) for shape in shapes),
        in_specs=[SMEM] + [VMEM] * (groups + 4),
        out_specs=(VMEM,) * len(shapes),
        scratch_shapes=[
            pltpu.VMEM(bg_sigma.shape, jnp.float32),
            pltpu.VMEM((coarse_x + 1, channels, fine_y), jnp.float32),
        ],
        compiler_params=ROOM,
        cost_estimate=pl.CostEstimate(flops=8 << 30, bytes_accessed=8 << 20, transcendentals=0),
        name="backward",
    )(order, *adjoint_parts, mix, bg_sigma, static_ctrl, ens_pert)
    grad_static, center = results[:2]
    middle = results[2:2 + n_mid]
    left, right = results[2 + n_mid:2 + n_mid + n_strip], results[2 + n_mid + n_strip:]
    last, wide = coarse_y - REACH, REACH + 1
    moves = [(1, 0, coarse_x)] if joined else [(-1, coarse_x - REACH, REACH), (1, 0, REACH + 1)]
    places, parts = [], []
    for (by, row, count), value, to_left, to_right in zip(moves, middle, left[1:], right[1:]):
        parts += [shifted(value, by, 0), shifted(to_left, by, -1), shifted(to_right, by, 1)]
        places += [(row, count, 0, coarse_y), (row, count, last, REACH), (row, count, 0, wide)]
    parts += [shifted(left[0], 0, -1), shifted(right[0], 0, 1)]
    places += [(0, coarse_x, last, REACH), (0, coarse_x, 0, wide)]
    grad_alpha = pl.pallas_call(
        functools.partial(fold_kernel, places),
        out_shape=jax.ShapeDtypeStruct(alpha.shape, jnp.float32),
        in_specs=[VMEM] * (2 + len(parts)),
        out_specs=VMEM,
        compiler_params=ROOM,
        cost_estimate=pl.CostEstimate(flops=1 << 20, bytes_accessed=2 << 20, transcendentals=0),
        name="fold",
    )(alpha, center, *parts)
    return grad_alpha, grad_static


def shared_sum(parts):
    count = len(parts)
    total = parts[0]
    for d in range(1, count):
        total = total + lax.ppermute(parts[d], "mem", [(i, (i + d) % count) for i in range(count)])
    return [total] + [lax.ppermute(total, "mem", [(i, (i + d) % count) for i in range(count)]) for d in range(1, count)]


def per_device(
    alpha,
    lv_sqrt,
    ens_pert,
    bg_sigma,
    static_ctrl,
    obs_owner,
    obs_column,
    obs_level,
    obs_frac,
    innovation,
    obs_rinv,
    obs_count,
):
    levels, fine_x, fine_y = bg_sigma.shape
    tiles = lax.axis_size("tx") * lax.axis_size("ty")
    capacity = 2 * obs_owner.shape[0] // tiles
    groups, me = lax.axis_size("mem"), lax.axis_index("mem")
    ahead = jnp.stack([(me + d) % groups for d in range(groups)]).astype(jnp.int32)
    behind = jnp.stack([(me - d) % groups for d in range(groups)]).astype(jnp.int32)
    copies = LANES // levels
    same = np.kron(np.eye(copies, dtype=np.float32), np.ones((levels, levels), np.float32))
    mix = jnp.tile(lv_sqrt, (copies, copies)) * same
    partial = ensemble(alpha, mix, ens_pert, ahead)
    outgoing, target = pack(
        tiles, levels, fine_x * fine_y, capacity,
        obs_count, obs_owner[:, 0], obs_column, obs_level, obs_frac, innovation, obs_rinv,
    )
    incoming = lax.all_to_all(outgoing, ("tx", "ty"), split_axis=0, concat_axis=0, tiled=True)
    departure, adjoint = stencil(shared_sum(partial), incoming, bg_sigma, static_ctrl, ahead, behind)
    returned = lax.all_to_all(departure, ("tx", "ty"), split_axis=0, concat_axis=0, tiled=True)
    departures = unpack(target, returned.reshape(-1, BLOCK))
    grad_alpha, grad_static = backward(alpha, shared_sum(adjoint), mix, bg_sigma, static_ctrl, ens_pert, behind)
    return (grad_alpha, grad_static, departures)


def solution(mesh):
    placed = (
        P("tx", "ty", "mem"),
        P(),
        P("mem", None, "tx", "ty"),
        P(None, "tx", "ty"),
        P(None, "tx", "ty"),
        P(("tx", "ty", "mem"), None),
        P(("tx", "ty", "mem")),
        P(("tx", "ty", "mem")),
        P(None, ("tx", "ty", "mem")),
        P(("tx", "ty", "mem")),
        P(("tx", "ty", "mem")),
        P(("tx", "ty", "mem")),
    )
    return jax.shard_map(
        per_device,
        mesh=mesh,
        in_specs=placed,
        out_specs=(P("tx", "ty", "mem"), P(None, "tx", "ty"), P(("tx", "ty", "mem"))),
        check_vma=False,
    )
```

```python
import functools
import math

import jax
import jax.numpy as jnp
from jax import lax
from jax.experimental import pallas as pl
from jax.experimental.pallas import tpu as pltpu
from jax.sharding import PartitionSpec as P

RATIO = 4
NSTEP = 4
NU = 0.2
VMEM = pl.BlockSpec(memory_space=pltpu.VMEM)
SMEM = pl.BlockSpec(memory_space=pltpu.SMEM)
HBM = pl.BlockSpec(memory_space=pltpu.HBM)


def room(mebibytes):
    return pltpu.CompilerParams(vmem_limit_bytes=mebibytes << 20)

BLOCK = 256
LANES = 128
NARROW = 8
WIDE = 16
HALF = jnp.bfloat16


def split_two(value):
    high = value.astype(HALF)
    return high, (value - high.astype(jnp.float32)).astype(HALF)


def dot_nt(a, b):
    return lax.dot_general(a, b, (((1,), (1,)), ((), ())), preferred_element_type=jnp.float32)


def dot_nn(a, b):
    return jnp.dot(a, b, preferred_element_type=jnp.float32)


def iota(shape, dim):
    return lax.broadcasted_iota(jnp.int32, shape, dim)


def pack_kernel(
    tiles, levels, plane, capacity,
    count_ref, *refs,
):
    sources, (out_ref, target_ref, carry, total, gathered, *held), sems = refs[:6], refs[6:-1], refs[-1]
    copies = [pltpu.make_async_copy(source, here, sems.at[i]) for i, (source, here) in enumerate(zip(sources, held))]
    for copy in copies:
        copy.start()
    owner_ref, level_ref, column_ref, frac_ref, innov_ref, rinv_ref = held
    blocks = target_ref.shape[0] * LANES // BLOCK
    keys = tiles * levels
    deep = capacity // BLOCK
    slot_rows = tiles * deep
    group = 4
    count = count_ref[0]

    def row_of(ref, j):
        pair = ref[pl.ds(2 * j, 2), :]
        return jnp.concatenate([pair[0:1], pair[1:2]], 1)

    def onehot(j):
        live = iota((1, BLOCK), 1) + j * BLOCK < count
        key = jnp.where(live, row_of(owner_ref, j) * levels + row_of(level_ref, j), -1)
        return live, iota((keys, BLOCK), 0) == key

    ones = jnp.ones((BLOCK, LANES), HALF)
    total[...] = jnp.zeros_like(total)
    for copy in copies[:2]:
        copy.wait()

    def count_group(g, unused):
        masks = [onehot(g * group + i)[1] for i in range(group)]
        counted = jnp.concatenate([jnp.where(mask, 1.0, 0.0).astype(HALF) for mask in masks], 1)
        total[...] += dot_nn(counted, jnp.concatenate([ones] * group, 0))
        return unused

    lax.fori_loop(0, blocks // group, count_group, 0)
    for copy in copies[2:]:
        copy.wait()
    high = jnp.floor(total[...] * (1.0 / LANES))
    low = total[...] - high * LANES
    row_key, col_key = iota((keys, keys), 0), iota((keys, keys), 1)
    before = jnp.where((col_key < row_key) & (col_key // levels == row_key // levels), 1.0, 0.0).astype(HALF)
    start = dot_nn(before, high.astype(HALF)) * LANES + dot_nn(before, low.astype(HALF))
    carry[...] = start + ((iota((keys, LANES), 0) // levels) * capacity).astype(jnp.float32)

    earlier = jnp.where(iota((BLOCK, BLOCK), 0) < iota((BLOCK, BLOCK), 1), 1.0, 0.0).astype(HALF)
    prefix = jnp.concatenate([earlier, ones], 1)
    gathered[...] = jnp.zeros_like(gathered)

    def place(j):
        live, mask = onehot(j)
        ranks = dot_nn(jnp.where(mask, 1.0, 0.0).astype(HALF), prefix)
        now = carry[...]
        here = ranks[:, :BLOCK] + jnp.concatenate([now] * (BLOCK // LANES), 1)
        carry[...] = now + ranks[:, BLOCK:]
        slot = jnp.sum(jnp.where(mask, here, 0.0), 0, keepdims=True)
        target = jnp.where(live, slot.astype(jnp.int32), -1)
        target_ref[pl.ds(2 * j, 2), :] = jnp.concatenate([target[:, :LANES], target[:, LANES:]], 0)
        rows = jnp.where(iota((slot_rows, BLOCK), 0) == (target >> 8), 1.0, 0.0).astype(HALF)
        lanes = jnp.where(iota((BLOCK, BLOCK), 0) == (target & (BLOCK - 1)), 1.0, 0.0).astype(HALF)
        column = row_of(column_ref, j)
        frac = frac_ref[:, pl.ds(pl.multiple_of(j * BLOCK, BLOCK), BLOCK)]
        terms = []
        for value in (frac[0:1], frac[1:2], frac[2:3], row_of(innov_ref, j), row_of(rinv_ref, j)):
            terms.extend(split_two(jnp.broadcast_to(value, (16, BLOCK))))
        for value in (row_of(level_ref, j), column >> 7, column & (LANES - 1)):
            terms.append(jnp.broadcast_to(value.astype(jnp.float32), (16, BLOCK)).astype(HALF))
        spread = [rows * jnp.concatenate([term] * (slot_rows // 16), 0) for term in terms]
        return jnp.concatenate(spread, 0), lanes

    def scatter_group(g, unused):
        placed = [place(g * group + i) for i in range(group)]
        left = jnp.concatenate([a for a, b in placed], 1)
        right = jnp.concatenate([b for a, b in placed], 1)
        gathered[...] += dot_nt(left, right)
        return unused

    lax.fori_loop(0, blocks // group, scatter_group, 0)

    def part(index, tile):
        begin = index * slot_rows + tile * deep
        return gathered[begin:begin + deep, :]

    for tile in range(tiles):
        for p in range(5):
            out_ref[tile, p * deep:(p + 1) * deep, :] = part(2 * p, tile) + part(2 * p + 1, tile)
        base = part(10, tile) * plane + part(11, tile) * LANES + part(12, tile)
        out_ref[tile, 5 * deep:6 * deep, :] = base


def pack(tiles, levels, plane, capacity, count, owner, column, level, frac, innov, rinv):
    slots = owner.shape[0]
    rows = slots // LANES
    deep = capacity // BLOCK
    values = [value.reshape(rows, LANES) for value in (owner, level, column)]
    values += [frac, innov.reshape(rows, LANES), rinv.reshape(rows, LANES)]
    vmem = pl.BlockSpec(memory_space=pltpu.VMEM)
    return pl.pallas_call(
        functools.partial(pack_kernel, tiles, levels, plane, capacity),
        out_shape=(
            jax.ShapeDtypeStruct((tiles, 6 * deep, BLOCK), jnp.float32),
            jax.ShapeDtypeStruct((rows, LANES), jnp.int32),
        ),
        in_specs=[SMEM] + [HBM] * 6,
        out_specs=(vmem, vmem),
        scratch_shapes=[
            pltpu.VMEM((tiles * levels, LANES), jnp.float32),
            pltpu.VMEM((tiles * levels, LANES), jnp.float32),
            pltpu.VMEM((13 * tiles * deep, BLOCK), jnp.float32),
        ]
        + [pltpu.VMEM(value.shape, value.dtype) for value in values]
        + [pltpu.SemaphoreType.DMA((len(values),))],
        compiler_params=room(16),
        cost_estimate=pl.CostEstimate(flops=8 << 30, bytes_accessed=1 << 20, transcendentals=0),
        name="pack",
    )(count, *values)


def stencil_kernel(
    me_ref, parts_refs, sigma_ref, static_ref, incoming_ref,
    dep_ref, adj_refs,
    field, field_t, adjoint, spans, spans_ref, sem,
):
    levels, fine_x, fine_y = sigma_ref.shape
    sources, packed_rows, block = incoming_ref.shape
    deep = packed_rows // 6
    plane = fine_x * fine_y
    chunk = LANES // fine_x
    groups = len(parts_refs)
    share = levels // groups
    rows = levels * fine_x
    me = me_ref[0]
    halves = block // LANES
    column = iota((sources * deep, LANES), 1)
    found = jnp.zeros((sources * deep, LANES), jnp.int32)
    for half in range(halves):
        lanes = slice(half * LANES, (half + 1) * LANES)
        used = incoming_ref[:, 4 * deep:5 * deep, lanes].reshape(sources * deep, LANES) > 0.0
        level = jnp.floor(incoming_ref[:, 5 * deep:, lanes].reshape(sources * deep, LANES) * (1.0 / plane))
        lowest = jnp.min(jnp.where(used, level, float(levels)), 1, keepdims=True).astype(jnp.int32)
        highest = jnp.max(jnp.where(used, level, -1.0), 1, keepdims=True).astype(jnp.int32)
        found = jnp.where((column == 2 * half) & (highest >= 0), lowest, found)
        found = jnp.where((column == 2 * half + 1) & (highest >= 0), highest + 2 - lowest, found)
    spans[...] = found
    fetch = pltpu.make_async_copy(spans, spans_ref, sem)
    fetch.start()
    adjoint[...] = jnp.zeros_like(adjoint)
    dep_ref[...] = jnp.zeros_like(dep_ref)
    field[rows:, :] = jnp.zeros((field.shape[0] - rows, fine_y), jnp.float32)
    for slot, part in enumerate(parts_refs):
        start = lax.rem(me + groups - slot, groups) * share
        static = sigma_ref[pl.ds(start, share)] * static_ref[pl.ds(start, share)]
        where = pl.ds(pl.multiple_of(start * fine_x, LANES), share * fine_x)
        field[where, :] = (part[...] + static).reshape(share * fine_x, fine_y)
    for shift in range(chunk):
        field_t[shift, :, rows:] = jnp.zeros((2 * fine_y, field_t.shape[2] - rows), HALF)
        for g in range(rows // LANES):
            begin = shift * fine_x + g * LANES
            high, low = split_two(field[begin:begin + LANES, :].T)
            field_t[shift, :fine_y, g * LANES:(g + 1) * LANES] = high
            field_t[shift, fine_y:, g * LANES:(g + 1) * LANES] = low

    fetch.wait()

    def block_of(source, at, half):
        def row(p):
            return incoming_ref[source, pl.ds(p * deep + at, 1), :][:, half * LANES:(half + 1) * LANES]

        base = row(5)
        level = jnp.floor(base * (1.0 / plane))
        rest = base - level * plane
        across = jnp.floor(rest * (1.0 / fine_y))
        along = rest - across * fine_y
        frac_x, frac_y, frac_l = row(0), row(1), row(2)
        rows_x = iota((fine_x, LANES), 0).astype(jnp.float32)
        pick_x = jnp.where(rows_x == across, 1.0 - frac_x, 0.0) + jnp.where(rows_x == across + 1.0, frac_x, 0.0)
        rows_y = iota((fine_y, LANES), 0).astype(jnp.float32)
        pick_y = jnp.where(rows_y == along, 1.0 - frac_y, 0.0) + jnp.where(rows_y == along + 1.0, frac_y, 0.0)

        def weights(bottom, reach):
            offset = level - bottom.astype(jnp.float32)
            picks = []
            for g in range(reach):
                pick_l = jnp.where(offset == float(g), 1.0 - frac_l, 0.0) + jnp.where(offset == float(g - 1), frac_l, 0.0)
                picks.append(pick_x * pick_l)
            return jnp.concatenate(split_two(jnp.concatenate(picks, 0)), 1)

        def finish(picked):
            departure = jnp.sum(picked * pick_y, 0, keepdims=True) - row(3)
            turned = jnp.concatenate(split_two((pick_y * (row(4) * departure)).T), 1)
            return departure, jnp.concatenate([turned, turned], 0)

        return weights, finish

    def look(bottom, pick):
        lanes = pl.ds(pl.multiple_of((bottom // chunk) * LANES, LANES), pick.shape[0])
        seen = dot_nn(field_t[lax.rem(bottom, chunk), :, lanes], pick)
        return seen[:fine_y, :LANES] + (seen[:fine_y, LANES:] + seen[fine_y:, :LANES])

    def spread(pick, term):
        both = dot_nn(pick, term)
        return both[:, :fine_y] + both[:, fine_y:]

    def rows_at(bottom, reach):
        return pl.ds(pl.multiple_of(bottom * fine_x, fine_x), reach * fine_x)

    def together(blocks, bottoms, reach):
        parts = [block_of(*block) for block in blocks]
        picks = [weights(bottom, reach) for (weights, finish), bottom in zip(parts, bottoms)]
        seen = [look(bottom, pick) for bottom, pick in zip(bottoms, picks)]
        done = [finish(value) for (weights, finish), value in zip(parts, seen)]
        adds = [spread(pick, term) for pick, (departure, term) in zip(picks, done)]
        keep(blocks, [departure for departure, term in done])
        for bottom, add in zip(bottoms, adds):
            adjoint[rows_at(bottom, reach), :] += add

    def keep(blocks, departures):
        for i in range(0, len(blocks), halves):
            source, at, half = blocks[i]
            dep_ref[source, pl.ds(at, 1), :] = jnp.concatenate(departures[i:i + halves], 1)

    def alone(block, first, needed):
        weights, finish = block_of(*block)
        windows = (needed + WIDE - 1) // WIDE

        def forward(w, total):
            bottom = first + w * WIDE
            return total + look(bottom, weights(bottom, WIDE))

        departure, term = finish(lax.fori_loop(0, windows, forward, jnp.zeros((fine_y, LANES), jnp.float32)))

        def backward(w, unused):
            bottom = first + w * WIDE
            adjoint[rows_at(bottom, WIDE), :] += spread(weights(bottom, WIDE), term)
            return unused

        lax.fori_loop(0, windows, backward, 0)
        return departure

    step = 2 if deep % 2 == 0 else 1

    def one_step(i, unused):
        source, at = i // (deep // step), lax.rem(i, deep // step) * step
        blocks = [(source, at + r, half) for r in range(step) for half in range(halves)]
        numbers = [(source * deep + at + r, half) for r in range(step) for half in range(halves)]
        bottoms = [spans_ref[row, 2 * half] for row, half in numbers]
        needs = [spans_ref[row, 2 * half + 1] for row, half in numbers]
        most = functools.reduce(jnp.maximum, needs)

        @pl.when((most > 0) & (most <= NARROW))
        def _():
            together(blocks, bottoms, NARROW)

        @pl.when((most > NARROW) & (most <= WIDE))
        def _():
            together(blocks, bottoms, WIDE)

        @pl.when(most > WIDE)
        def _():
            keep(blocks, [alone(*each) for each in zip(blocks, bottoms, needs)])

        return unused

    lax.fori_loop(0, sources * deep // step, one_step, 0)
    for slot, adj_ref in enumerate(adj_refs):
        start = lax.rem(me + slot, groups) * share * fine_x
        adj_ref[...] = adjoint[pl.ds(pl.multiple_of(start, LANES), share * fine_x), :].reshape(share, fine_x, fine_y)


def stencil(parts, incoming, bg_sigma, static_ctrl, me):
    levels, fine_x, fine_y = bg_sigma.shape
    sources, packed_rows, block = incoming.shape
    deep, groups = packed_rows // 6, len(parts)
    rows = levels * fine_x
    padded = rows + WIDE * fine_x

    def kernel(*refs):
        parts_end = 1 + groups
        stencil_kernel(
            refs[0], refs[1:parts_end], *refs[parts_end:parts_end + 4],
            refs[parts_end + 4:parts_end + 4 + groups], *refs[parts_end + 4 + groups:]
        )

    results = pl.pallas_call(
        kernel,
        out_shape=(jax.ShapeDtypeStruct((sources, deep, block), jnp.float32),)
        + tuple(jax.ShapeDtypeStruct(part.shape, jnp.float32) for part in parts),
        in_specs=[SMEM] + [VMEM] * (groups + 3),
        out_specs=(VMEM,) * (1 + groups),
        scratch_shapes=[
            pltpu.VMEM((padded, fine_y), jnp.float32),
            pltpu.VMEM((LANES // fine_x, 2 * fine_y, padded), HALF),
            pltpu.VMEM((padded, fine_y), jnp.float32),
            pltpu.VMEM((sources * deep, LANES), jnp.int32),
            pltpu.SMEM((sources * deep, LANES), jnp.int32),
            pltpu.SemaphoreType.DMA,
        ],
        compiler_params=room(20),
        cost_estimate=pl.CostEstimate(flops=16 << 30, bytes_accessed=1 << 20, transcendentals=0),
        name="stencil",
    )(me, *parts, bg_sigma, static_ctrl, incoming)
    return results[0], results[1:]


def unpack_kernel(target_ref, table_ref, out_ref):
    slot_rows = table_ref.shape[0]
    high, low = split_two(table_ref[...])
    both = jnp.concatenate([high.astype(jnp.float32), low.astype(jnp.float32)], 0)
    turned = both.T.astype(HALF)
    group = 4

    def some_blocks(g, unused):
        for i in range(group):
            pair = target_ref[pl.ds(2 * (g * group + i), 2), :]
            target = jnp.concatenate([pair[0:1], pair[1:2]], 1)
            rows = jnp.where(iota((slot_rows, BLOCK), 0) == (target >> 8), 1.0, 0.0).astype(HALF)
            lines = dot_nn(turned, jnp.concatenate([rows, rows], 0))
            lane = iota((BLOCK, BLOCK), 0) == (target & (BLOCK - 1))
            found = jnp.sum(jnp.where(lane, lines, 0.0), 0, keepdims=True)
            out_ref[pl.ds(2 * (g * group + i), 2), :] = jnp.concatenate([found[:, :LANES], found[:, LANES:]], 0)
        return unused

    lax.fori_loop(0, target_ref.shape[0] // (2 * group), some_blocks, 0)


def unpack(target, table):
    vmem = pl.BlockSpec(memory_space=pltpu.VMEM)
    return pl.pallas_call(
        unpack_kernel,
        out_shape=jax.ShapeDtypeStruct(target.shape, jnp.float32),
        in_specs=[vmem, vmem],
        out_specs=vmem,
        compiler_params=room(8),
        cost_estimate=pl.CostEstimate(flops=2 << 30, bytes_accessed=1 << 18, transcendentals=0),
        name="unpack",
    )(target, table).reshape(-1)


REACH = NSTEP
EDGE = 8
PAD = 2 * EDGE
SCALE = NU**NSTEP


def interpolation(shape, fine_dim, coarse_dim, shift):
    fine, coarse = iota(shape, fine_dim), iota(shape, coarse_dim) - shift
    frac = (fine % RATIO).astype(jnp.float32) * (1.0 / RATIO)
    low = jnp.where(coarse == fine // RATIO, 1.0 - frac, 0.0)
    return (low + jnp.where(coarse == fine // RATIO + 1, frac, 0.0)).astype(HALF)


def interpolation_rows(fine_x, depth, copies, transposed):
    long, short = EDGE * fine_x, EDGE * depth
    shape = (short, long) if transposed else (long, copies * short)
    fine, coarse = iota(shape, 1 if transposed else 0), iota(shape, 0 if transposed else 1)
    for copy in range(1, copies):
        coarse = jnp.where(coarse >= short, coarse - short, coarse)
    place, target = fine % fine_x, coarse // EDGE
    frac = (place % RATIO).astype(jnp.float32) * (1.0 / RATIO)
    low = jnp.where(target == place // RATIO, 1.0 - frac, 0.0)
    weight = low + jnp.where(target == place // RATIO + 1, frac, 0.0)
    return jnp.where(fine // fine_x == coarse % EDGE, weight, 0.0).astype(HALF)


def mixing(mix_ref):
    levels = mix_ref.shape[0]
    tile = jnp.where(iota((LANES, levels), 0) % levels == iota((LANES, levels), 1), 1.0, 0.0).astype(HALF)
    same = iota((LANES, LANES), 0) // levels == iota((LANES, LANES), 1) // levels
    terms = []
    for term in split_two(mix_ref[...]):
        tiled = dot_nt(dot_nn(tile, term).astype(HALF), tile)
        terms.append(jnp.where(same, tiled, 0.0).astype(HALF))
    return terms


def neighbours(field):
    width = field.shape[1]
    return pltpu.roll(field, 1, 1) + pltpu.roll(field, width - 1, 1)


def ensemble_kernel(
    coarse_x, coarse_y, offsets,
    me_ref, alpha_ref, above_ref, below_ref,
    left_ref, left_above_ref, left_below_ref, right_ref, right_above_ref, right_below_ref,
    mix_ref, pert_hbm, out_refs, pert_ref, sem, ext, coarse,
):
    members, levels, fine_x, fine_y = pert_ref.shape
    channels = alpha_ref.shape[2]
    fetch = pltpu.make_async_copy(pert_hbm, pert_ref, sem)
    fetch.start()
    ext[:, :EDGE, :] = jnp.zeros((ext.shape[0], EDGE, channels), jnp.float32)
    ext[:, EDGE + coarse_y:, :] = jnp.zeros((ext.shape[0], EDGE, channels), jnp.float32)
    above, below = offsets
    groups = (
        (0, REACH, above, above_ref, left_above_ref, right_above_ref),
        (REACH, coarse_x, 0, alpha_ref, left_ref, right_ref),
        (REACH + coarse_x, REACH + 1, below, below_ref, left_below_ref, right_below_ref),
    )
    for begin, count, offset, middle, left, right in groups:
        ext[begin:begin + count, EDGE:EDGE + coarse_y, :] = middle[offset:offset + count]
        for i in range(count):
            at = offset + i
            ext[begin + i, EDGE - REACH:EDGE, :] = left[at * REACH:(at + 1) * REACH, :]
            ext[begin + i, EDGE + coarse_y:EDGE + coarse_y + REACH + 1, :] = right[
                at * (REACH + 1):(at + 1) * (REACH + 1), :
            ]
    spread_y = interpolation((fine_y, coarse_y + PAD), 0, 1, EDGE)
    spread_y = jnp.concatenate([spread_y.astype(jnp.float32)] * 2, 1).astype(HALF)
    high, low = mixing(mix_ref)
    mix = jnp.concatenate([high, high, low], 1)

    def one_group(g, unused):
        lanes = pl.ds(pl.multiple_of(g * LANES, LANES), LANES)
        field = ext[:, :, lanes]
        for step in range(NSTEP):
            inner = field[1:-1]
            field = inner + field[2:] + field[:-2] + neighbours(inner)
        high, low = split_two(field * SCALE)
        for c in range(coarse_x + 1):
            wide = dot_nn(spread_y, jnp.concatenate([high[c], low[c]], 0))
            wide_high, wide_low = split_two(wide)
            coarse[c, lanes, :] = dot_nt(mix, jnp.concatenate([wide_high, wide_low, wide_high], 1))
        return unused

    lax.fori_loop(0, channels // LANES, one_group, 0)
    fetch.wait()
    depth = coarse_x + 2
    spread_x = interpolation_rows(fine_x, depth, 2, False)
    share = levels // len(out_refs)
    unroll = math.gcd(members // 2, 5)

    for slot, out_ref in enumerate(out_refs):
        for sub in range(share // EDGE):
            first = pl.multiple_of(lax.rem(me_ref[0] + slot, len(out_refs)) * share + sub * EDGE, EDGE)

            def stacked(k):
                rows = pl.ds(pl.multiple_of(k * levels + first, EDGE), EDGE)
                parts = [coarse[c, rows, :] for c in range(coarse_x + 1)]
                return jnp.concatenate(parts + [jnp.zeros((EDGE, fine_y), jnp.float32)], 0)

            def perturbation(k):
                return pert_ref[k, pl.ds(first, EDGE)].reshape(EDGE * fine_x, fine_y).astype(jnp.float32)

            def pairs(p, total):
                for i in range(unroll):
                    k = 2 * (unroll * p + i)
                    high, low = split_two(jnp.concatenate([stacked(k), stacked(k + 1)], 1))
                    fine = dot_nn(spread_x, jnp.concatenate([high, low], 0))
                    total = total + (fine[:, :fine_y] * perturbation(k) + fine[:, fine_y:] * perturbation(k + 1))
                return total

            total = lax.fori_loop(
                0, members // (2 * unroll), pairs, jnp.zeros((EDGE * fine_x, fine_y), jnp.float32)
            )
            out_ref[sub * EDGE:(sub + 1) * EDGE] = total.reshape(EDGE, fine_x, fine_y)


def backward_kernel(
    coarse_x, coarse_y, joined,
    me_ref, parts_refs, mix_ref, sigma_ref, static_ref, pert_hbm,
    grad_ref, center_ref, middle_refs, left_refs, right_refs,
    adjoint, coarse, pert_ref, sems,
):
    members, levels, fine_x, fine_y = pert_ref.shape
    channels = members * levels
    unroll = members // sems.shape[0]
    copies = []
    for p in range(sems.shape[0]):
        some = pl.ds(p * unroll, unroll)
        copies.append(pltpu.make_async_copy(pert_hbm.at[some], pert_ref.at[some], sems.at[p]))
        copies[p].start()
    share = levels // len(parts_refs)
    for slot, part in enumerate(parts_refs):
        first = lax.rem(me_ref[0] + len(parts_refs) - slot, len(parts_refs)) * share
        adjoint[pl.ds(first, share)] = part[...]
    grad_ref[...] = static_ref[...] + sigma_ref[...] * adjoint[...]
    depth = coarse_x + 2
    fold_x = interpolation_rows(fine_x, depth, 1, True)

    for p, copy in enumerate(copies):
        copy.wait()

        def one_level_group(group, unused):
            some = pl.ds(group * EDGE, EDGE)
            field = adjoint[some].reshape(EDGE * fine_x, fine_y)
            for k in range(p * unroll, (p + 1) * unroll):
                scaled = pert_ref[k, some].reshape(EDGE * fine_x, fine_y).astype(jnp.float32)
                high, low = split_two(scaled * field)
                both = dot_nn(fold_x, jnp.concatenate([high, low], 1))
                rows = pl.ds(pl.multiple_of(k * levels + group * EDGE, EDGE), EDGE)
                for c in range(coarse_x + 1):
                    piece = both[c * EDGE:(c + 1) * EDGE]
                    coarse[c, rows, :] = piece[:, :fine_y] + piece[:, fine_y:]
            return unused

        lax.fori_loop(0, levels // EDGE, one_level_group, 0)

    fold_y = interpolation((coarse_y + PAD, fine_y), 1, 0, EDGE)
    fold_y = jnp.concatenate([fold_y, fold_y], 1)
    high, low = mixing(mix_ref)
    mix = jnp.concatenate([high, high, low], 0)

    def one_group(g, unused):
        lanes = pl.ds(pl.multiple_of(g * LANES, LANES), LANES)
        rows = []
        for c in range(coarse_x + 1):
            high, low = split_two(coarse[c, lanes, :])
            narrow = dot_nt(fold_y, jnp.concatenate([high, low], 1))
            high, low = split_two(narrow)
            rows.append(dot_nn(jnp.concatenate([high, low, high], 1), mix)[None])
        field = jnp.concatenate(rows, 0) * SCALE
        empty = jnp.zeros((1,) + field.shape[1:], jnp.float32)
        for step in range(NSTEP):
            own = field + neighbours(field)
            field = jnp.concatenate([field, empty, empty], 0) + jnp.concatenate([empty, own, empty], 0) + jnp.concatenate(
                [empty, empty, field], 0
            )
        inside = field[REACH:REACH + coarse_x]
        up, down = field[:REACH], field[REACH + coarse_x:]
        if joined:
            none = jnp.zeros((coarse_x - REACH - 1,) + field.shape[1:], jnp.float32)
            outside = [jnp.concatenate([down, none], 0) + jnp.concatenate([none, empty, up], 0)]
        else:
            outside = [up, down]
        center_ref[:, :, lanes] = inside[:, EDGE:EDGE + coarse_y]
        for ref, value in zip(middle_refs, outside):
            ref[:, :, lanes] = value[:, EDGE:EDGE + coarse_y]
        for left, right, value in zip(left_refs, right_refs, [inside] + outside):
            for i in range(value.shape[0]):
                left[i * REACH:(i + 1) * REACH, lanes] = value[i, EDGE - REACH:EDGE]
                right[i * (REACH + 1):(i + 1) * (REACH + 1), lanes] = value[
                    i, EDGE + coarse_y:EDGE + coarse_y + REACH + 1
                ]
        return unused

    lax.fori_loop(0, channels // LANES, one_group, 0)


def fold_kernel(places, alpha_ref, center_ref, *refs):
    part_refs, out_ref = refs[:-1], refs[-1]
    out_ref[...] = alpha_ref[...] + center_ref[...]
    for (row, count, column, width), ref in zip(places, part_refs):
        if width == out_ref.shape[1]:
            out_ref[row:row + count] += ref[...]
        else:
            for i in range(count):
                out_ref[row + i, column:column + width, :] += ref[i * width:(i + 1) * width, :]


def shifted(value, by_x, by_y):
    count_x, count_y = lax.axis_size("tx"), lax.axis_size("ty")
    pairs = [
        (x * count_y + y, (x + by_x) % count_x * count_y + (y + by_y) % count_y)
        for x in range(count_x)
        for y in range(count_y)
    ]
    return lax.ppermute(value, ("tx", "ty"), pairs)


def ensemble(alpha, mix, ens_pert, me, beside):
    coarse_x, coarse_y, channels = alpha.shape
    members, levels, fine_x, fine_y = ens_pert.shape
    joined = lax.axis_size("tx") == 2
    ends = alpha[:, coarse_y - REACH:]
    starts = alpha[:, :REACH + 1]

    def flat(strip):
        return strip.reshape(-1, channels)

    if joined:
        other = shifted(alpha, 1, 0)
        above = below = other
        left_above = left_below = shifted(flat(ends), 1, 1)
        right_above = right_below = shifted(flat(starts), 1, -1)
        offsets = (coarse_x - REACH, 0)
    else:
        last = slice(coarse_x - REACH, coarse_x)
        first = slice(0, REACH + 1)
        above, below = shifted(alpha[last], 1, 0), shifted(alpha[first], -1, 0)
        left_above, left_below = shifted(flat(ends[last]), 1, 1), shifted(flat(ends[first]), -1, 1)
        right_above, right_below = shifted(flat(starts[last]), 1, -1), shifted(flat(starts[first]), -1, -1)
        offsets = (0, 0)
    left, right = shifted(flat(ends), 0, 1), shifted(flat(starts), 0, -1)
    left, beside = lax.optimization_barrier((left, beside))
    groups = lax.axis_size("mem")

    def kernel(*refs):
        ensemble_kernel(coarse_x, coarse_y, offsets, *refs[:12], refs[12:12 + groups], *refs[12 + groups:])

    parts = pl.pallas_call(
        kernel,
        out_shape=tuple(jax.ShapeDtypeStruct((levels // groups, fine_x, fine_y), jnp.float32) for _ in range(groups)),
        in_specs=[SMEM] + [VMEM] * 10 + [HBM],
        out_specs=(VMEM,) * groups,
        scratch_shapes=[
            pltpu.VMEM(ens_pert.shape, ens_pert.dtype),
            pltpu.SemaphoreType.DMA,
            pltpu.VMEM((coarse_x + 2 * REACH + 1, coarse_y + PAD, channels), jnp.float32),
            pltpu.VMEM((coarse_x + 1, channels, fine_y), jnp.float32),
        ],
        compiler_params=room(50),
        cost_estimate=pl.CostEstimate(flops=8 << 30, bytes_accessed=8 << 20, transcendentals=0),
        name="ensemble",
    )(me, alpha, above, below, left, left_above, left_below, right, right_above, right_below, mix, ens_pert)
    return parts, beside


def backward(alpha, adjoint_parts, mix, bg_sigma, static_ctrl, ens_pert, me):
    coarse_x, coarse_y, channels = alpha.shape
    members, levels, fine_x, fine_y = ens_pert.shape
    joined = lax.axis_size("tx") == 2
    groups = len(adjoint_parts)
    outside = [coarse_x] if joined else [REACH, REACH + 1]
    strips = [coarse_x] + outside
    shapes = [bg_sigma.shape, alpha.shape]
    shapes += [(rows, coarse_y, channels) for rows in outside]
    shapes += [(rows * REACH, channels) for rows in strips]
    shapes += [(rows * (REACH + 1), channels) for rows in strips]
    n_in, n_mid, n_strip = 5 + groups, len(outside), len(strips)

    def kernel(*refs):
        me_ref, parts, rest = refs[0], refs[1:1 + groups], refs[1 + groups:n_in]
        outs = refs[n_in:n_in + len(shapes)]
        middle = outs[2:2 + n_mid]
        left = outs[2 + n_mid:2 + n_mid + n_strip]
        right = outs[2 + n_mid + n_strip:]
        backward_kernel(
            coarse_x, coarse_y, joined, me_ref, parts, *rest,
            outs[0], outs[1], middle, left, right, *refs[n_in + len(shapes):]
        )

    results = pl.pallas_call(
        kernel,
        out_shape=tuple(jax.ShapeDtypeStruct(shape, jnp.float32) for shape in shapes),
        in_specs=[SMEM] + [VMEM] * (groups + 3) + [HBM],
        out_specs=(VMEM,) * len(shapes),
        scratch_shapes=[
            pltpu.VMEM(bg_sigma.shape, jnp.float32),
            pltpu.VMEM((coarse_x + 1, channels, fine_y), jnp.float32),
            pltpu.VMEM(ens_pert.shape, ens_pert.dtype),
            pltpu.SemaphoreType.DMA((members // math.gcd(members, 5),)),
        ],
        compiler_params=room(50),
        cost_estimate=pl.CostEstimate(flops=8 << 30, bytes_accessed=8 << 20, transcendentals=0),
        name="backward",
    )(me, *adjoint_parts, mix, bg_sigma, static_ctrl, ens_pert)
    grad_static, center = results[:2]
    middle = results[2:2 + n_mid]
    left, right = results[2 + n_mid:2 + n_mid + n_strip], results[2 + n_mid + n_strip:]
    last, wide = coarse_y - REACH, REACH + 1
    moves = [(1, 0, coarse_x)] if joined else [(-1, coarse_x - REACH, REACH), (1, 0, REACH + 1)]
    places, parts = [], []
    for (by, row, count), value, to_left, to_right in zip(moves, middle, left[1:], right[1:]):
        parts += [shifted(value, by, 0), shifted(to_left, by, -1), shifted(to_right, by, 1)]
        places += [(row, count, 0, coarse_y), (row, count, last, REACH), (row, count, 0, wide)]
    parts += [shifted(left[0], 0, -1), shifted(right[0], 0, 1)]
    places += [(0, coarse_x, last, REACH), (0, coarse_x, 0, wide)]
    grad_alpha = pl.pallas_call(
        functools.partial(fold_kernel, places),
        out_shape=jax.ShapeDtypeStruct(alpha.shape, jnp.float32),
        in_specs=[VMEM] * (2 + len(parts)),
        out_specs=VMEM,
        compiler_params=room(8),
        cost_estimate=pl.CostEstimate(flops=1 << 20, bytes_accessed=2 << 20, transcendentals=0),
        name="fold",
    )(alpha, center, *parts)
    return grad_alpha, grad_static


def owned_sum(parts):
    count = len(parts)
    total = parts[0]
    for d in range(1, count):
        total = total + lax.ppermute(parts[d], "mem", [(i, (i + d) % count) for i in range(count)])
    return total


def gathered(own):
    count = lax.axis_size("mem")
    return [own] + [lax.ppermute(own, "mem", [(i, (i + d) % count) for i in range(count)]) for d in range(1, count)]


def per_device(
    alpha,
    lv_sqrt,
    ens_pert,
    bg_sigma,
    static_ctrl,
    obs_owner,
    obs_column,
    obs_level,
    obs_frac,
    innovation,
    obs_rinv,
    obs_count,
):
    levels, fine_x, fine_y = bg_sigma.shape
    tiles = lax.axis_size("tx") * lax.axis_size("ty")
    capacity = 2 * obs_owner.shape[0] // tiles
    me = lax.axis_index("mem").astype(jnp.int32).reshape(1)
    outgoing, target = pack(
        tiles, levels, fine_x * fine_y, capacity,
        obs_count, obs_owner[:, 0], obs_column, obs_level, obs_frac, innovation, obs_rinv,
    )
    partial, outgoing = ensemble(alpha, lv_sqrt, ens_pert, me, outgoing)
    increment, outgoing = lax.optimization_barrier((owned_sum(partial), outgoing))
    incoming = lax.all_to_all(outgoing, ("tx", "ty"), split_axis=0, concat_axis=0, tiled=True)
    departure, adjoint = stencil(gathered(increment), incoming, bg_sigma, static_ctrl, me)
    total, departure = lax.optimization_barrier((owned_sum(adjoint), departure))
    returned = lax.all_to_all(departure, ("tx", "ty"), split_axis=0, concat_axis=0, tiled=True)
    departures = unpack(target, returned.reshape(-1, BLOCK))
    parts, departures = lax.optimization_barrier((gathered(total), departures))
    grad_alpha, grad_static = backward(alpha, parts, lv_sqrt, bg_sigma, static_ctrl, ens_pert, me)
    return (grad_alpha, grad_static, departures)


def solution(mesh):
    placed = (
        P("tx", "ty", "mem"),
        P(),
        P("mem", None, "tx", "ty"),
        P(None, "tx", "ty"),
        P(None, "tx", "ty"),
        P(("tx", "ty", "mem"), None),
        P(("tx", "ty", "mem")),
        P(("tx", "ty", "mem")),
        P(None, ("tx", "ty", "mem")),
        P(("tx", "ty", "mem")),
        P(("tx", "ty", "mem")),
        P(("tx", "ty", "mem")),
    )
    return jax.shard_map(
        per_device,
        mesh=mesh,
        in_specs=placed,
        out_specs=(P("tx", "ty", "mem"), P(None, "tx", "ty"), P(("tx", "ty", "mem"))),
        check_vma=False,
    )
```

```python
import functools
import math

import jax
import jax.numpy as jnp
from jax import lax
from jax.experimental import pallas as pl
from jax.experimental.pallas import tpu as pltpu
from jax.sharding import PartitionSpec as P

RATIO = 4
NSTEP = 4
NU = 0.2
VMEM = pl.BlockSpec(memory_space=pltpu.VMEM)
SMEM = pl.BlockSpec(memory_space=pltpu.SMEM)
HBM = pl.BlockSpec(memory_space=pltpu.HBM)


def room(mebibytes):
    return pltpu.CompilerParams(vmem_limit_bytes=mebibytes << 20)

BLOCK = 256
LANES = 128
NARROW = 8
WIDE = 16
HALF = jnp.bfloat16


def split_two(value):
    high = value.astype(HALF)
    return high, (value - high.astype(jnp.float32)).astype(HALF)


def dot_nt(a, b):
    return lax.dot_general(a, b, (((1,), (1,)), ((), ())), preferred_element_type=jnp.float32)


def dot_nn(a, b):
    return jnp.dot(a, b, preferred_element_type=jnp.float32)


def iota(shape, dim):
    return lax.broadcasted_iota(jnp.int32, shape, dim)


def pack_kernel(
    tiles, levels, plane, capacity,
    count_ref, *refs,
):
    sources, (out_ref, target_ref, carry, total, gathered, *held), sems = refs[:3], refs[3:-1], refs[-1]
    copies = [pltpu.make_async_copy(source, here, sems.at[i]) for i, (source, here) in enumerate(zip(sources, held))]
    for copy in copies:
        copy.start()
    ints_ref, floats_ref, frac_ref = held
    size = target_ref.shape[0]
    owner_ref, level_ref, column_ref = [ints_ref.at[pl.ds(i * size, size)] for i in range(3)]
    innov_ref, rinv_ref = [floats_ref.at[pl.ds(i * size, size)] for i in range(2)]
    blocks = target_ref.shape[0] * LANES // BLOCK
    keys = tiles * levels
    deep = capacity // BLOCK
    slot_rows = tiles * deep
    group = 4
    count = count_ref[0]

    def row_of(ref, j):
        pair = ref[pl.ds(2 * j, 2), :]
        return jnp.concatenate([pair[0:1], pair[1:2]], 1)

    def onehot(j):
        live = iota((1, BLOCK), 1) + j * BLOCK < count
        key = jnp.where(live, row_of(owner_ref, j) * levels + row_of(level_ref, j), -1)
        return live, iota((keys, BLOCK), 0) == key

    ones = jnp.ones((BLOCK, LANES), HALF)
    total[...] = jnp.zeros_like(total)
    for copy in copies[:1]:
        copy.wait()

    def count_group(g, unused):
        masks = [onehot(g * group + i)[1] for i in range(group)]
        counted = jnp.concatenate([jnp.where(mask, 1.0, 0.0).astype(HALF) for mask in masks], 1)
        total[...] += dot_nn(counted, jnp.concatenate([ones] * group, 0))
        return unused

    lax.fori_loop(0, blocks // group, count_group, 0)
    for copy in copies[1:]:
        copy.wait()
    high = jnp.floor(total[...] * (1.0 / LANES))
    low = total[...] - high * LANES
    row_key, col_key = iota((keys, keys), 0), iota((keys, keys), 1)
    before = jnp.where((col_key < row_key) & (col_key // levels == row_key // levels), 1.0, 0.0).astype(HALF)
    start = dot_nn(before, high.astype(HALF)) * LANES + dot_nn(before, low.astype(HALF))
    carry[...] = start + ((iota((keys, LANES), 0) // levels) * capacity).astype(jnp.float32)

    earlier = jnp.where(iota((BLOCK, BLOCK), 0) < iota((BLOCK, BLOCK), 1), 1.0, 0.0).astype(HALF)
    prefix = jnp.concatenate([earlier, ones], 1)
    gathered[...] = jnp.zeros_like(gathered)

    def place(j):
        live, mask = onehot(j)
        ranks = dot_nn(jnp.where(mask, 1.0, 0.0).astype(HALF), prefix)
        now = carry[...]
        here = ranks[:, :BLOCK] + jnp.concatenate([now] * (BLOCK // LANES), 1)
        carry[...] = now + ranks[:, BLOCK:]
        slot = jnp.sum(jnp.where(mask, here, 0.0), 0, keepdims=True)
        target = jnp.where(live, slot.astype(jnp.int32), -1)
        target_ref[pl.ds(2 * j, 2), :] = jnp.concatenate([target[:, :LANES], target[:, LANES:]], 0)
        rows = jnp.where(iota((slot_rows, BLOCK), 0) == (target >> 8), 1.0, 0.0).astype(HALF)
        lanes = jnp.where(iota((BLOCK, BLOCK), 0) == (target & (BLOCK - 1)), 1.0, 0.0).astype(HALF)
        column = row_of(column_ref, j)
        frac = frac_ref[:, pl.ds(pl.multiple_of(j * BLOCK, BLOCK), BLOCK)]
        terms = []
        for value in (frac[0:1], frac[1:2], frac[2:3], row_of(innov_ref, j), row_of(rinv_ref, j)):
            terms.extend(split_two(jnp.broadcast_to(value, (16, BLOCK))))
        for value in (row_of(level_ref, j), column >> 7, column & (LANES - 1)):
            terms.append(jnp.broadcast_to(value.astype(jnp.float32), (16, BLOCK)).astype(HALF))
        spread = [rows * jnp.concatenate([term] * (slot_rows // 16), 0) for term in terms]
        return jnp.concatenate(spread, 0), lanes

    def scatter_group(g, unused):
        placed = [place(g * group + i) for i in range(group)]
        left = jnp.concatenate([a for a, b in placed], 1)
        right = jnp.concatenate([b for a, b in placed], 1)
        gathered[...] += dot_nt(left, right)
        return unused

    lax.fori_loop(0, blocks // group, scatter_group, 0)

    def part(index, tile):
        begin = index * slot_rows + tile * deep
        return gathered[begin:begin + deep, :]

    for tile in range(tiles):
        for p in range(5):
            out_ref[tile, p * deep:(p + 1) * deep, :] = part(2 * p, tile) + part(2 * p + 1, tile)
        base = part(10, tile) * plane + part(11, tile) * LANES + part(12, tile)
        out_ref[tile, 5 * deep:6 * deep, :] = base


def pack(tiles, levels, plane, capacity, count, owner, column, level, frac, innov, rinv):
    slots = owner.shape[0]
    rows = slots // LANES
    deep = capacity // BLOCK
    values = [jnp.concatenate(some).reshape(-1, LANES) for some in ((owner, level, column), (innov, rinv))] + [frac]
    vmem = pl.BlockSpec(memory_space=pltpu.VMEM)
    return pl.pallas_call(
        functools.partial(pack_kernel, tiles, levels, plane, capacity),
        out_shape=(
            jax.ShapeDtypeStruct((tiles, 6 * deep, BLOCK), jnp.float32),
            jax.ShapeDtypeStruct((rows, LANES), jnp.int32),
        ),
        in_specs=[SMEM] + [HBM] * 3,
        out_specs=(vmem, vmem),
        scratch_shapes=[
            pltpu.VMEM((tiles * levels, LANES), jnp.float32),
            pltpu.VMEM((tiles * levels, LANES), jnp.float32),
            pltpu.VMEM((13 * tiles * deep, BLOCK), jnp.float32),
        ]
        + [pltpu.VMEM(value.shape, value.dtype) for value in values]
        + [pltpu.SemaphoreType.DMA((len(values),))],
        compiler_params=room(16),
        cost_estimate=pl.CostEstimate(flops=8 << 30, bytes_accessed=1 << 20, transcendentals=0),
        name="pack",
    )(count, *values)


def stencil_kernel(
    me_ref, parts_refs, sigma_ref, static_ref, incoming_ref,
    dep_ref, adj_refs,
    field, field_t, adjoint, spans, spans_ref, sem,
):
    levels, fine_x, fine_y = sigma_ref.shape
    sources, packed_rows, block = incoming_ref.shape
    deep = packed_rows // 6
    plane = fine_x * fine_y
    chunk = LANES // fine_x
    groups = len(parts_refs)
    share = levels // groups
    rows = levels * fine_x
    me = me_ref[0]
    halves = block // LANES
    column = iota((sources * deep, LANES), 1)
    found = jnp.zeros((sources * deep, LANES), jnp.int32)
    for half in range(halves):
        lanes = slice(half * LANES, (half + 1) * LANES)
        used = incoming_ref[:, 4 * deep:5 * deep, lanes].reshape(sources * deep, LANES) > 0.0
        level = jnp.floor(incoming_ref[:, 5 * deep:, lanes].reshape(sources * deep, LANES) * (1.0 / plane))
        lowest = jnp.min(jnp.where(used, level, float(levels)), 1, keepdims=True).astype(jnp.int32)
        highest = jnp.max(jnp.where(used, level, -1.0), 1, keepdims=True).astype(jnp.int32)
        found = jnp.where((column == 2 * half) & (highest >= 0), lowest, found)
        found = jnp.where((column == 2 * half + 1) & (highest >= 0), highest + 2 - lowest, found)
    spans[...] = found
    fetch = pltpu.make_async_copy(spans, spans_ref, sem)
    fetch.start()
    adjoint[...] = jnp.zeros_like(adjoint)
    dep_ref[...] = jnp.zeros_like(dep_ref)
    field[rows:, :] = jnp.zeros((field.shape[0] - rows, fine_y), jnp.float32)
    for slot, part in enumerate(parts_refs):
        start = lax.rem(me + groups - slot, groups) * share
        static = sigma_ref[pl.ds(start, share)] * static_ref[pl.ds(start, share)]
        where = pl.ds(pl.multiple_of(start * fine_x, LANES), share * fine_x)
        field[where, :] = (part[...] + static).reshape(share * fine_x, fine_y)
    for shift in range(chunk):
        field_t[shift, :, rows:] = jnp.zeros((2 * fine_y, field_t.shape[2] - rows), HALF)
        for g in range(rows // LANES):
            begin = shift * fine_x + g * LANES
            high, low = split_two(field[begin:begin + LANES, :].T)
            field_t[shift, :fine_y, g * LANES:(g + 1) * LANES] = high
            field_t[shift, fine_y:, g * LANES:(g + 1) * LANES] = low

    fetch.wait()

    def block_of(source, at, half):
        def row(p):
            return incoming_ref[source, pl.ds(p * deep + at, 1), :][:, half * LANES:(half + 1) * LANES]

        base = row(5)
        level = jnp.floor(base * (1.0 / plane))
        rest = base - level * plane
        across = jnp.floor(rest * (1.0 / fine_y))
        along = rest - across * fine_y
        frac_x, frac_y, frac_l = row(0), row(1), row(2)
        rows_x = iota((fine_x, LANES), 0).astype(jnp.float32)
        pick_x = jnp.where(rows_x == across, 1.0 - frac_x, 0.0) + jnp.where(rows_x == across + 1.0, frac_x, 0.0)
        rows_y = iota((fine_y, LANES), 0).astype(jnp.float32)
        pick_y = jnp.where(rows_y == along, 1.0 - frac_y, 0.0) + jnp.where(rows_y == along + 1.0, frac_y, 0.0)

        def weights(bottom, reach):
            offset = level - bottom.astype(jnp.float32)
            picks = []
            for g in range(reach):
                pick_l = jnp.where(offset == float(g), 1.0 - frac_l, 0.0) + jnp.where(offset == float(g - 1), frac_l, 0.0)
                picks.append(pick_x * pick_l)
            return jnp.concatenate(split_two(jnp.concatenate(picks, 0)), 1)

        def finish(picked):
            departure = jnp.sum(picked * pick_y, 0, keepdims=True) - row(3)
            turned = jnp.concatenate(split_two((pick_y * (row(4) * departure)).T), 1)
            return departure, jnp.concatenate([turned, turned], 0)

        return weights, finish

    def look(bottom, pick):
        lanes = pl.ds(pl.multiple_of((bottom // chunk) * LANES, LANES), pick.shape[0])
        seen = dot_nn(field_t[lax.rem(bottom, chunk), :, lanes], pick)
        return seen[:fine_y, :LANES] + (seen[:fine_y, LANES:] + seen[fine_y:, :LANES])

    def spread(pick, term):
        both = dot_nn(pick, term)
        return both[:, :fine_y] + both[:, fine_y:]

    def rows_at(bottom, reach):
        return pl.ds(pl.multiple_of(bottom * fine_x, fine_x), reach * fine_x)

    def together(blocks, bottoms, reach):
        parts = [block_of(*block) for block in blocks]
        picks = [weights(bottom, reach) for (weights, finish), bottom in zip(parts, bottoms)]
        seen = [look(bottom, pick) for bottom, pick in zip(bottoms, picks)]
        done = [finish(value) for (weights, finish), value in zip(parts, seen)]
        adds = [spread(pick, term) for pick, (departure, term) in zip(picks, done)]
        keep(blocks, [departure for departure, term in done])
        for bottom, add in zip(bottoms, adds):
            adjoint[rows_at(bottom, reach), :] += add

    def keep(blocks, departures):
        for i in range(0, len(blocks), halves):
            source, at, half = blocks[i]
            dep_ref[source, pl.ds(at, 1), :] = jnp.concatenate(departures[i:i + halves], 1)

    def alone(block, first, needed):
        weights, finish = block_of(*block)
        windows = (needed + WIDE - 1) // WIDE

        def forward(w, total):
            bottom = first + w * WIDE
            return total + look(bottom, weights(bottom, WIDE))

        departure, term = finish(lax.fori_loop(0, windows, forward, jnp.zeros((fine_y, LANES), jnp.float32)))

        def backward(w, unused):
            bottom = first + w * WIDE
            adjoint[rows_at(bottom, WIDE), :] += spread(weights(bottom, WIDE), term)
            return unused

        lax.fori_loop(0, windows, backward, 0)
        return departure

    step = 2 if deep % 2 == 0 else 1

    def one_step(i, unused):
        source, at = i // (deep // step), lax.rem(i, deep // step) * step
        blocks = [(source, at + r, half) for r in range(step) for half in range(halves)]
        numbers = [(source * deep + at + r, half) for r in range(step) for half in range(halves)]
        bottoms = [spans_ref[row, 2 * half] for row, half in numbers]
        needs = [spans_ref[row, 2 * half + 1] for row, half in numbers]
        most = functools.reduce(jnp.maximum, needs)

        @pl.when((most > 0) & (most <= NARROW))
        def _():
            together(blocks, bottoms, NARROW)

        @pl.when((most > NARROW) & (most <= WIDE))
        def _():
            together(blocks, bottoms, WIDE)

        @pl.when(most > WIDE)
        def _():
            keep(blocks, [alone(*each) for each in zip(blocks, bottoms, needs)])

        return unused

    lax.fori_loop(0, sources * deep // step, one_step, 0)
    for slot, adj_ref in enumerate(adj_refs):
        start = lax.rem(me + slot, groups) * share * fine_x
        adj_ref[...] = adjoint[pl.ds(pl.multiple_of(start, LANES), share * fine_x), :].reshape(share, fine_x, fine_y)


def stencil(parts, incoming, bg_sigma, static_ctrl, me):
    levels, fine_x, fine_y = bg_sigma.shape
    sources, packed_rows, block = incoming.shape
    deep, groups = packed_rows // 6, len(parts)
    rows = levels * fine_x
    padded = rows + WIDE * fine_x

    def kernel(*refs):
        parts_end = 1 + groups
        stencil_kernel(
            refs[0], refs[1:parts_end], *refs[parts_end:parts_end + 4],
            refs[parts_end + 4:parts_end + 4 + groups], *refs[parts_end + 4 + groups:]
        )

    results = pl.pallas_call(
        kernel,
        out_shape=(jax.ShapeDtypeStruct((sources, deep, block), jnp.float32),)
        + tuple(jax.ShapeDtypeStruct(part.shape, jnp.float32) for part in parts),
        in_specs=[SMEM] + [VMEM] * (groups + 3),
        out_specs=(VMEM,) * (1 + groups),
        scratch_shapes=[
            pltpu.VMEM((padded, fine_y), jnp.float32),
            pltpu.VMEM((LANES // fine_x, 2 * fine_y, padded), HALF),
            pltpu.VMEM((padded, fine_y), jnp.float32),
            pltpu.VMEM((sources * deep, LANES), jnp.int32),
            pltpu.SMEM((sources * deep, LANES), jnp.int32),
            pltpu.SemaphoreType.DMA,
        ],
        compiler_params=room(20),
        cost_estimate=pl.CostEstimate(flops=16 << 30, bytes_accessed=1 << 20, transcendentals=0),
        name="stencil",
    )(me, *parts, bg_sigma, static_ctrl, incoming)
    return results[0], results[1:]


def unpack_kernel(target_ref, table_ref, out_ref):
    slot_rows = table_ref.shape[0]
    high, low = split_two(table_ref[...])
    both = jnp.concatenate([high.astype(jnp.float32), low.astype(jnp.float32)], 0)
    turned = both.T.astype(HALF)
    group = 4

    def some_blocks(g, unused):
        for i in range(group):
            pair = target_ref[pl.ds(2 * (g * group + i), 2), :]
            target = jnp.concatenate([pair[0:1], pair[1:2]], 1)
            rows = jnp.where(iota((slot_rows, BLOCK), 0) == (target >> 8), 1.0, 0.0).astype(HALF)
            lines = dot_nn(turned, jnp.concatenate([rows, rows], 0))
            lane = iota((BLOCK, BLOCK), 0) == (target & (BLOCK - 1))
            found = jnp.sum(jnp.where(lane, lines, 0.0), 0, keepdims=True)
            out_ref[pl.ds(2 * (g * group + i), 2), :] = jnp.concatenate([found[:, :LANES], found[:, LANES:]], 0)
        return unused

    lax.fori_loop(0, target_ref.shape[0] // (2 * group), some_blocks, 0)


def unpack(target, table):
    vmem = pl.BlockSpec(memory_space=pltpu.VMEM)
    return pl.pallas_call(
        unpack_kernel,
        out_shape=jax.ShapeDtypeStruct(target.shape, jnp.float32),
        in_specs=[vmem, vmem],
        out_specs=vmem,
        compiler_params=room(8),
        cost_estimate=pl.CostEstimate(flops=2 << 30, bytes_accessed=1 << 18, transcendentals=0),
        name="unpack",
    )(target, table).reshape(-1)


REACH = NSTEP
EDGE = 8
PAD = 2 * EDGE
SCALE = NU**NSTEP


def interpolation(shape, fine_dim, coarse_dim, shift):
    fine, coarse = iota(shape, fine_dim), iota(shape, coarse_dim) - shift
    frac = (fine % RATIO).astype(jnp.float32) * (1.0 / RATIO)
    low = jnp.where(coarse == fine // RATIO, 1.0 - frac, 0.0)
    return (low + jnp.where(coarse == fine // RATIO + 1, frac, 0.0)).astype(HALF)


def interpolation_rows(fine_x, depth, copies, transposed):
    long, short = EDGE * fine_x, EDGE * depth
    shape = (short, long) if transposed else (long, copies * short)
    fine, coarse = iota(shape, 1 if transposed else 0), iota(shape, 0 if transposed else 1)
    for copy in range(1, copies):
        coarse = jnp.where(coarse >= short, coarse - short, coarse)
    place, target = fine % fine_x, coarse // EDGE
    frac = (place % RATIO).astype(jnp.float32) * (1.0 / RATIO)
    low = jnp.where(target == place // RATIO, 1.0 - frac, 0.0)
    weight = low + jnp.where(target == place // RATIO + 1, frac, 0.0)
    return jnp.where(fine // fine_x == coarse % EDGE, weight, 0.0).astype(HALF)


def mixing(mix_ref):
    levels = mix_ref.shape[0]
    tile = jnp.where(iota((LANES, levels), 0) % levels == iota((LANES, levels), 1), 1.0, 0.0).astype(HALF)
    same = iota((LANES, LANES), 0) // levels == iota((LANES, LANES), 1) // levels
    terms = []
    for term in split_two(mix_ref[...]):
        tiled = dot_nt(dot_nn(tile, term).astype(HALF), tile)
        terms.append(jnp.where(same, tiled, 0.0).astype(HALF))
    return terms


def neighbours(field):
    width = field.shape[1]
    return pltpu.roll(field, 1, 1) + pltpu.roll(field, width - 1, 1)


def ensemble_kernel(
    coarse_x, coarse_y, offsets,
    me_ref, alpha_ref, above_ref, below_ref,
    left_ref, left_above_ref, left_below_ref, right_ref, right_above_ref, right_below_ref,
    mix_ref, pert_hbm, out_refs, pert_ref, sem, ext, coarse,
):
    members, levels, fine_x, fine_y = pert_ref.shape
    channels = alpha_ref.shape[2]
    fetch = pltpu.make_async_copy(pert_hbm, pert_ref, sem)
    fetch.start()
    ext[:, :EDGE, :] = jnp.zeros((ext.shape[0], EDGE, channels), jnp.float32)
    ext[:, EDGE + coarse_y:, :] = jnp.zeros((ext.shape[0], EDGE, channels), jnp.float32)
    above, below = offsets
    groups = (
        (0, REACH, above, above_ref, left_above_ref, right_above_ref),
        (REACH, coarse_x, 0, alpha_ref, left_ref, right_ref),
        (REACH + coarse_x, REACH + 1, below, below_ref, left_below_ref, right_below_ref),
    )
    for begin, count, offset, middle, left, right in groups:
        ext[begin:begin + count, EDGE:EDGE + coarse_y, :] = middle[offset:offset + count]
        for i in range(count):
            at = offset + i
            ext[begin + i, EDGE - REACH:EDGE, :] = left[at * REACH:(at + 1) * REACH, :]
            ext[begin + i, EDGE + coarse_y:EDGE + coarse_y + REACH + 1, :] = right[
                at * (REACH + 1):(at + 1) * (REACH + 1), :
            ]
    spread_y = interpolation((coarse_y + PAD, fine_y), 1, 0, EDGE)
    spread_y = jnp.concatenate([spread_y, spread_y], 0)
    high, low = mixing(mix_ref)
    mix = jnp.concatenate([high, high, low], 1)

    def one_group(g, unused):
        lanes = pl.ds(pl.multiple_of(g * LANES, LANES), LANES)
        field = ext[:, :, lanes]
        for step in range(NSTEP):
            inner = field[1:-1]
            field = inner + field[2:] + field[:-2] + neighbours(inner)
        high, low = split_two(field * SCALE)
        both = jnp.concatenate([high.astype(jnp.float32), low.astype(jnp.float32)], 1)
        for c in range(coarse_x + 1):
            wide_high, wide_low = split_two(dot_nn(both[c].T.astype(HALF), spread_y))
            coarse[c, lanes, :] = dot_nn(mix, jnp.concatenate([wide_high, wide_low, wide_high], 0))
        return unused

    lax.fori_loop(0, channels // LANES, one_group, 0)
    fetch.wait()
    depth = coarse_x + 2
    spread_x = interpolation_rows(fine_x, depth, 2, False)
    share = levels // len(out_refs)
    unroll = math.gcd(members // 2, 5)

    for slot, out_ref in enumerate(out_refs):
        for sub in range(share // EDGE):
            first = pl.multiple_of(lax.rem(me_ref[0] + slot, len(out_refs)) * share + sub * EDGE, EDGE)

            def stacked(k):
                rows = pl.ds(pl.multiple_of(k * levels + first, EDGE), EDGE)
                parts = [coarse[c, rows, :] for c in range(coarse_x + 1)]
                return jnp.concatenate(parts + [jnp.zeros((EDGE, fine_y), jnp.float32)], 0)

            def perturbation(k):
                return pert_ref[k, pl.ds(first, EDGE)].reshape(EDGE * fine_x, fine_y).astype(jnp.float32)

            def pairs(p, total):
                for i in range(unroll):
                    k = 2 * (unroll * p + i)
                    high, low = split_two(jnp.concatenate([stacked(k), stacked(k + 1)], 1))
                    fine = dot_nn(spread_x, jnp.concatenate([high, low], 0))
                    total = total + (fine[:, :fine_y] * perturbation(k) + fine[:, fine_y:] * perturbation(k + 1))
                return total

            total = lax.fori_loop(
                0, members // (2 * unroll), pairs, jnp.zeros((EDGE * fine_x, fine_y), jnp.float32)
            )
            out_ref[sub * EDGE:(sub + 1) * EDGE] = total.reshape(EDGE, fine_x, fine_y)


def backward_kernel(
    coarse_x, coarse_y, joined, base,
    me_ref, parts_refs, mix_ref, sigma_ref, static_ref, pert_hbm,
    earlier_refs, grad_ref, center_ref, middle_refs, left_refs, right_refs,
    adjoint, coarse, pert_ref, sems,
):
    members, levels, fine_x, fine_y = pert_ref.shape
    channels = members * levels
    unroll = members // sems.shape[0]
    copies = []
    for p in range(sems.shape[0]):
        some = pl.ds(p * unroll, unroll)
        there = pert_hbm.at[pl.ds(base + p * unroll, unroll)]
        copies.append(pltpu.make_async_copy(there, pert_ref.at[some], sems.at[p]))
        copies[p].start()
    share = levels // len(parts_refs)
    for slot, part in enumerate(parts_refs):
        first = lax.rem(me_ref[0] + len(parts_refs) - slot, len(parts_refs)) * share
        adjoint[pl.ds(first, share)] = part[...]
    shift = 0
    for earlier, strip in zip(earlier_refs, left_refs + right_refs):
        shift = earlier.shape[1]
        strip[:, :shift] = earlier[...]
    if grad_ref is not None:
        grad_ref[...] = static_ref[...] + sigma_ref[...] * adjoint[...]
    depth = coarse_x + 2
    fold_x = interpolation_rows(fine_x, depth, 1, True)

    for p, copy in enumerate(copies):
        copy.wait()

        def one_level_group(group, unused):
            some = pl.ds(group * EDGE, EDGE)
            field = adjoint[some].reshape(EDGE * fine_x, fine_y)
            for k in range(p * unroll, (p + 1) * unroll):
                scaled = pert_ref[k, some].reshape(EDGE * fine_x, fine_y).astype(jnp.float32)
                high, low = split_two(scaled * field)
                both = dot_nn(fold_x, jnp.concatenate([high, low], 1))
                rows = pl.ds(pl.multiple_of(k * levels + group * EDGE, EDGE), EDGE)
                for c in range(coarse_x + 1):
                    piece = both[c * EDGE:(c + 1) * EDGE]
                    coarse[c, rows, :] = piece[:, :fine_y] + piece[:, fine_y:]
            return unused

        lax.fori_loop(0, levels // EDGE, one_level_group, 0)

    fold_y = interpolation((coarse_y + PAD, fine_y), 1, 0, EDGE)
    fold_y = jnp.concatenate([fold_y, fold_y], 1)
    high, low = mixing(mix_ref)
    mix = jnp.concatenate([high, high, low], 0)

    def one_group(g, unused):
        lanes = pl.ds(pl.multiple_of(g * LANES, LANES), LANES)
        rows = []
        for c in range(coarse_x + 1):
            high, low = split_two(coarse[c, lanes, :])
            narrow = dot_nt(fold_y, jnp.concatenate([high, low], 1))
            high, low = split_two(narrow)
            rows.append(dot_nn(jnp.concatenate([high, low, high], 1), mix)[None])
        field = jnp.concatenate(rows, 0) * SCALE
        empty = jnp.zeros((1,) + field.shape[1:], jnp.float32)
        for step in range(NSTEP):
            own = field + neighbours(field)
            field = jnp.concatenate([field, empty, empty], 0) + jnp.concatenate([empty, own, empty], 0) + jnp.concatenate(
                [empty, empty, field], 0
            )
        shifted_lanes = pl.ds(pl.multiple_of(shift + g * LANES, LANES), LANES)
        inside = field[REACH:REACH + coarse_x]
        up, down = field[:REACH], field[REACH + coarse_x:]
        if joined:
            none = jnp.zeros((coarse_x - REACH - 1,) + field.shape[1:], jnp.float32)
            outside = [jnp.concatenate([down, none], 0) + jnp.concatenate([none, empty, up], 0)]
        else:
            outside = [up, down]
        center_ref[:, :, lanes] = inside[:, EDGE:EDGE + coarse_y]
        for ref, value in zip(middle_refs, outside):
            ref[:, :, lanes] = value[:, EDGE:EDGE + coarse_y]
        for left, right, value in zip(left_refs, right_refs, [inside] + outside):
            for i in range(value.shape[0]):
                left[i * REACH:(i + 1) * REACH, shifted_lanes] = value[i, EDGE - REACH:EDGE]
                right[i * (REACH + 1):(i + 1) * (REACH + 1), shifted_lanes] = value[
                    i, EDGE + coarse_y:EDGE + coarse_y + REACH + 1
                ]
        return unused

    lax.fori_loop(0, channels // LANES, one_group, 0)


def fold_kernel(places, alpha_ref, *refs):
    part_refs, out_ref = refs[:-1], refs[-1]
    out_ref[...] = alpha_ref[...]
    for (row, count, column, width, begin), ref in zip(places, part_refs):
        lanes = slice(begin, begin + ref.shape[-1])
        if width == out_ref.shape[1]:
            out_ref[row:row + count, :, lanes] += ref[...]
        else:
            for i in range(count):
                out_ref[row + i, column:column + width, lanes] += ref[i * width:(i + 1) * width, :]


def shifted(value, by_x, by_y):
    count_x, count_y = lax.axis_size("tx"), lax.axis_size("ty")
    pairs = [
        (x * count_y + y, (x + by_x) % count_x * count_y + (y + by_y) % count_y)
        for x in range(count_x)
        for y in range(count_y)
    ]
    return lax.ppermute(value, ("tx", "ty"), pairs)


def ensemble(alpha, mix, ens_pert, me, beside):
    coarse_x, coarse_y, channels = alpha.shape
    members, levels, fine_x, fine_y = ens_pert.shape
    joined = lax.axis_size("tx") == 2
    ends = alpha[:, coarse_y - REACH:]
    starts = alpha[:, :REACH + 1]

    def flat(strip):
        return strip.reshape(-1, channels)

    if joined:
        other = shifted(alpha, 1, 0)
        above = below = other
        left_above = left_below = shifted(flat(ends), 1, 1)
        right_above = right_below = shifted(flat(starts), 1, -1)
        offsets = (coarse_x - REACH, 0)
    else:
        last = slice(coarse_x - REACH, coarse_x)
        first = slice(0, REACH + 1)
        above, below = shifted(alpha[last], 1, 0), shifted(alpha[first], -1, 0)
        left_above, left_below = shifted(flat(ends[last]), 1, 1), shifted(flat(ends[first]), -1, 1)
        right_above, right_below = shifted(flat(starts[last]), 1, -1), shifted(flat(starts[first]), -1, -1)
        offsets = (0, 0)
    left, right = shifted(flat(ends), 0, 1), shifted(flat(starts), 0, -1)
    left, beside = lax.optimization_barrier((left, beside))
    groups = lax.axis_size("mem")

    def kernel(*refs):
        ensemble_kernel(coarse_x, coarse_y, offsets, *refs[:12], refs[12:12 + groups], *refs[12 + groups:])

    parts = pl.pallas_call(
        kernel,
        out_shape=tuple(jax.ShapeDtypeStruct((levels // groups, fine_x, fine_y), jnp.float32) for _ in range(groups)),
        in_specs=[SMEM] + [VMEM] * 10 + [HBM],
        out_specs=(VMEM,) * groups,
        scratch_shapes=[
            pltpu.VMEM(ens_pert.shape, ens_pert.dtype),
            pltpu.SemaphoreType.DMA,
            pltpu.VMEM((coarse_x + 2 * REACH + 1, coarse_y + PAD, channels), jnp.float32),
            pltpu.VMEM((coarse_x + 1, channels, fine_y), jnp.float32),
        ],
        compiler_params=room(50),
        cost_estimate=pl.CostEstimate(flops=8 << 30, bytes_accessed=8 << 20, transcendentals=0),
        name="ensemble",
    )(me, alpha, above, below, left, left_above, left_below, right, right_above, right_below, mix, ens_pert)
    return parts, beside


def backward_chunk(alpha, adjoint_parts, mix, bg_sigma, static_ctrl, ens_pert, me, begin, end, earlier, before):
    coarse_x, coarse_y = alpha.shape[:2]
    levels, fine_x, fine_y = ens_pert.shape[1:]
    members = end - begin
    channels = members * levels
    joined = lax.axis_size("tx") == 2
    groups = len(adjoint_parts)
    outside = [coarse_x] if joined else [REACH, REACH + 1]
    strips = [coarse_x] + outside
    shapes = [(coarse_x, coarse_y, channels)]
    shapes += [(rows, coarse_y, channels) for rows in outside]
    shapes += [(rows * REACH, end * levels) for rows in strips]
    shapes += [(rows * (REACH + 1), end * levels) for rows in strips]
    last = end == ens_pert.shape[0]
    if last:
        shapes += [bg_sigma.shape]
    n_in, n_mid, n_strip = 5 + groups + len(earlier), len(outside), len(strips)

    def kernel(*refs):
        me_ref, parts, rest = refs[0], refs[1:1 + groups], refs[1 + groups:5 + groups]
        outs = refs[n_in:n_in + len(shapes)]
        middle = outs[1:1 + n_mid]
        left = outs[1 + n_mid:1 + n_mid + n_strip]
        right = outs[1 + n_mid + n_strip:1 + n_mid + 2 * n_strip]
        backward_kernel(
            coarse_x, coarse_y, joined, begin, me_ref, parts, *rest, refs[5 + groups:n_in],
            outs[-1] if last else None, outs[0], middle, left, right, *refs[n_in + len(shapes):]
        )

    results = pl.pallas_call(
        kernel,
        out_shape=tuple(jax.ShapeDtypeStruct(shape, jnp.float32) for shape in shapes),
        in_specs=[SMEM] + [VMEM] * (groups + 3) + [HBM] + [VMEM] * len(earlier),
        out_specs=(VMEM,) * len(shapes),
        scratch_shapes=[
            pltpu.VMEM(bg_sigma.shape, jnp.float32),
            pltpu.VMEM((coarse_x + 1, channels, fine_y), jnp.float32),
            pltpu.VMEM((members,) + ens_pert.shape[1:], ens_pert.dtype),
            pltpu.SemaphoreType.DMA((members // 4,)),
        ],
        compiler_params=room(50),
        cost_estimate=pl.CostEstimate(flops=4 << 30, bytes_accessed=4 << 20, transcendentals=0),
        name="backward",
    )(me, *adjoint_parts, mix, bg_sigma, static_ctrl, ens_pert, *earlier)
    edges = results[1 + n_mid:1 + n_mid + 2 * n_strip]
    moves = [(1, 0, coarse_x)] if joined else [(-1, coarse_x - REACH, REACH), (1, 0, REACH + 1)]
    places, parts = [(0, coarse_x, 0, coarse_y, begin * levels)], [results[0]]
    for (by, row, count), value in zip(moves, results[1:1 + n_mid]):
        parts.append(shifted(value, by, 0))
        places.append((row, count, 0, coarse_y, begin * levels))
    if joined and not last:
        places, parts = places[:1], [parts[0] + parts[1]]
    if last:
        edges, before = lax.optimization_barrier((edges, before))
        for (by, row, count), to_left, to_right in zip([(0, 0, coarse_x)] + moves, edges[:n_strip], edges[n_strip:]):
            parts += [shifted(to_left, by, -1), shifted(to_right, by, 1)]
            places += [(row, count, coarse_y - REACH, REACH, 0), (row, count, 0, REACH + 1, 0)]
    return before + parts, places, edges, results[-1]


def backward(alpha, adjoint_parts, mix, bg_sigma, static_ctrl, ens_pert, me):
    members, levels = ens_pert.shape[:2]
    copies = LANES // levels
    cut = max(members * 2 // 5 // copies, 1) * copies
    parts, places, edges = [], [], []
    for begin, end in ((0, cut), (cut, members)):
        parts, at, edges, grad_static = backward_chunk(
            alpha, adjoint_parts, mix, bg_sigma, static_ctrl, ens_pert, me, begin, end, edges, parts
        )
        places += at
    grad_alpha = pl.pallas_call(
        functools.partial(fold_kernel, places),
        out_shape=jax.ShapeDtypeStruct(alpha.shape, jnp.float32),
        in_specs=[VMEM] * (1 + len(parts)),
        out_specs=VMEM,
        compiler_params=room(12),
        cost_estimate=pl.CostEstimate(flops=1 << 20, bytes_accessed=2 << 20, transcendentals=0),
        name="fold",
    )(alpha, *parts)
    return grad_alpha, grad_static


def owned_sum(parts):
    count = len(parts)
    total = parts[0]
    for d in range(1, count):
        total = total + lax.ppermute(parts[d], "mem", [(i, (i + d) % count) for i in range(count)])
    return total


def gathered(own):
    count = lax.axis_size("mem")
    return [own] + [lax.ppermute(own, "mem", [(i, (i + d) % count) for i in range(count)]) for d in range(1, count)]


def per_device(
    alpha,
    lv_sqrt,
    ens_pert,
    bg_sigma,
    static_ctrl,
    obs_owner,
    obs_column,
    obs_level,
    obs_frac,
    innovation,
    obs_rinv,
    obs_count,
):
    levels, fine_x, fine_y = bg_sigma.shape
    tiles = lax.axis_size("tx") * lax.axis_size("ty")
    capacity = 2 * obs_owner.shape[0] // tiles
    me = lax.axis_index("mem").astype(jnp.int32).reshape(1)
    outgoing, target = pack(
        tiles, levels, fine_x * fine_y, capacity,
        obs_count, obs_owner[:, 0], obs_column, obs_level, obs_frac, innovation, obs_rinv,
    )
    partial, outgoing = ensemble(alpha, lv_sqrt, ens_pert, me, outgoing)
    increment = gathered(owned_sum(partial))
    increment[-1], outgoing = lax.optimization_barrier((increment[-1], outgoing))
    incoming = lax.all_to_all(outgoing, ("tx", "ty"), split_axis=0, concat_axis=0, tiled=True)
    departure, adjoint = stencil(increment, incoming, bg_sigma, static_ctrl, me)
    parts = gathered(owned_sum(adjoint))
    parts[-1], departure = lax.optimization_barrier((parts[-1], departure))
    returned = lax.all_to_all(departure, ("tx", "ty"), split_axis=0, concat_axis=0, tiled=True)
    departures = unpack(target, returned.reshape(-1, BLOCK))
    parts, departures = lax.optimization_barrier((parts, departures))
    grad_alpha, grad_static = backward(alpha, parts, lv_sqrt, bg_sigma, static_ctrl, ens_pert, me)
    return (grad_alpha, grad_static, departures)


def solution(mesh):
    placed = (
        P("tx", "ty", "mem"),
        P(),
        P("mem", None, "tx", "ty"),
        P(None, "tx", "ty"),
        P(None, "tx", "ty"),
        P(("tx", "ty", "mem"), None),
        P(("tx", "ty", "mem")),
        P(("tx", "ty", "mem")),
        P(None, ("tx", "ty", "mem")),
        P(("tx", "ty", "mem")),
        P(("tx", "ty", "mem")),
        P(("tx", "ty", "mem")),
    )
    return jax.shard_map(
        per_device,
        mesh=mesh,
        in_specs=placed,
        out_specs=(P("tx", "ty", "mem"), P(None, "tx", "ty"), P(("tx", "ty", "mem"))),
        check_vma=False,
    )
```

```python
import functools
import math

import jax
import jax.numpy as jnp
from jax import lax
from jax.experimental import pallas as pl
from jax.experimental.pallas import tpu as pltpu
from jax.sharding import PartitionSpec as P

RATIO = 4
NSTEP = 4
NU = 0.2
VMEM = pl.BlockSpec(memory_space=pltpu.VMEM)
SMEM = pl.BlockSpec(memory_space=pltpu.SMEM)
HBM = pl.BlockSpec(memory_space=pltpu.HBM)


def room(mebibytes):
    return pltpu.CompilerParams(vmem_limit_bytes=mebibytes << 20)

BLOCK = 256
LANES = 128
STEPS = (8, 12, 16)
WIDE = STEPS[-1]
HALF = jnp.bfloat16


def split_two(value):
    high = value.astype(HALF)
    return high, (value - high.astype(jnp.float32)).astype(HALF)


def dot_nt(a, b):
    return lax.dot_general(a, b, (((1,), (1,)), ((), ())), preferred_element_type=jnp.float32)


def dot_nn(a, b):
    return jnp.dot(a, b, preferred_element_type=jnp.float32)


def iota(shape, dim):
    return lax.broadcasted_iota(jnp.int32, shape, dim)


def pack_kernel(
    tiles, levels, plane, capacity,
    count_ref, *refs,
):
    sources, (out_ref, target_ref, carry, total, gathered, *held), sems = refs[:3], refs[3:-1], refs[-1]
    copies = [pltpu.make_async_copy(source, here, sems.at[i]) for i, (source, here) in enumerate(zip(sources, held))]
    for copy in copies:
        copy.start()
    ints_ref, floats_ref, frac_ref = held
    size = target_ref.shape[0]
    owner_ref, level_ref, column_ref = [ints_ref.at[pl.ds(i * size, size)] for i in range(3)]
    innov_ref, rinv_ref = [floats_ref.at[pl.ds(i * size, size)] for i in range(2)]
    blocks = target_ref.shape[0] * LANES // BLOCK
    keys = tiles * levels
    deep = capacity // BLOCK
    slot_rows = tiles * deep
    group = 4
    count = count_ref[0]

    def row_of(ref, j):
        pair = ref[pl.ds(2 * j, 2), :]
        return jnp.concatenate([pair[0:1], pair[1:2]], 1)

    def onehot(j):
        live = iota((1, BLOCK), 1) + j * BLOCK < count
        key = jnp.where(live, row_of(owner_ref, j) * levels + row_of(level_ref, j), -1)
        return live, iota((keys, BLOCK), 0) == key

    ones = jnp.ones((BLOCK, LANES), HALF)
    total[...] = jnp.zeros_like(total)
    for copy in copies[:1]:
        copy.wait()

    many = math.gcd(blocks, 8)

    def count_group(g, unused):
        masks = [onehot(g * many + i)[1] for i in range(many)]
        counted = jnp.concatenate([jnp.where(mask, 1.0, 0.0).astype(HALF) for mask in masks], 1)
        total[...] += dot_nn(counted, jnp.concatenate([ones] * many, 0))
        return unused

    lax.fori_loop(0, blocks // many, count_group, 0)
    high = jnp.floor(total[...] * (1.0 / LANES))
    low = total[...] - high * LANES
    row_key, col_key = iota((keys, keys), 0), iota((keys, keys), 1)
    before = jnp.where((col_key < row_key) & (col_key // levels == row_key // levels), 1.0, 0.0).astype(HALF)
    start = dot_nn(before, high.astype(HALF)) * LANES + dot_nn(before, low.astype(HALF))
    carry[...] = start + ((iota((keys, LANES), 0) // levels) * capacity).astype(jnp.float32)

    earlier = jnp.where(iota((BLOCK, BLOCK), 0) < iota((BLOCK, BLOCK), 1), 1.0, 0.0).astype(HALF)
    prefix = jnp.concatenate([earlier, ones], 1)
    gathered[...] = jnp.zeros_like(gathered)

    def rank_group(g, unused):
        now = carry[...]
        seen = [onehot(g * many + i) for i in range(many)]
        ranks = [dot_nn(jnp.where(mask, 1.0, 0.0).astype(HALF), prefix) for live, mask in seen]
        for i, ((live, mask), rank) in enumerate(zip(seen, ranks)):
            here = rank[:, :BLOCK] + jnp.concatenate([now] * (BLOCK // LANES), 1)
            now = now + rank[:, BLOCK:]
            slot = jnp.sum(jnp.where(mask, here, 0.0), 0, keepdims=True)
            target = jnp.where(live, slot.astype(jnp.int32), -1)
            target_ref[pl.ds(2 * (g * many + i), 2), :] = jnp.concatenate([target[:, :LANES], target[:, LANES:]], 0)
        carry[...] = now
        return unused

    lax.fori_loop(0, blocks // many, rank_group, 0)
    for copy in copies[1:]:
        copy.wait()

    def place(j):
        target = row_of(target_ref, j)
        rows = jnp.where(iota((slot_rows, BLOCK), 0) == (target >> 8), 1.0, 0.0).astype(HALF)
        lanes = jnp.where(iota((BLOCK, BLOCK), 0) == (target & (BLOCK - 1)), 1.0, 0.0).astype(HALF)
        column = row_of(column_ref, j)
        frac = frac_ref[:, pl.ds(pl.multiple_of(j * BLOCK, BLOCK), BLOCK)]
        terms = []
        for value in (frac[0:1], frac[1:2], frac[2:3], row_of(innov_ref, j), row_of(rinv_ref, j)):
            terms.extend(split_two(jnp.broadcast_to(value, (16, BLOCK))))
        for value in (row_of(level_ref, j), column >> 7, column & (LANES - 1)):
            terms.append(jnp.broadcast_to(value.astype(jnp.float32), (16, BLOCK)).astype(HALF))
        spread = [rows * jnp.concatenate([term] * (slot_rows // 16), 0) for term in terms]
        return jnp.concatenate(spread, 0), lanes

    def scatter_group(g, unused):
        placed = [place(g * group + i) for i in range(group)]
        left = jnp.concatenate([a for a, b in placed], 1)
        right = jnp.concatenate([b for a, b in placed], 1)
        gathered[...] += dot_nt(left, right)
        return unused

    lax.fori_loop(0, blocks // group, scatter_group, 0)

    def part(index, tile):
        begin = index * slot_rows + tile * deep
        return gathered[begin:begin + deep, :]

    for tile in range(tiles):
        for p in range(5):
            out_ref[tile, p * deep:(p + 1) * deep, :] = part(2 * p, tile) + part(2 * p + 1, tile)
        base = part(10, tile) * plane + part(11, tile) * LANES + part(12, tile)
        out_ref[tile, 5 * deep:6 * deep, :] = base


def pack(tiles, levels, plane, capacity, count, owner, column, level, frac, innov, rinv):
    slots = owner.shape[0]
    rows = slots // LANES
    deep = capacity // BLOCK
    values = [jnp.concatenate(some).reshape(-1, LANES) for some in ((owner, level, column), (innov, rinv))] + [frac]
    vmem = pl.BlockSpec(memory_space=pltpu.VMEM)
    return pl.pallas_call(
        functools.partial(pack_kernel, tiles, levels, plane, capacity),
        out_shape=(
            jax.ShapeDtypeStruct((tiles, 6 * deep, BLOCK), jnp.float32),
            jax.ShapeDtypeStruct((rows, LANES), jnp.int32),
        ),
        in_specs=[SMEM] + [HBM] * 3,
        out_specs=(vmem, vmem),
        scratch_shapes=[
            pltpu.VMEM((tiles * levels, LANES), jnp.float32),
            pltpu.VMEM((tiles * levels, LANES), jnp.float32),
            pltpu.VMEM((13 * tiles * deep, BLOCK), jnp.float32),
        ]
        + [pltpu.VMEM(value.shape, value.dtype) for value in values]
        + [pltpu.SemaphoreType.DMA((len(values),))],
        compiler_params=room(16),
        cost_estimate=pl.CostEstimate(flops=1 << 20, bytes_accessed=1 << 20, transcendentals=0),
        name="pack",
    )(count, *values)


def stencil_kernel(
    me_ref, parts_refs, sigma_ref, static_ref, incoming_ref,
    dep_ref, adj_refs,
    field, field_t, adjoint, spans, spans_ref, sem,
):
    levels, fine_x, fine_y = sigma_ref.shape
    sources, packed_rows, block = incoming_ref.shape
    deep = packed_rows // 6
    plane = fine_x * fine_y
    chunk = LANES // fine_x
    groups = len(parts_refs)
    share = levels // groups
    rows = levels * fine_x
    me = me_ref[0]
    halves = block // LANES
    column = iota((sources * deep, LANES), 1)
    found = jnp.zeros((sources * deep, LANES), jnp.int32)
    for half in range(halves):
        lanes = slice(half * LANES, (half + 1) * LANES)
        used = incoming_ref[:, 4 * deep:5 * deep, lanes].reshape(sources * deep, LANES) > 0.0
        level = jnp.floor(incoming_ref[:, 5 * deep:, lanes].reshape(sources * deep, LANES) * (1.0 / plane))
        lowest = jnp.min(jnp.where(used, level, float(levels)), 1, keepdims=True).astype(jnp.int32)
        highest = jnp.max(jnp.where(used, level, -1.0), 1, keepdims=True).astype(jnp.int32)
        found = jnp.where((column == 2 * half) & (highest >= 0), lowest, found)
        found = jnp.where((column == 2 * half + 1) & (highest >= 0), highest + 2 - lowest, found)
    spans[...] = found
    fetch = pltpu.make_async_copy(spans, spans_ref, sem)
    fetch.start()
    adjoint[...] = jnp.zeros_like(adjoint)
    dep_ref[...] = jnp.zeros_like(dep_ref)
    field[rows:, :] = jnp.zeros((field.shape[0] - rows, fine_y), jnp.float32)
    for slot, part in enumerate(parts_refs):
        start = lax.rem(me + groups - slot, groups) * share
        static = sigma_ref[pl.ds(start, share)] * static_ref[pl.ds(start, share)]
        where = pl.ds(pl.multiple_of(start * fine_x, LANES), share * fine_x)
        field[where, :] = (part[...] + static).reshape(share * fine_x, fine_y)
    for shift in range(chunk):
        field_t[shift, :, rows:] = jnp.zeros((2 * fine_y, field_t.shape[2] - rows), HALF)
        for g in range(rows // LANES):
            begin = shift * fine_x + g * LANES
            high, low = split_two(field[begin:begin + LANES, :].T)
            field_t[shift, :fine_y, g * LANES:(g + 1) * LANES] = high
            field_t[shift, fine_y:, g * LANES:(g + 1) * LANES] = low

    fetch.wait()

    def block_of(source, at, half):
        def row(p):
            return incoming_ref[source, pl.ds(p * deep + at, 1), :][:, half * LANES:(half + 1) * LANES]

        base = row(5)
        level = jnp.floor(base * (1.0 / plane))
        rest = base - level * plane
        across = jnp.floor(rest * (1.0 / fine_y))
        along = rest - across * fine_y
        frac_x, frac_y, frac_l = row(0), row(1), row(2)
        rows_x = iota((fine_x, LANES), 0).astype(jnp.float32)
        pick_x = jnp.where(rows_x == across, 1.0 - frac_x, 0.0) + jnp.where(rows_x == across + 1.0, frac_x, 0.0)
        rows_y = iota((fine_y, LANES), 0).astype(jnp.float32)
        pick_y = jnp.where(rows_y == along, 1.0 - frac_y, 0.0) + jnp.where(rows_y == along + 1.0, frac_y, 0.0)

        def weights(bottom, reach):
            offset = level - bottom.astype(jnp.float32)
            picks = []
            for g in range(reach):
                pick_l = jnp.where(offset == float(g), 1.0 - frac_l, 0.0) + jnp.where(offset == float(g - 1), frac_l, 0.0)
                picks.append(pick_x * pick_l)
            return jnp.concatenate(split_two(jnp.concatenate(picks, 0)), 1)

        def finish(picked):
            departure = jnp.sum(picked * pick_y, 0, keepdims=True) - row(3)
            turned = jnp.concatenate(split_two((pick_y * (row(4) * departure)).T), 1)
            return departure, jnp.concatenate([turned, turned], 0)

        return weights, finish

    def look(bottom, pick):
        lanes = pl.ds(pl.multiple_of((bottom // chunk) * LANES, LANES), pick.shape[0])
        seen = dot_nn(field_t[lax.rem(bottom, chunk), :, lanes], pick)
        return seen[:fine_y, :LANES] + (seen[:fine_y, LANES:] + seen[fine_y:, :LANES])

    def spread(pick, term):
        both = dot_nn(pick, term)
        return both[:, :fine_y] + both[:, fine_y:]

    def rows_at(bottom, reach):
        return pl.ds(pl.multiple_of(bottom * fine_x, fine_x), reach * fine_x)

    def together(blocks, bottoms, reach):
        parts = [block_of(*block) for block in blocks]
        picks = [weights(bottom, reach) for (weights, finish), bottom in zip(parts, bottoms)]
        seen = [look(bottom, pick) for bottom, pick in zip(bottoms, picks)]
        done = [finish(value) for (weights, finish), value in zip(parts, seen)]
        adds = [spread(pick, term) for pick, (departure, term) in zip(picks, done)]
        keep(blocks, [departure for departure, term in done])
        for bottom, add in zip(bottoms, adds):
            adjoint[rows_at(bottom, reach), :] += add

    def keep(blocks, departures):
        for i in range(0, len(blocks), halves):
            source, at, half = blocks[i]
            dep_ref[source, pl.ds(at, 1), :] = jnp.concatenate(departures[i:i + halves], 1)

    def alone(block, first, needed):
        weights, finish = block_of(*block)
        windows = (needed + WIDE - 1) // WIDE

        def forward(w, total):
            bottom = first + w * WIDE
            return total + look(bottom, weights(bottom, WIDE))

        departure, term = finish(lax.fori_loop(0, windows, forward, jnp.zeros((fine_y, LANES), jnp.float32)))

        def backward(w, unused):
            bottom = first + w * WIDE
            adjoint[rows_at(bottom, WIDE), :] += spread(weights(bottom, WIDE), term)
            return unused

        lax.fori_loop(0, windows, backward, 0)
        return departure

    step = 2 if deep % 2 == 0 else 1

    def one_step(i, unused):
        source, at = i // (deep // step), lax.rem(i, deep // step) * step
        blocks = [(source, at + r, half) for r in range(step) for half in range(halves)]
        numbers = [(source * deep + at + r, half) for r in range(step) for half in range(halves)]
        bottoms = [spans_ref[row, 2 * half] for row, half in numbers]
        needs = [spans_ref[row, 2 * half + 1] for row, half in numbers]
        most = functools.reduce(jnp.maximum, needs)

        for below, reach in zip((0,) + STEPS, STEPS):
            @pl.when((most > below) & (most <= reach))
            def _():
                together(blocks, bottoms, reach)

        @pl.when(most > WIDE)
        def _():
            keep(blocks, [alone(*each) for each in zip(blocks, bottoms, needs)])

        return unused

    lax.fori_loop(0, sources * deep // step, one_step, 0)
    for slot, adj_ref in enumerate(adj_refs):
        start = lax.rem(me + slot, groups) * share * fine_x
        adj_ref[...] = adjoint[pl.ds(pl.multiple_of(start, LANES), share * fine_x), :].reshape(share, fine_x, fine_y)


def stencil(parts, incoming, bg_sigma, static_ctrl, me):
    levels, fine_x, fine_y = bg_sigma.shape
    sources, packed_rows, block = incoming.shape
    deep, groups = packed_rows // 6, len(parts)
    rows = levels * fine_x
    padded = rows + WIDE * fine_x

    def kernel(*refs):
        parts_end = 1 + groups
        stencil_kernel(
            refs[0], refs[1:parts_end], *refs[parts_end:parts_end + 4],
            refs[parts_end + 4:parts_end + 4 + groups], *refs[parts_end + 4 + groups:]
        )

    results = pl.pallas_call(
        kernel,
        out_shape=(jax.ShapeDtypeStruct((sources, deep, block), jnp.float32),)
        + tuple(jax.ShapeDtypeStruct(part.shape, jnp.float32) for part in parts),
        in_specs=[SMEM] + [VMEM] * (groups + 3),
        out_specs=(VMEM,) * (1 + groups),
        scratch_shapes=[
            pltpu.VMEM((padded, fine_y), jnp.float32),
            pltpu.VMEM((LANES // fine_x, 2 * fine_y, padded), HALF),
            pltpu.VMEM((padded, fine_y), jnp.float32),
            pltpu.VMEM((sources * deep, LANES), jnp.int32),
            pltpu.SMEM((sources * deep, LANES), jnp.int32),
            pltpu.SemaphoreType.DMA,
        ],
        compiler_params=room(20),
        cost_estimate=pl.CostEstimate(flops=16 << 30, bytes_accessed=1 << 20, transcendentals=0),
        name="stencil",
    )(me, *parts, bg_sigma, static_ctrl, incoming)
    return results[0], results[1:]


def unpack_kernel(target_ref, table_ref, out_ref):
    slot_rows = table_ref.shape[0]
    high, low = split_two(table_ref[...])
    both = jnp.concatenate([high.astype(jnp.float32), low.astype(jnp.float32)], 0)
    turned = both.T.astype(HALF)
    group = 4

    def some_blocks(g, unused):
        for i in range(group):
            pair = target_ref[pl.ds(2 * (g * group + i), 2), :]
            target = jnp.concatenate([pair[0:1], pair[1:2]], 1)
            rows = jnp.where(iota((slot_rows, BLOCK), 0) == (target >> 8), 1.0, 0.0).astype(HALF)
            lines = dot_nn(turned, jnp.concatenate([rows, rows], 0))
            lane = iota((BLOCK, BLOCK), 0) == (target & (BLOCK - 1))
            found = jnp.sum(jnp.where(lane, lines, 0.0), 0, keepdims=True)
            out_ref[pl.ds(2 * (g * group + i), 2), :] = jnp.concatenate([found[:, :LANES], found[:, LANES:]], 0)
        return unused

    lax.fori_loop(0, target_ref.shape[0] // (2 * group), some_blocks, 0)


def unpack(target, table):
    vmem = pl.BlockSpec(memory_space=pltpu.VMEM)
    return pl.pallas_call(
        unpack_kernel,
        out_shape=jax.ShapeDtypeStruct(target.shape, jnp.float32),
        in_specs=[vmem, vmem],
        out_specs=vmem,
        compiler_params=room(8),
        cost_estimate=pl.CostEstimate(flops=2 << 30, bytes_accessed=1 << 18, transcendentals=0),
        name="unpack",
    )(target, table).reshape(-1)


REACH = NSTEP
EDGE = 8
PAD = 2 * EDGE
SCALE = NU**NSTEP


def interpolation(shape, fine_dim, coarse_dim, shift):
    fine, coarse = iota(shape, fine_dim), iota(shape, coarse_dim) - shift
    frac = (fine % RATIO).astype(jnp.float32) * (1.0 / RATIO)
    low = jnp.where(coarse == fine // RATIO, 1.0 - frac, 0.0)
    return (low + jnp.where(coarse == fine // RATIO + 1, frac, 0.0)).astype(HALF)


def interpolation_rows(fine_x, depth, copies, transposed):
    long, short = EDGE * fine_x, EDGE * depth
    shape = (short, long) if transposed else (long, copies * short)
    fine, coarse = iota(shape, 1 if transposed else 0), iota(shape, 0 if transposed else 1)
    for copy in range(1, copies):
        coarse = jnp.where(coarse >= short, coarse - short, coarse)
    place, target = fine % fine_x, coarse // EDGE
    frac = (place % RATIO).astype(jnp.float32) * (1.0 / RATIO)
    low = jnp.where(target == place // RATIO, 1.0 - frac, 0.0)
    weight = low + jnp.where(target == place // RATIO + 1, frac, 0.0)
    return jnp.where(fine // fine_x == coarse % EDGE, weight, 0.0).astype(HALF)


def mixing(mix_ref):
    levels = mix_ref.shape[0]
    tile = jnp.where(iota((LANES, levels), 0) % levels == iota((LANES, levels), 1), 1.0, 0.0).astype(HALF)
    same = iota((LANES, LANES), 0) // levels == iota((LANES, LANES), 1) // levels
    terms = []
    for term in split_two(mix_ref[...]):
        tiled = dot_nt(dot_nn(tile, term).astype(HALF), tile)
        terms.append(jnp.where(same, tiled, 0.0).astype(HALF))
    return terms


def neighbours(field):
    width = field.shape[1]
    return pltpu.roll(field, 1, 1) + pltpu.roll(field, width - 1, 1)


def ensemble_kernel(
    coarse_x, coarse_y, offsets,
    me_ref, alpha_ref, above_ref, below_ref,
    left_ref, left_above_ref, left_below_ref, right_ref, right_above_ref, right_below_ref,
    mix_ref, pert_hbm, out_refs, pert_ref, sem, ext, coarse,
):
    members, levels, fine_x, fine_y = pert_ref.shape
    channels = alpha_ref.shape[2]
    fetch = pltpu.make_async_copy(pert_hbm, pert_ref, sem)
    fetch.start()
    ext[:, :EDGE, :] = jnp.zeros((ext.shape[0], EDGE, channels), jnp.float32)
    ext[:, EDGE + coarse_y:, :] = jnp.zeros((ext.shape[0], EDGE, channels), jnp.float32)
    above, below = offsets
    groups = (
        (0, REACH, above, above_ref, left_above_ref, right_above_ref),
        (REACH, coarse_x, 0, alpha_ref, left_ref, right_ref),
        (REACH + coarse_x, REACH + 1, below, below_ref, left_below_ref, right_below_ref),
    )
    for begin, count, offset, middle, left, right in groups:
        ext[begin:begin + count, EDGE:EDGE + coarse_y, :] = middle[offset:offset + count]
        for i in range(count):
            at = offset + i
            ext[begin + i, EDGE - REACH:EDGE, :] = left[at * REACH:(at + 1) * REACH, :]
            ext[begin + i, EDGE + coarse_y:EDGE + coarse_y + REACH + 1, :] = right[
                at * (REACH + 1):(at + 1) * (REACH + 1), :
            ]
    spread_y = interpolation((coarse_y + PAD, fine_y), 1, 0, EDGE)
    spread_y = jnp.concatenate([spread_y, spread_y], 0)
    high, low = mixing(mix_ref)
    mix = jnp.concatenate([high, high, low], 1)

    def one_group(g, unused):
        lanes = pl.ds(pl.multiple_of(g * LANES, LANES), LANES)
        field = ext[:, :, lanes]
        for step in range(NSTEP):
            inner = field[1:-1]
            field = inner + field[2:] + field[:-2] + neighbours(inner)
        high, low = split_two(field * SCALE)
        both = jnp.concatenate([high.astype(jnp.float32), low.astype(jnp.float32)], 1)
        for c in range(coarse_x + 1):
            wide_high, wide_low = split_two(dot_nn(both[c].T.astype(HALF), spread_y))
            coarse[c, lanes, :] = dot_nn(mix, jnp.concatenate([wide_high, wide_low, wide_high], 0))
        return unused

    lax.fori_loop(0, channels // LANES, one_group, 0, unroll=True)
    fetch.wait()
    depth = coarse_x + 2
    spread_x = interpolation_rows(fine_x, depth, 2, False)
    share = levels // len(out_refs)
    unroll = math.gcd(members // 2, 5)

    for slot, out_ref in enumerate(out_refs):
        for sub in range(share // EDGE):
            first = pl.multiple_of(lax.rem(me_ref[0] + slot, len(out_refs)) * share + sub * EDGE, EDGE)

            def stacked(k):
                rows = pl.ds(pl.multiple_of(k * levels + first, EDGE), EDGE)
                parts = [coarse[c, rows, :] for c in range(coarse_x + 1)]
                return jnp.concatenate(parts + [jnp.zeros((EDGE, fine_y), jnp.float32)], 0)

            def perturbation(k):
                return pert_ref[k, pl.ds(first, EDGE)].reshape(EDGE * fine_x, fine_y).astype(jnp.float32)

            def pairs(p, total):
                for i in range(unroll):
                    k = 2 * (unroll * p + i)
                    high, low = split_two(jnp.concatenate([stacked(k), stacked(k + 1)], 1))
                    fine = dot_nn(spread_x, jnp.concatenate([high, low], 0))
                    total = total + (fine[:, :fine_y] * perturbation(k) + fine[:, fine_y:] * perturbation(k + 1))
                return total

            total = lax.fori_loop(
                0, members // (2 * unroll), pairs, jnp.zeros((EDGE * fine_x, fine_y), jnp.float32)
            )
            out_ref[sub * EDGE:(sub + 1) * EDGE] = total.reshape(EDGE, fine_x, fine_y)


def backward_kernel(
    coarse_x, coarse_y, joined,
    me_ref, parts_refs, mix_ref, sigma_ref, static_ref, pert_hbm,
    grad_ref, center_ref, middle_refs, left_refs, right_refs,
    adjoint, coarse, pert_ref, sems,
):
    members, levels, fine_x, fine_y = pert_ref.shape
    channels = members * levels
    unroll = members // sems.shape[0]
    copies = []
    for p in range(sems.shape[0]):
        some = pl.ds(p * unroll, unroll)
        copies.append(pltpu.make_async_copy(pert_hbm.at[some], pert_ref.at[some], sems.at[p]))
        copies[p].start()
    share = levels // len(parts_refs)
    for slot, part in enumerate(parts_refs):
        first = lax.rem(me_ref[0] + len(parts_refs) - slot, len(parts_refs)) * share
        adjoint[pl.ds(first, share)] = part[...]
    grad_ref[...] = static_ref[...] + sigma_ref[...] * adjoint[...]
    depth = coarse_x + 2
    fold_x = interpolation_rows(fine_x, depth, 1, True)

    for p, copy in enumerate(copies):
        copy.wait()

        def one_level_group(group, unused):
            some = pl.ds(group * EDGE, EDGE)
            field = adjoint[some].reshape(EDGE * fine_x, fine_y)
            for k in range(p * unroll, (p + 1) * unroll):
                scaled = pert_ref[k, some].reshape(EDGE * fine_x, fine_y).astype(jnp.float32)
                high, low = split_two(scaled * field)
                both = dot_nn(fold_x, jnp.concatenate([high, low], 1))
                rows = pl.ds(pl.multiple_of(k * levels + group * EDGE, EDGE), EDGE)
                for c in range(coarse_x + 1):
                    piece = both[c * EDGE:(c + 1) * EDGE]
                    coarse[c, rows, :] = piece[:, :fine_y] + piece[:, fine_y:]
            return unused

        lax.fori_loop(0, levels // EDGE, one_level_group, 0)

    fold_y = interpolation((coarse_y + PAD, fine_y), 1, 0, EDGE)
    fold_y = jnp.concatenate([fold_y, fold_y], 1)
    high, low = mixing(mix_ref)
    mix = jnp.concatenate([high, high, low], 0)

    def one_group(g, unused):
        lanes = pl.ds(pl.multiple_of(g * LANES, LANES), LANES)
        rows = []
        for c in range(coarse_x + 1):
            high, low = split_two(coarse[c, lanes, :])
            narrow = dot_nt(fold_y, jnp.concatenate([high, low], 1))
            high, low = split_two(narrow)
            rows.append(dot_nn(jnp.concatenate([high, low, high], 1), mix)[None])
        field = jnp.concatenate(rows, 0) * SCALE
        empty = jnp.zeros((1,) + field.shape[1:], jnp.float32)
        for step in range(NSTEP):
            own = field + neighbours(field)
            field = jnp.concatenate([field, empty, empty], 0) + jnp.concatenate([empty, own, empty], 0) + jnp.concatenate(
                [empty, empty, field], 0
            )
        inside = field[REACH:REACH + coarse_x]
        up, down = field[:REACH], field[REACH + coarse_x:]
        if joined:
            none = jnp.zeros((coarse_x - REACH - 1,) + field.shape[1:], jnp.float32)
            outside = [jnp.concatenate([down, none], 0) + jnp.concatenate([none, empty, up], 0)]
        else:
            outside = [up, down]
        center_ref[:, :, lanes] = inside[:, EDGE:EDGE + coarse_y]
        for ref, value in zip(middle_refs, outside):
            ref[:, :, lanes] = value[:, EDGE:EDGE + coarse_y]
        for left, right, value in zip(left_refs, right_refs, [inside] + outside):
            for i in range(value.shape[0]):
                left[i * REACH:(i + 1) * REACH, lanes] = value[i, EDGE - REACH:EDGE]
                right[i * (REACH + 1):(i + 1) * (REACH + 1), lanes] = value[
                    i, EDGE + coarse_y:EDGE + coarse_y + REACH + 1
                ]
        return unused

    lax.fori_loop(0, channels // LANES, one_group, 0, unroll=True)


def fold_kernel(places, alpha_ref, center_ref, *refs):
    part_refs, out_ref = refs[:-1], refs[-1]
    out_ref[...] = alpha_ref[...] + center_ref[...]
    for (row, count, column, width), ref in zip(places, part_refs):
        if width == out_ref.shape[1]:
            out_ref[row:row + count] += ref[...]
        else:
            for i in range(count):
                out_ref[row + i, column:column + width, :] += ref[i * width:(i + 1) * width, :]


def shifted(value, by_x, by_y):
    count_x, count_y = lax.axis_size("tx"), lax.axis_size("ty")
    pairs = [
        (x * count_y + y, (x + by_x) % count_x * count_y + (y + by_y) % count_y)
        for x in range(count_x)
        for y in range(count_y)
    ]
    return lax.ppermute(value, ("tx", "ty"), pairs)


def ensemble(alpha, mix, ens_pert, me, beside):
    coarse_x, coarse_y, channels = alpha.shape
    members, levels, fine_x, fine_y = ens_pert.shape
    joined = lax.axis_size("tx") == 2
    ends = alpha[:, coarse_y - REACH:]
    starts = alpha[:, :REACH + 1]

    def flat(strip):
        return strip.reshape(-1, channels)

    if joined:
        other = shifted(alpha, 1, 0)
        above = below = other
        left_above = left_below = shifted(flat(ends), 1, 1)
        right_above = right_below = shifted(flat(starts), 1, -1)
        offsets = (coarse_x - REACH, 0)
    else:
        last = slice(coarse_x - REACH, coarse_x)
        first = slice(0, REACH + 1)
        above, below = shifted(alpha[last], 1, 0), shifted(alpha[first], -1, 0)
        left_above, left_below = shifted(flat(ends[last]), 1, 1), shifted(flat(ends[first]), -1, 1)
        right_above, right_below = shifted(flat(starts[last]), 1, -1), shifted(flat(starts[first]), -1, -1)
        offsets = (0, 0)
    left, right = shifted(flat(ends), 0, 1), shifted(flat(starts), 0, -1)
    left, beside = lax.optimization_barrier((left, beside))
    groups = lax.axis_size("mem")

    def kernel(*refs):
        ensemble_kernel(coarse_x, coarse_y, offsets, *refs[:12], refs[12:12 + groups], *refs[12 + groups:])

    parts = pl.pallas_call(
        kernel,
        out_shape=tuple(jax.ShapeDtypeStruct((levels // groups, fine_x, fine_y), jnp.float32) for _ in range(groups)),
        in_specs=[SMEM] + [VMEM] * 10 + [HBM],
        out_specs=(VMEM,) * groups,
        scratch_shapes=[
            pltpu.VMEM(ens_pert.shape, ens_pert.dtype),
            pltpu.SemaphoreType.DMA,
            pltpu.VMEM((coarse_x + 2 * REACH + 1, coarse_y + PAD, channels), jnp.float32),
            pltpu.VMEM((coarse_x + 1, channels, fine_y), jnp.float32),
        ],
        compiler_params=room(50),
        cost_estimate=pl.CostEstimate(flops=8 << 30, bytes_accessed=8 << 20, transcendentals=0),
        name="ensemble",
    )(me, alpha, above, below, left, left_above, left_below, right, right_above, right_below, mix, ens_pert)
    return parts, beside


def backward(alpha, adjoint_parts, mix, bg_sigma, static_ctrl, ens_pert, me):
    coarse_x, coarse_y, channels = alpha.shape
    members, levels, fine_x, fine_y = ens_pert.shape
    joined = lax.axis_size("tx") == 2
    groups = len(adjoint_parts)
    outside = [coarse_x] if joined else [REACH, REACH + 1]
    strips = [coarse_x] + outside
    shapes = [bg_sigma.shape, alpha.shape]
    shapes += [(rows, coarse_y, channels) for rows in outside]
    shapes += [(rows * REACH, channels) for rows in strips]
    shapes += [(rows * (REACH + 1), channels) for rows in strips]
    n_in, n_mid, n_strip = 5 + groups, len(outside), len(strips)

    def kernel(*refs):
        me_ref, parts, rest = refs[0], refs[1:1 + groups], refs[1 + groups:n_in]
        outs = refs[n_in:n_in + len(shapes)]
        middle = outs[2:2 + n_mid]
        left = outs[2 + n_mid:2 + n_mid + n_strip]
        right = outs[2 + n_mid + n_strip:]
        backward_kernel(
            coarse_x, coarse_y, joined, me_ref, parts, *rest,
            outs[0], outs[1], middle, left, right, *refs[n_in + len(shapes):]
        )

    results = pl.pallas_call(
        kernel,
        out_shape=tuple(jax.ShapeDtypeStruct(shape, jnp.float32) for shape in shapes),
        in_specs=[SMEM] + [VMEM] * (groups + 3) + [HBM],
        out_specs=(VMEM,) * len(shapes),
        scratch_shapes=[
            pltpu.VMEM(bg_sigma.shape, jnp.float32),
            pltpu.VMEM((coarse_x + 1, channels, fine_y), jnp.float32),
            pltpu.VMEM(ens_pert.shape, ens_pert.dtype),
            pltpu.SemaphoreType.DMA((members // math.gcd(members, 5),)),
        ],
        compiler_params=room(50),
        cost_estimate=pl.CostEstimate(flops=8 << 30, bytes_accessed=8 << 20, transcendentals=0),
        name="backward",
    )(me, *adjoint_parts, mix, bg_sigma, static_ctrl, ens_pert)
    grad_static, center = results[:2]
    middle = results[2:2 + n_mid]
    left, right = results[2 + n_mid:2 + n_mid + n_strip], results[2 + n_mid + n_strip:]
    last, wide = coarse_y - REACH, REACH + 1
    moves = [(1, 0, coarse_x)] if joined else [(-1, coarse_x - REACH, REACH), (1, 0, REACH + 1)]
    places, parts = [], []
    for (by, row, count), value, to_left, to_right in zip(moves, middle, left[1:], right[1:]):
        parts += [shifted(value, by, 0), shifted(to_left, by, -1), shifted(to_right, by, 1)]
        places += [(row, count, 0, coarse_y), (row, count, last, REACH), (row, count, 0, wide)]
    parts += [shifted(left[0], 0, -1), shifted(right[0], 0, 1)]
    places += [(0, coarse_x, last, REACH), (0, coarse_x, 0, wide)]
    grad_alpha = pl.pallas_call(
        functools.partial(fold_kernel, places),
        out_shape=jax.ShapeDtypeStruct(alpha.shape, jnp.float32),
        in_specs=[VMEM] * (2 + len(parts)),
        out_specs=VMEM,
        compiler_params=room(8),
        cost_estimate=pl.CostEstimate(flops=1 << 20, bytes_accessed=2 << 20, transcendentals=0),
        name="fold",
    )(alpha, center, *parts)
    return grad_alpha, grad_static


def owned_sum(parts):
    count = len(parts)
    total = parts[0]
    for d in range(1, count):
        total = total + lax.ppermute(parts[d], "mem", [(i, (i + d) % count) for i in range(count)])
    return total


def gathered(own):
    count = lax.axis_size("mem")
    return [own] + [lax.ppermute(own, "mem", [(i, (i + d) % count) for i in range(count)]) for d in range(1, count)]


def per_device(
    alpha,
    lv_sqrt,
    ens_pert,
    bg_sigma,
    static_ctrl,
    obs_owner,
    obs_column,
    obs_level,
    obs_frac,
    innovation,
    obs_rinv,
    obs_count,
):
    levels, fine_x, fine_y = bg_sigma.shape
    tiles = lax.axis_size("tx") * lax.axis_size("ty")
    capacity = 2 * obs_owner.shape[0] // tiles
    me = lax.axis_index("mem").astype(jnp.int32).reshape(1)
    outgoing, target = pack(
        tiles, levels, fine_x * fine_y, capacity,
        obs_count, obs_owner[:, 0], obs_column, obs_level, obs_frac, innovation, obs_rinv,
    )
    partial, outgoing = ensemble(alpha, lv_sqrt, ens_pert, me, outgoing)
    incoming = lax.all_to_all(outgoing, ("tx", "ty"), split_axis=0, concat_axis=0, tiled=True)
    partial, incoming = lax.optimization_barrier((partial, incoming))
    increment = owned_sum(partial)
    departure, adjoint = stencil(gathered(increment), incoming, bg_sigma, static_ctrl, me)
    total, departure = lax.optimization_barrier((owned_sum(adjoint), departure))
    returned = lax.all_to_all(departure, ("tx", "ty"), split_axis=0, concat_axis=0, tiled=True)
    departures = unpack(target, returned.reshape(-1, BLOCK))
    parts, departures = lax.optimization_barrier((gathered(total), departures))
    grad_alpha, grad_static = backward(alpha, parts, lv_sqrt, bg_sigma, static_ctrl, ens_pert, me)
    return (grad_alpha, grad_static, departures)


def solution(mesh):
    placed = (
        P("tx", "ty", "mem"),
        P(),
        P("mem", None, "tx", "ty"),
        P(None, "tx", "ty"),
        P(None, "tx", "ty"),
        P(("tx", "ty", "mem"), None),
        P(("tx", "ty", "mem")),
        P(("tx", "ty", "mem")),
        P(None, ("tx", "ty", "mem")),
        P(("tx", "ty", "mem")),
        P(("tx", "ty", "mem")),
        P(("tx", "ty", "mem")),
    )
    return jax.shard_map(
        per_device,
        mesh=mesh,
        in_specs=placed,
        out_specs=(P("tx", "ty", "mem"), P(None, "tx", "ty"), P(("tx", "ty", "mem"))),
        check_vma=False,
    )
```

```python
import functools
import math

import jax
import jax.numpy as jnp
from jax import lax
from jax.experimental import pallas as pl
from jax.experimental.pallas import tpu as pltpu
from jax.sharding import PartitionSpec as P

RATIO = 4
NSTEP = 4
NU = 0.2
VMEM = pl.BlockSpec(memory_space=pltpu.VMEM)
SMEM = pl.BlockSpec(memory_space=pltpu.SMEM)
HBM = pl.BlockSpec(memory_space=pltpu.HBM)


def room(mebibytes):
    return pltpu.CompilerParams(vmem_limit_bytes=mebibytes << 20)

BLOCK = 256
LANES = 128
STEPS = (8, 12, 16)
WIDE = STEPS[-1]
HALF = jnp.bfloat16


def split_two(value):
    high = value.astype(HALF)
    return high, (value - high.astype(jnp.float32)).astype(HALF)


def dot_nt(a, b):
    return lax.dot_general(a, b, (((1,), (1,)), ((), ())), preferred_element_type=jnp.float32)


def dot_nn(a, b):
    return jnp.dot(a, b, preferred_element_type=jnp.float32)


def iota(shape, dim):
    return lax.broadcasted_iota(jnp.int32, shape, dim)


def pack_kernel(
    tiles, levels, plane, capacity,
    count_ref, *refs,
):
    sources, (out_ref, target_ref, carry, total, gathered, left_a, right_a, left_b, right_b, *held), sems = refs[:3], refs[3:-1], refs[-1]
    copies = [pltpu.make_async_copy(source, here, sems.at[i]) for i, (source, here) in enumerate(zip(sources, held))]
    for copy in copies:
        copy.start()
    ints_ref, floats_ref, frac_ref = held
    size = target_ref.shape[0]
    owner_ref, level_ref, column_ref = [ints_ref.at[pl.ds(i * size, size)] for i in range(3)]
    innov_ref, rinv_ref = [floats_ref.at[pl.ds(i * size, size)] for i in range(2)]
    blocks = target_ref.shape[0] * LANES // BLOCK
    keys = tiles * levels
    deep = capacity // BLOCK
    slot_rows = tiles * deep
    group = 4
    count = count_ref[0]

    def row_of(ref, j):
        pair = ref[pl.ds(2 * j, 2), :]
        return jnp.concatenate([pair[0:1], pair[1:2]], 1)

    def onehot(j):
        live = iota((1, BLOCK), 1) + j * BLOCK < count
        key = jnp.where(live, row_of(owner_ref, j) * levels + row_of(level_ref, j), -1)
        return live, iota((keys, BLOCK), 0) == key

    ones = jnp.ones((BLOCK, LANES), HALF)
    total[...] = jnp.zeros_like(total)
    for copy in copies[:1]:
        copy.wait()

    many = math.gcd(blocks, 8)

    def count_group(g, unused):
        masks = [onehot(g * many + i)[1] for i in range(many)]
        counted = jnp.concatenate([jnp.where(mask, 1.0, 0.0).astype(HALF) for mask in masks], 1)
        total[...] += dot_nn(counted, jnp.concatenate([ones] * many, 0))
        return unused

    lax.fori_loop(0, blocks // many, count_group, 0)
    high = jnp.floor(total[...] * (1.0 / LANES))
    low = total[...] - high * LANES
    row_key, col_key = iota((keys, keys), 0), iota((keys, keys), 1)
    before = jnp.where((col_key < row_key) & (col_key // levels == row_key // levels), 1.0, 0.0).astype(HALF)
    start = dot_nn(before, high.astype(HALF)) * LANES + dot_nn(before, low.astype(HALF))
    carry[...] = start + ((iota((keys, LANES), 0) // levels) * capacity).astype(jnp.float32)

    earlier = jnp.where(iota((BLOCK, BLOCK), 0) < iota((BLOCK, BLOCK), 1), 1.0, 0.0).astype(HALF)
    prefix = jnp.concatenate([earlier, ones], 1)
    gathered[...] = jnp.zeros_like(gathered)

    def rank_group(g, unused):
        now = carry[...]
        seen = [onehot(g * many + i) for i in range(many)]
        ranks = [dot_nn(jnp.where(mask, 1.0, 0.0).astype(HALF), prefix) for live, mask in seen]
        for i, ((live, mask), rank) in enumerate(zip(seen, ranks)):
            here = rank[:, :BLOCK] + jnp.concatenate([now] * (BLOCK // LANES), 1)
            now = now + rank[:, BLOCK:]
            slot = jnp.sum(jnp.where(mask, here, 0.0), 0, keepdims=True)
            target = jnp.where(live, slot.astype(jnp.int32), -1)
            target_ref[pl.ds(2 * (g * many + i), 2), :] = jnp.concatenate([target[:, :LANES], target[:, LANES:]], 0)
        carry[...] = now
        return unused

    lax.fori_loop(0, blocks // many, rank_group, 0)
    for copy in copies[1:]:
        copy.wait()

    def place(j):
        target = row_of(target_ref, j)
        rows = jnp.where(iota((slot_rows, BLOCK), 0) == (target >> 8), 1.0, 0.0).astype(HALF)
        lanes = jnp.where(iota((BLOCK, BLOCK), 0) == (target & (BLOCK - 1)), 1.0, 0.0).astype(HALF)
        column = row_of(column_ref, j)
        frac = frac_ref[:, pl.ds(pl.multiple_of(j * BLOCK, BLOCK), BLOCK)]
        terms = []
        for value in (frac[0:1], frac[1:2], frac[2:3], row_of(innov_ref, j), row_of(rinv_ref, j)):
            terms.extend(split_two(jnp.broadcast_to(value, (16, BLOCK))))
        for value in (row_of(level_ref, j), column >> 7, column & (LANES - 1)):
            terms.append(jnp.broadcast_to(value.astype(jnp.float32), (16, BLOCK)).astype(HALF))
        spread = [rows * jnp.concatenate([term] * (slot_rows // 16), 0) for term in terms]
        return jnp.concatenate(spread, 0), lanes

    def build(g, left, right):
        for i in range(group):
            lanes = slice(i * BLOCK, (i + 1) * BLOCK)
            left[:, lanes], right[:, lanes] = place(g * group + i)

    def multiply(left, right):
        gathered[...] += dot_nt(left[...], right[...])

    def scatter_pair(g, unused):
        build(2 * g + 1, left_b, right_b)
        multiply(left_a, right_a)
        build(jnp.minimum(2 * g + 2, blocks // group - 1), left_a, right_a)
        multiply(left_b, right_b)
        return unused

    build(0, left_a, right_a)
    lax.fori_loop(0, blocks // (2 * group), scatter_pair, 0)

    def part(index, tile):
        begin = index * slot_rows + tile * deep
        return gathered[begin:begin + deep, :]

    for tile in range(tiles):
        for p in range(5):
            out_ref[tile, p * deep:(p + 1) * deep, :] = part(2 * p, tile) + part(2 * p + 1, tile)
        base = part(10, tile) * plane + part(11, tile) * LANES + part(12, tile)
        out_ref[tile, 5 * deep:6 * deep, :] = base


def pack(tiles, levels, plane, capacity, count, owner, column, level, frac, innov, rinv):
    slots = owner.shape[0]
    rows = slots // LANES
    deep = capacity // BLOCK
    values = [jnp.concatenate(some).reshape(-1, LANES) for some in ((owner, level, column), (innov, rinv))] + [frac]
    vmem = pl.BlockSpec(memory_space=pltpu.VMEM)
    return pl.pallas_call(
        functools.partial(pack_kernel, tiles, levels, plane, capacity),
        out_shape=(
            jax.ShapeDtypeStruct((tiles, 6 * deep, BLOCK), jnp.float32),
            jax.ShapeDtypeStruct((rows, LANES), jnp.int32),
        ),
        in_specs=[SMEM] + [HBM] * 3,
        out_specs=(vmem, vmem),
        scratch_shapes=[
            pltpu.VMEM((tiles * levels, LANES), jnp.float32),
            pltpu.VMEM((tiles * levels, LANES), jnp.float32),
            pltpu.VMEM((13 * tiles * deep, BLOCK), jnp.float32),
        ]
        + [pltpu.VMEM((count_rows, 4 * BLOCK), HALF) for count_rows in (13 * tiles * deep, BLOCK) * 2]
        + [pltpu.VMEM(value.shape, value.dtype) for value in values]
        + [pltpu.SemaphoreType.DMA((len(values),))],
        compiler_params=room(16),
        cost_estimate=pl.CostEstimate(flops=1 << 20, bytes_accessed=1 << 20, transcendentals=0),
        name="pack",
    )(count, *values)


def stencil_kernel(
    me_ref, parts_refs, sigma_ref, static_ref, incoming_ref,
    dep_ref, adj_refs,
    field, field_t, adjoint, spans, spans_ref, sem,
):
    levels, fine_x, fine_y = sigma_ref.shape
    sources, packed_rows, block = incoming_ref.shape
    deep = packed_rows // 6
    plane = fine_x * fine_y
    chunk = LANES // fine_x
    groups = len(parts_refs)
    share = levels // groups
    rows = levels * fine_x
    me = me_ref[0]
    halves = block // LANES
    column = iota((sources * deep, LANES), 1)
    found = jnp.zeros((sources * deep, LANES), jnp.int32)
    for half in range(halves):
        lanes = slice(half * LANES, (half + 1) * LANES)
        used = incoming_ref[:, 4 * deep:5 * deep, lanes].reshape(sources * deep, LANES) > 0.0
        level = jnp.floor(incoming_ref[:, 5 * deep:, lanes].reshape(sources * deep, LANES) * (1.0 / plane))
        lowest = jnp.min(jnp.where(used, level, float(levels)), 1, keepdims=True).astype(jnp.int32)
        highest = jnp.max(jnp.where(used, level, -1.0), 1, keepdims=True).astype(jnp.int32)
        found = jnp.where((column == 2 * half) & (highest >= 0), lowest, found)
        found = jnp.where((column == 2 * half + 1) & (highest >= 0), highest + 2 - lowest, found)
    spans[...] = found
    fetch = pltpu.make_async_copy(spans, spans_ref, sem)
    fetch.start()
    adjoint[...] = jnp.zeros_like(adjoint)
    dep_ref[...] = jnp.zeros_like(dep_ref)
    field[rows:, :] = jnp.zeros((field.shape[0] - rows, fine_y), jnp.float32)
    for slot, part in enumerate(parts_refs):
        start = lax.rem(me + groups - slot, groups) * share
        static = sigma_ref[pl.ds(start, share)] * static_ref[pl.ds(start, share)]
        where = pl.ds(pl.multiple_of(start * fine_x, LANES), share * fine_x)
        field[where, :] = (part[...] + static).reshape(share * fine_x, fine_y)
    for shift in range(chunk):
        field_t[shift, :, rows:] = jnp.zeros((2 * fine_y, field_t.shape[2] - rows), HALF)
        for g in range(rows // LANES):
            begin = shift * fine_x + g * LANES
            high, low = split_two(field[begin:begin + LANES, :].T)
            field_t[shift, :fine_y, g * LANES:(g + 1) * LANES] = high
            field_t[shift, fine_y:, g * LANES:(g + 1) * LANES] = low

    fetch.wait()

    def block_of(source, at, half):
        def row(p):
            return incoming_ref[source, pl.ds(p * deep + at, 1), :][:, half * LANES:(half + 1) * LANES]

        base = row(5)
        level = jnp.floor(base * (1.0 / plane))
        rest = base - level * plane
        across = jnp.floor(rest * (1.0 / fine_y))
        along = rest - across * fine_y
        frac_x, frac_y, frac_l = row(0), row(1), row(2)
        rows_x = iota((fine_x, LANES), 0).astype(jnp.float32)
        pick_x = jnp.where(rows_x == across, 1.0 - frac_x, 0.0) + jnp.where(rows_x == across + 1.0, frac_x, 0.0)
        rows_y = iota((fine_y, LANES), 0).astype(jnp.float32)
        pick_y = jnp.where(rows_y == along, 1.0 - frac_y, 0.0) + jnp.where(rows_y == along + 1.0, frac_y, 0.0)

        def weights(bottom, reach):
            offset = level - bottom.astype(jnp.float32)
            rows_l = iota((reach, LANES), 0).astype(jnp.float32)
            pick_l = jnp.where(rows_l == offset, 1.0 - frac_l, 0.0) + jnp.where(rows_l == offset + 1.0, frac_l, 0.0)
            picks = [pick_x * pick_l[g:g + 1] for g in range(reach)]
            return jnp.concatenate(split_two(jnp.concatenate(picks, 0)), 1)

        def finish(picked):
            departure = jnp.sum(picked * pick_y, 0, keepdims=True) - row(3)
            turned = jnp.concatenate(split_two((pick_y * (row(4) * departure)).T), 1)
            return departure, jnp.concatenate([turned, turned], 0)

        return weights, finish

    def look(bottom, pick):
        lanes = pl.ds(pl.multiple_of((bottom // chunk) * LANES, LANES), pick.shape[0])
        seen = dot_nn(field_t[lax.rem(bottom, chunk), :, lanes], pick)
        return seen[:fine_y, :LANES] + (seen[:fine_y, LANES:] + seen[fine_y:, :LANES])

    def spread(pick, term):
        both = dot_nn(pick, term)
        return both[:, :fine_y] + both[:, fine_y:]

    def rows_at(bottom, reach):
        return pl.ds(pl.multiple_of(bottom * fine_x, fine_x), reach * fine_x)

    def together(blocks, bottoms, reach):
        parts = [block_of(*block) for block in blocks]
        picks = [weights(bottom, reach) for (weights, finish), bottom in zip(parts, bottoms)]
        seen = [look(bottom, pick) for bottom, pick in zip(bottoms, picks)]
        done = [finish(value) for (weights, finish), value in zip(parts, seen)]
        adds = [spread(pick, term) for pick, (departure, term) in zip(picks, done)]
        keep(blocks, [departure for departure, term in done])
        for bottom, add in zip(bottoms, adds):
            adjoint[rows_at(bottom, reach), :] += add

    def keep(blocks, departures):
        for i in range(0, len(blocks), halves):
            source, at, half = blocks[i]
            dep_ref[source, pl.ds(at, 1), :] = jnp.concatenate(departures[i:i + halves], 1)

    def alone(block, first, needed):
        weights, finish = block_of(*block)
        windows = (needed + WIDE - 1) // WIDE

        def forward(w, total):
            bottom = first + w * WIDE
            return total + look(bottom, weights(bottom, WIDE))

        departure, term = finish(lax.fori_loop(0, windows, forward, jnp.zeros((fine_y, LANES), jnp.float32)))

        def backward(w, unused):
            bottom = first + w * WIDE
            adjoint[rows_at(bottom, WIDE), :] += spread(weights(bottom, WIDE), term)
            return unused

        lax.fori_loop(0, windows, backward, 0)
        return departure

    step = 2 if deep % 2 == 0 else 1

    def one_step(i, unused):
        source, at = i // (deep // step), lax.rem(i, deep // step) * step
        blocks = [(source, at + r, half) for r in range(step) for half in range(halves)]
        numbers = [(source * deep + at + r, half) for r in range(step) for half in range(halves)]
        bottoms = [spans_ref[row, 2 * half] for row, half in numbers]
        needs = [spans_ref[row, 2 * half + 1] for row, half in numbers]
        most = functools.reduce(jnp.maximum, needs)

        for below, reach in zip((0,) + STEPS, STEPS):
            @pl.when((most > below) & (most <= reach))
            def _():
                together(blocks, bottoms, reach)

        @pl.when(most > WIDE)
        def _():
            keep(blocks, [alone(*each) for each in zip(blocks, bottoms, needs)])

        return unused

    lax.fori_loop(0, sources * deep // step, one_step, 0)
    for slot, adj_ref in enumerate(adj_refs):
        start = lax.rem(me + slot, groups) * share * fine_x
        adj_ref[...] = adjoint[pl.ds(pl.multiple_of(start, LANES), share * fine_x), :].reshape(share, fine_x, fine_y)


def stencil(parts, incoming, bg_sigma, static_ctrl, me):
    levels, fine_x, fine_y = bg_sigma.shape
    sources, packed_rows, block = incoming.shape
    deep, groups = packed_rows // 6, len(parts)
    rows = levels * fine_x
    padded = rows + WIDE * fine_x

    def kernel(*refs):
        parts_end = 1 + groups
        stencil_kernel(
            refs[0], refs[1:parts_end], *refs[parts_end:parts_end + 4],
            refs[parts_end + 4:parts_end + 4 + groups], *refs[parts_end + 4 + groups:]
        )

    results = pl.pallas_call(
        kernel,
        out_shape=(jax.ShapeDtypeStruct((sources, deep, block), jnp.float32),)
        + tuple(jax.ShapeDtypeStruct(part.shape, jnp.float32) for part in parts),
        in_specs=[SMEM] + [VMEM] * (groups + 3),
        out_specs=(VMEM,) * (1 + groups),
        scratch_shapes=[
            pltpu.VMEM((padded, fine_y), jnp.float32),
            pltpu.VMEM((LANES // fine_x, 2 * fine_y, padded), HALF),
            pltpu.VMEM((padded, fine_y), jnp.float32),
            pltpu.VMEM((sources * deep, LANES), jnp.int32),
            pltpu.SMEM((sources * deep, LANES), jnp.int32),
            pltpu.SemaphoreType.DMA,
        ],
        compiler_params=room(20),
        cost_estimate=pl.CostEstimate(flops=16 << 30, bytes_accessed=1 << 20, transcendentals=0),
        name="stencil",
    )(me, *parts, bg_sigma, static_ctrl, incoming)
    return results[0], results[1:]


def unpack_kernel(target_ref, table_ref, out_ref):
    slot_rows = table_ref.shape[0]
    high, low = split_two(table_ref[...])
    both = jnp.concatenate([high.astype(jnp.float32), low.astype(jnp.float32)], 0)
    turned = both.T.astype(HALF)
    group = 4

    def some_blocks(g, unused):
        for i in range(group):
            pair = target_ref[pl.ds(2 * (g * group + i), 2), :]
            target = jnp.concatenate([pair[0:1], pair[1:2]], 1)
            rows = jnp.where(iota((slot_rows, BLOCK), 0) == (target >> 8), 1.0, 0.0).astype(HALF)
            lines = dot_nn(turned, jnp.concatenate([rows, rows], 0))
            lane = iota((BLOCK, BLOCK), 0) == (target & (BLOCK - 1))
            found = jnp.sum(jnp.where(lane, lines, 0.0), 0, keepdims=True)
            out_ref[pl.ds(2 * (g * group + i), 2), :] = jnp.concatenate([found[:, :LANES], found[:, LANES:]], 0)
        return unused

    lax.fori_loop(0, target_ref.shape[0] // (2 * group), some_blocks, 0)


def unpack(target, table):
    vmem = pl.BlockSpec(memory_space=pltpu.VMEM)
    return pl.pallas_call(
        unpack_kernel,
        out_shape=jax.ShapeDtypeStruct(target.shape, jnp.float32),
        in_specs=[vmem, vmem],
        out_specs=vmem,
        compiler_params=room(8),
        cost_estimate=pl.CostEstimate(flops=2 << 30, bytes_accessed=1 << 18, transcendentals=0),
        name="unpack",
    )(target, table).reshape(-1)


REACH = NSTEP
EDGE = 8
PAD = 2 * EDGE
SCALE = NU**NSTEP


def interpolation(shape, fine_dim, coarse_dim, shift):
    fine, coarse = iota(shape, fine_dim), iota(shape, coarse_dim) - shift
    frac = (fine % RATIO).astype(jnp.float32) * (1.0 / RATIO)
    low = jnp.where(coarse == fine // RATIO, 1.0 - frac, 0.0)
    return (low + jnp.where(coarse == fine // RATIO + 1, frac, 0.0)).astype(HALF)


def interpolation_rows(fine_x, depth, copies, transposed):
    long, short = EDGE * fine_x, EDGE * depth
    shape = (short, long) if transposed else (long, copies * short)
    fine, coarse = iota(shape, 1 if transposed else 0), iota(shape, 0 if transposed else 1)
    for copy in range(1, copies):
        coarse = jnp.where(coarse >= short, coarse - short, coarse)
    place, target = fine % fine_x, coarse // EDGE
    frac = (place % RATIO).astype(jnp.float32) * (1.0 / RATIO)
    low = jnp.where(target == place // RATIO, 1.0 - frac, 0.0)
    weight = low + jnp.where(target == place // RATIO + 1, frac, 0.0)
    return jnp.where(fine // fine_x == coarse % EDGE, weight, 0.0).astype(HALF)


def mixing(mix_ref):
    levels = mix_ref.shape[0]
    tile = jnp.where(iota((LANES, levels), 0) % levels == iota((LANES, levels), 1), 1.0, 0.0).astype(HALF)
    same = iota((LANES, LANES), 0) // levels == iota((LANES, LANES), 1) // levels
    terms = []
    for term in split_two(mix_ref[...]):
        tiled = dot_nt(dot_nn(tile, term).astype(HALF), tile)
        terms.append(jnp.where(same, tiled, 0.0).astype(HALF))
    return terms


def corner_counts(coarse_x, joined):
    above = [[j, j + 1] for j in range(REACH)]
    below = [[REACH - i, REACH + 1 - i] for i in range(REACH + 1)]
    if not joined:
        return [above, below]
    gap = [[0, 0]] * (coarse_x - REACH)
    high, low = gap + above, below + gap[1:]
    return [[[max(a, b) for a, b in zip(*pair)] for pair in zip(high, low)]]


def neighbours(field):
    width = field.shape[1]
    return pltpu.roll(field, 1, 1) + pltpu.roll(field, width - 1, 1)


def ensemble_kernel(
    coarse_x, coarse_y, offsets,
    me_ref, alpha_ref, above_ref, below_ref,
    left_ref, left_above_ref, left_below_ref, right_ref, right_above_ref, right_below_ref,
    mix_ref, pert_hbm, out_refs, pert_ref, sem, ext, coarse,
):
    members, levels, fine_x, fine_y = pert_ref.shape
    channels = alpha_ref.shape[2]
    fetch = pltpu.make_async_copy(pert_hbm, pert_ref, sem)
    fetch.start()
    ext[:, :EDGE, :] = jnp.zeros((ext.shape[0], EDGE, channels), jnp.float32)
    ext[:, EDGE + coarse_y:, :] = jnp.zeros((ext.shape[0], EDGE, channels), jnp.float32)
    above, below = offsets
    groups = (
        (0, REACH, above, above_ref, left_above_ref, right_above_ref),
        (REACH, coarse_x, 0, alpha_ref, left_ref, right_ref),
        (REACH + coarse_x, REACH + 1, below, below_ref, left_below_ref, right_below_ref),
    )
    for begin, count, offset, middle, left, right in groups:
        ext[begin:begin + count, EDGE:EDGE + coarse_y, :] = middle[offset:offset + count]
        for i in range(count):
            at = offset + i
            ext[begin + i, EDGE - REACH:EDGE, :] = left[at * REACH:(at + 1) * REACH, :]
            ext[begin + i, EDGE + coarse_y:EDGE + coarse_y + REACH + 1, :] = right[
                at * (REACH + 1):(at + 1) * (REACH + 1), :
            ]
    spread_y = interpolation((coarse_y + PAD, fine_y), 1, 0, EDGE)
    spread_y = jnp.concatenate([spread_y, spread_y], 0)
    high, low = mixing(mix_ref)
    mix = jnp.concatenate([high, high, low], 1)

    def one_group(g, unused):
        lanes = pl.ds(pl.multiple_of(g * LANES, LANES), LANES)
        field = ext[:, :, lanes]
        for step in range(NSTEP):
            inner = field[1:-1]
            field = inner + field[2:] + field[:-2] + neighbours(inner)
        high, low = split_two(field * SCALE)
        both = jnp.concatenate([high.astype(jnp.float32), low.astype(jnp.float32)], 1)
        for c in range(coarse_x + 1):
            wide_high, wide_low = split_two(dot_nn(both[c].T.astype(HALF), spread_y))
            coarse[c, lanes, :] = dot_nn(mix, jnp.concatenate([wide_high, wide_low, wide_high], 0))
        return unused

    lax.fori_loop(0, channels // LANES, one_group, 0, unroll=True)
    fetch.wait()
    depth = coarse_x + 2
    spread_x = interpolation_rows(fine_x, depth, 2, False)
    share = levels // len(out_refs)
    unroll = math.gcd(members // 2, 5)

    for slot, out_ref in enumerate(out_refs):
        for sub in range(share // EDGE):
            first = pl.multiple_of(lax.rem(me_ref[0] + slot, len(out_refs)) * share + sub * EDGE, EDGE)

            def stacked(k):
                rows = pl.ds(pl.multiple_of(k * levels + first, EDGE), EDGE)
                parts = [coarse[c, rows, :] for c in range(coarse_x + 1)]
                return jnp.concatenate(parts + [jnp.zeros((EDGE, fine_y), jnp.float32)], 0)

            def perturbation(k):
                return pert_ref[k, pl.ds(first, EDGE)].reshape(EDGE * fine_x, fine_y).astype(jnp.float32)

            def pairs(p, total):
                for i in range(unroll):
                    k = 2 * (unroll * p + i)
                    high, low = split_two(jnp.concatenate([stacked(k), stacked(k + 1)], 1))
                    fine = dot_nn(spread_x, jnp.concatenate([high, low], 0))
                    total = total + (fine[:, :fine_y] * perturbation(k) + fine[:, fine_y:] * perturbation(k + 1))
                return total

            total = lax.fori_loop(
                0, members // (2 * unroll), pairs, jnp.zeros((EDGE * fine_x, fine_y), jnp.float32)
            )
            out_ref[sub * EDGE:(sub + 1) * EDGE] = total.reshape(EDGE, fine_x, fine_y)


def backward_kernel(
    coarse_x, coarse_y, joined, strips,
    me_ref, parts_refs, mix_ref, sigma_ref, static_ref, pert_hbm,
    grad_ref, center_ref, middle_refs, left_refs, right_refs,
    adjoint, coarse, pert_ref, sems,
):
    members, levels, fine_x, fine_y = pert_ref.shape
    channels = members * levels
    unroll = members // sems.shape[0]
    copies = []
    for p in range(sems.shape[0]):
        some = pl.ds(p * unroll, unroll)
        copies.append(pltpu.make_async_copy(pert_hbm.at[some], pert_ref.at[some], sems.at[p]))
        copies[p].start()
    share = levels // len(parts_refs)
    for slot, part in enumerate(parts_refs):
        first = lax.rem(me_ref[0] + len(parts_refs) - slot, len(parts_refs)) * share
        adjoint[pl.ds(first, share)] = part[...]
    grad_ref[...] = static_ref[...] + sigma_ref[...] * adjoint[...]
    depth = coarse_x + 2
    fold_x = interpolation_rows(fine_x, depth, 1, True)

    for p, copy in enumerate(copies):
        copy.wait()

        def one_level_group(group, unused):
            some = pl.ds(group * EDGE, EDGE)
            field = adjoint[some].reshape(EDGE * fine_x, fine_y)
            for k in range(p * unroll, (p + 1) * unroll):
                scaled = pert_ref[k, some].reshape(EDGE * fine_x, fine_y).astype(jnp.float32)
                high, low = split_two(scaled * field)
                both = dot_nn(fold_x, jnp.concatenate([high, low], 1))
                rows = pl.ds(pl.multiple_of(k * levels + group * EDGE, EDGE), EDGE)
                for c in range(coarse_x + 1):
                    piece = both[c * EDGE:(c + 1) * EDGE]
                    coarse[c, rows, :] = piece[:, :fine_y] + piece[:, fine_y:]
            return unused

        lax.fori_loop(0, levels // EDGE, one_level_group, 0)

    fold_y = interpolation((coarse_y + PAD, fine_y), 1, 0, EDGE)
    fold_y = jnp.concatenate([fold_y, fold_y], 1)
    high, low = mixing(mix_ref)
    mix = jnp.concatenate([high, high, low], 0)

    def one_group(g, unused):
        lanes = pl.ds(pl.multiple_of(g * LANES, LANES), LANES)
        rows = []
        for c in range(coarse_x + 1):
            high, low = split_two(coarse[c, lanes, :])
            narrow = dot_nt(fold_y, jnp.concatenate([high, low], 1))
            high, low = split_two(narrow)
            rows.append(dot_nn(jnp.concatenate([high, low, high], 1), mix)[None])
        field = jnp.concatenate(rows, 0) * SCALE
        empty = jnp.zeros((1,) + field.shape[1:], jnp.float32)
        for step in range(NSTEP):
            own = field + neighbours(field)
            field = jnp.concatenate([field, empty, empty], 0) + jnp.concatenate([empty, own, empty], 0) + jnp.concatenate(
                [empty, empty, field], 0
            )
        inside = field[REACH:REACH + coarse_x]
        up, down = field[:REACH], field[REACH + coarse_x:]
        if joined:
            none = jnp.zeros((coarse_x - REACH - 1,) + field.shape[1:], jnp.float32)
            outside = [jnp.concatenate([down, none], 0) + jnp.concatenate([none, empty, up], 0)]
        else:
            outside = [up, down]
        center_ref[:, :, lanes] = inside[:, EDGE:EDGE + coarse_y]
        for ref, value in zip(middle_refs, outside):
            ref[:, :, lanes] = value[:, EDGE:EDGE + coarse_y]
        for left, right, value, counts in zip(left_refs, right_refs, [inside] + outside, strips):
            at_left, at_right = 0, 0
            for i, (to_left, to_right) in enumerate(counts):
                if to_left:
                    left[at_left:at_left + to_left, lanes] = value[i, EDGE - to_left:EDGE]
                if to_right:
                    right[at_right:at_right + to_right, lanes] = value[i, EDGE + coarse_y:EDGE + coarse_y + to_right]
                at_left, at_right = at_left + to_left, at_right + to_right
        return unused

    lax.fori_loop(0, channels // LANES, one_group, 0, unroll=True)


def fold_kernel(places, alpha_ref, center_ref, *refs):
    part_refs, out_ref = refs[:-1], refs[-1]
    coarse_y = out_ref.shape[1]
    out_ref[...] = alpha_ref[...] + center_ref[...]
    for (row, counts, at_end), ref in zip(places, part_refs):
        if at_end is None:
            out_ref[row:row + counts] += ref[...]
            continue
        at = 0
        for i, count in enumerate(counts):
            if count:
                begin = coarse_y - count if at_end else 0
                out_ref[row + i, begin:begin + count, :] += ref[at:at + count, :]
            at += count


def shifted(value, by_x, by_y):
    count_x, count_y = lax.axis_size("tx"), lax.axis_size("ty")
    pairs = [
        (x * count_y + y, (x + by_x) % count_x * count_y + (y + by_y) % count_y)
        for x in range(count_x)
        for y in range(count_y)
    ]
    return lax.ppermute(value, ("tx", "ty"), pairs)


def ensemble(alpha, mix, ens_pert, me, beside):
    coarse_x, coarse_y, channels = alpha.shape
    members, levels, fine_x, fine_y = ens_pert.shape
    joined = lax.axis_size("tx") == 2
    ends = alpha[:, coarse_y - REACH:]
    starts = alpha[:, :REACH + 1]

    def flat(strip):
        return strip.reshape(-1, channels)

    if joined:
        other = shifted(alpha, 1, 0)
        above = below = other
        left_above = left_below = shifted(flat(ends), 1, 1)
        right_above = right_below = shifted(flat(starts), 1, -1)
        offsets = (coarse_x - REACH, 0)
    else:
        last = slice(coarse_x - REACH, coarse_x)
        first = slice(0, REACH + 1)
        above, below = shifted(alpha[last], 1, 0), shifted(alpha[first], -1, 0)
        left_above, left_below = shifted(flat(ends[last]), 1, 1), shifted(flat(ends[first]), -1, 1)
        right_above, right_below = shifted(flat(starts[last]), 1, -1), shifted(flat(starts[first]), -1, -1)
        offsets = (0, 0)
    left, right = shifted(flat(ends), 0, 1), shifted(flat(starts), 0, -1)
    left, beside = lax.optimization_barrier((left, beside))
    groups = lax.axis_size("mem")

    def kernel(*refs):
        ensemble_kernel(coarse_x, coarse_y, offsets, *refs[:12], refs[12:12 + groups], *refs[12 + groups:])

    parts = pl.pallas_call(
        kernel,
        out_shape=tuple(jax.ShapeDtypeStruct((levels // groups, fine_x, fine_y), jnp.float32) for _ in range(groups)),
        in_specs=[SMEM] + [VMEM] * 10 + [HBM],
        out_specs=(VMEM,) * groups,
        scratch_shapes=[
            pltpu.VMEM(ens_pert.shape, ens_pert.dtype),
            pltpu.SemaphoreType.DMA,
            pltpu.VMEM((coarse_x + 2 * REACH + 1, coarse_y + PAD, channels), jnp.float32),
            pltpu.VMEM((coarse_x + 1, channels, fine_y), jnp.float32),
        ],
        compiler_params=room(50),
        cost_estimate=pl.CostEstimate(flops=8 << 30, bytes_accessed=8 << 20, transcendentals=0),
        name="ensemble",
    )(me, alpha, above, below, left, left_above, left_below, right, right_above, right_below, mix, ens_pert)
    return parts, beside


def backward(alpha, adjoint_parts, mix, bg_sigma, static_ctrl, ens_pert, me, beside):
    coarse_x, coarse_y, channels = alpha.shape
    members, levels, fine_x, fine_y = ens_pert.shape
    joined = lax.axis_size("tx") == 2
    groups = len(adjoint_parts)
    outside = [coarse_x] if joined else [REACH, REACH + 1]
    strips = [[[REACH, REACH + 1]] * coarse_x] + corner_counts(coarse_x, joined)
    shapes = [bg_sigma.shape, alpha.shape]
    shapes += [(rows, coarse_y, channels) for rows in outside]
    shapes += [(sum(count[side] for count in counts), channels) for side in range(2) for counts in strips]
    n_in, n_mid, n_strip = 5 + groups, len(outside), len(strips)

    def kernel(*refs):
        me_ref, parts, rest = refs[0], refs[1:1 + groups], refs[1 + groups:n_in]
        outs = refs[n_in:n_in + len(shapes)]
        middle = outs[2:2 + n_mid]
        left = outs[2 + n_mid:2 + n_mid + n_strip]
        right = outs[2 + n_mid + n_strip:]
        backward_kernel(
            coarse_x, coarse_y, joined, strips, me_ref, parts, *rest,
            outs[0], outs[1], middle, left, right, *refs[n_in + len(shapes):]
        )

    results = pl.pallas_call(
        kernel,
        out_shape=tuple(jax.ShapeDtypeStruct(shape, jnp.float32) for shape in shapes),
        in_specs=[SMEM] + [VMEM] * (groups + 3) + [HBM],
        out_specs=(VMEM,) * len(shapes),
        scratch_shapes=[
            pltpu.VMEM(bg_sigma.shape, jnp.float32),
            pltpu.VMEM((coarse_x + 1, channels, fine_y), jnp.float32),
            pltpu.VMEM(ens_pert.shape, ens_pert.dtype),
            pltpu.SemaphoreType.DMA((members // math.gcd(members, 5),)),
        ],
        compiler_params=room(50),
        cost_estimate=pl.CostEstimate(flops=8 << 30, bytes_accessed=8 << 20, transcendentals=0),
        name="backward",
    )(me, *adjoint_parts, mix, bg_sigma, static_ctrl, ens_pert)
    results, beside = lax.optimization_barrier((results, beside))
    grad_static, center = results[:2]
    middle = results[2:2 + n_mid]
    left, right = results[2 + n_mid:2 + n_mid + n_strip], results[2 + n_mid + n_strip:]
    moves = [(1, 0)] if joined else [(-1, coarse_x - REACH), (1, 0)]
    places, parts = [], []
    for (by, row), value in zip(moves, middle):
        parts.append(shifted(value, by, 0))
        places.append((row, value.shape[0], None))
    for (by, row), counts, to_left, to_right in zip([(0, 0)] + moves, strips, left, right):
        parts += [shifted(to_left, by, -1), shifted(to_right, by, 1)]
        places += [(row, [count[0] for count in counts], True), (row, [count[1] for count in counts], False)]
    grad_alpha = pl.pallas_call(
        functools.partial(fold_kernel, places),
        out_shape=jax.ShapeDtypeStruct(alpha.shape, jnp.float32),
        in_specs=[VMEM] * (2 + len(parts)),
        out_specs=VMEM,
        compiler_params=room(8),
        cost_estimate=pl.CostEstimate(flops=1 << 20, bytes_accessed=2 << 20, transcendentals=0),
        name="fold",
    )(alpha, center, *parts)
    return grad_alpha, grad_static, beside


def owned_sum(parts):
    count = len(parts)
    total = parts[0]
    for d in range(1, count):
        total = total + lax.ppermute(parts[d], "mem", [(i, (i + d) % count) for i in range(count)])
    return total


def gathered(own):
    count = lax.axis_size("mem")
    return [own] + [lax.ppermute(own, "mem", [(i, (i + d) % count) for i in range(count)]) for d in range(1, count)]


def per_device(
    alpha,
    lv_sqrt,
    ens_pert,
    bg_sigma,
    static_ctrl,
    obs_owner,
    obs_column,
    obs_level,
    obs_frac,
    innovation,
    obs_rinv,
    obs_count,
):
    levels, fine_x, fine_y = bg_sigma.shape
    tiles = lax.axis_size("tx") * lax.axis_size("ty")
    capacity = 2 * obs_owner.shape[0] // tiles
    me = lax.axis_index("mem").astype(jnp.int32).reshape(1)
    outgoing, target = pack(
        tiles, levels, fine_x * fine_y, capacity,
        obs_count, obs_owner[:, 0], obs_column, obs_level, obs_frac, innovation, obs_rinv,
    )
    partial, outgoing = ensemble(alpha, lv_sqrt, ens_pert, me, outgoing)
    incoming = lax.all_to_all(outgoing, ("tx", "ty"), split_axis=0, concat_axis=0, tiled=True)
    partial, incoming = lax.optimization_barrier((partial, incoming))
    increment = owned_sum(partial)
    departure, adjoint = stencil(gathered(increment), incoming, bg_sigma, static_ctrl, me)
    parts, departure = lax.optimization_barrier((gathered(owned_sum(adjoint)), departure))
    returned = lax.all_to_all(departure, ("tx", "ty"), split_axis=0, concat_axis=0, tiled=True)
    grad_alpha, grad_static, returned = backward(
        alpha, parts, lv_sqrt, bg_sigma, static_ctrl, ens_pert, me, returned
    )
    departures = unpack(target, returned.reshape(-1, BLOCK))
    return (grad_alpha, grad_static, departures)


def solution(mesh):
    placed = (
        P("tx", "ty", "mem"),
        P(),
        P("mem", None, "tx", "ty"),
        P(None, "tx", "ty"),
        P(None, "tx", "ty"),
        P(("tx", "ty", "mem"), None),
        P(("tx", "ty", "mem")),
        P(("tx", "ty", "mem")),
        P(None, ("tx", "ty", "mem")),
        P(("tx", "ty", "mem")),
        P(("tx", "ty", "mem")),
        P(("tx", "ty", "mem")),
    )
    return jax.shard_map(
        per_device,
        mesh=mesh,
        in_specs=placed,
        out_specs=(P("tx", "ty", "mem"), P(None, "tx", "ty"), P(("tx", "ty", "mem"))),
        check_vma=False,
    )
```

```python
import functools
import math

import jax
import jax.numpy as jnp
from jax import lax
from jax.experimental import pallas as pl
from jax.experimental.pallas import tpu as pltpu
from jax.sharding import PartitionSpec as P

RATIO = 4
NSTEP = 4
NU = 0.2
VMEM = pl.BlockSpec(memory_space=pltpu.VMEM)
SMEM = pl.BlockSpec(memory_space=pltpu.SMEM)
HBM = pl.BlockSpec(memory_space=pltpu.HBM)


def room(mebibytes):
    return pltpu.CompilerParams(vmem_limit_bytes=mebibytes << 20)

BLOCK = 256
LANES = 128
STEPS = (8, 12, 16, 32)
HALF = jnp.bfloat16


def split_two(value):
    high = value.astype(HALF)
    return high, (value - high.astype(jnp.float32)).astype(HALF)


def dot_nt(a, b):
    return lax.dot_general(a, b, (((1,), (1,)), ((), ())), preferred_element_type=jnp.float32)


def dot_nn(a, b):
    return jnp.dot(a, b, preferred_element_type=jnp.float32)


def iota(shape, dim):
    return lax.broadcasted_iota(jnp.int32, shape, dim)


def row_of(ref, j):
    pair = ref[pl.ds(2 * j, 2), :]
    return jnp.concatenate([pair[0:1], pair[1:2]], 1)


def rank_kernel(tiles, levels, capacity, count_ref, ints_ref, target_ref, carry, total):
    size = target_ref.shape[0]
    owner_ref, level_ref = [ints_ref.at[pl.ds(i * size, size)] for i in range(2)]
    blocks = size * LANES // BLOCK
    keys = tiles * levels
    count = count_ref[0]

    def onehot(j):
        live = iota((1, BLOCK), 1) + j * BLOCK < count
        key = jnp.where(live, row_of(owner_ref, j) * levels + row_of(level_ref, j), -1)
        return live, iota((keys, BLOCK), 0) == key

    ones = jnp.ones((BLOCK, LANES), HALF)
    total[...] = jnp.zeros_like(total)

    many = math.gcd(blocks, 8)

    def count_group(g, unused):
        masks = [onehot(g * many + i)[1] for i in range(many)]
        counted = jnp.concatenate([jnp.where(mask, 1.0, 0.0).astype(HALF) for mask in masks], 1)
        total[...] += dot_nn(counted, jnp.concatenate([ones] * many, 0))
        return unused

    lax.fori_loop(0, blocks // many, count_group, 0)
    high = jnp.floor(total[...] * (1.0 / LANES))
    low = total[...] - high * LANES
    row_key, col_key = iota((keys, keys), 0), iota((keys, keys), 1)
    before = jnp.where((col_key < row_key) & (col_key // levels == row_key // levels), 1.0, 0.0).astype(HALF)
    start = dot_nn(before, high.astype(HALF)) * LANES + dot_nn(before, low.astype(HALF))
    carry[...] = start + ((iota((keys, LANES), 0) // levels) * capacity).astype(jnp.float32)

    earlier = jnp.where(iota((BLOCK, BLOCK), 0) < iota((BLOCK, BLOCK), 1), 1.0, 0.0).astype(HALF)
    prefix = jnp.concatenate([earlier, ones], 1)

    def rank_group(g, unused):
        now = carry[...]
        seen = [onehot(g * many + i) for i in range(many)]
        ranks = [dot_nn(jnp.where(mask, 1.0, 0.0).astype(HALF), prefix) for live, mask in seen]
        for i, ((live, mask), rank) in enumerate(zip(seen, ranks)):
            here = rank[:, :BLOCK] + jnp.concatenate([now] * (BLOCK // LANES), 1)
            now = now + rank[:, BLOCK:]
            slot = jnp.sum(jnp.where(mask, here, 0.0), 0, keepdims=True)
            target = jnp.where(live, slot.astype(jnp.int32), -1)
            target_ref[pl.ds(2 * (g * many + i), 2), :] = jnp.concatenate([target[:, :LANES], target[:, LANES:]], 0)
        carry[...] = now
        return unused

    lax.fori_loop(0, blocks // many, rank_group, 0)


def ranked(tiles, levels, capacity, count, ints):
    return pl.pallas_call(
        functools.partial(rank_kernel, tiles, levels, capacity),
        out_shape=jax.ShapeDtypeStruct((ints.shape[0] // 3, LANES), jnp.int32),
        in_specs=[SMEM, VMEM],
        out_specs=VMEM,
        scratch_shapes=[
            pltpu.VMEM((tiles * levels, LANES), jnp.float32),
            pltpu.VMEM((tiles * levels, LANES), jnp.float32),
        ],
        compiler_params=room(16),
        cost_estimate=pl.CostEstimate(flops=1 << 20, bytes_accessed=1 << 17, transcendentals=0),
        name="rank",
    )(count, ints)


def pack_kernel(tiles, plane, capacity, target_ref, ints_ref, floats_ref, frac_ref, out_ref, *scratch):
    gathered, left_a, right_a, left_b, right_b = scratch
    size = target_ref.shape[0]
    level_ref, column_ref = [ints_ref.at[pl.ds(i * size, size)] for i in (1, 2)]
    innov_ref, rinv_ref = [floats_ref.at[pl.ds(i * size, size)] for i in range(2)]
    blocks = size * LANES // BLOCK
    deep = capacity // BLOCK
    slot_rows = tiles * deep
    group = 4
    gathered[...] = jnp.zeros_like(gathered)

    def place(j):
        target = row_of(target_ref, j)
        rows = jnp.where(iota((slot_rows, BLOCK), 0) == (target >> 8), 1.0, 0.0).astype(HALF)
        lanes = jnp.where(iota((BLOCK, BLOCK), 0) == (target & (BLOCK - 1)), 1.0, 0.0).astype(HALF)
        column = row_of(column_ref, j)
        frac = frac_ref[:, pl.ds(pl.multiple_of(j * BLOCK, BLOCK), BLOCK)]
        terms = []
        for value in (frac[0:1], frac[1:2], frac[2:3], row_of(innov_ref, j), row_of(rinv_ref, j)):
            terms.extend(split_two(jnp.broadcast_to(value, (16, BLOCK))))
        for value in (row_of(level_ref, j), column >> 7, column & (LANES - 1)):
            terms.append(jnp.broadcast_to(value.astype(jnp.float32), (16, BLOCK)).astype(HALF))
        spread = [rows * jnp.concatenate([term] * (slot_rows // 16), 0) for term in terms]
        return jnp.concatenate(spread, 0), lanes

    def build(g, left, right):
        for i in range(group):
            lanes = slice(i * BLOCK, (i + 1) * BLOCK)
            left[:, lanes], right[:, lanes] = place(g * group + i)

    def multiply(left, right):
        gathered[...] += dot_nt(left[...], right[...])

    def scatter_pair(g, unused):
        build(2 * g + 1, left_b, right_b)
        multiply(left_a, right_a)
        build(jnp.minimum(2 * g + 2, blocks // group - 1), left_a, right_a)
        multiply(left_b, right_b)
        return unused

    build(0, left_a, right_a)
    lax.fori_loop(0, blocks // (2 * group), scatter_pair, 0)

    def part(index, tile):
        begin = index * slot_rows + tile * deep
        return gathered[begin:begin + deep, :]

    for tile in range(tiles):
        for p in range(5):
            out_ref[tile, p * deep:(p + 1) * deep, :] = part(2 * p, tile) + part(2 * p + 1, tile)
        base = part(10, tile) * plane + part(11, tile) * LANES + part(12, tile)
        out_ref[tile, 5 * deep:6 * deep, :] = base


def pack(tiles, plane, capacity, target, ints, floats, frac):
    deep = capacity // BLOCK
    rows = 13 * tiles * deep
    return pl.pallas_call(
        functools.partial(pack_kernel, tiles, plane, capacity),
        out_shape=jax.ShapeDtypeStruct((tiles, 6 * deep, BLOCK), jnp.float32),
        in_specs=[VMEM] * 4,
        out_specs=VMEM,
        scratch_shapes=[pltpu.VMEM((rows, BLOCK), jnp.float32)]
        + [pltpu.VMEM((count, 4 * BLOCK), HALF) for count in (rows, BLOCK) * 2],
        compiler_params=room(16),
        cost_estimate=pl.CostEstimate(flops=8 << 30, bytes_accessed=1 << 20, transcendentals=0),
        name="pack",
    )(target, ints, floats, frac)


def stencil_kernel(
    me_ref, parts_refs, sigma_ref, static_ref, incoming_ref,
    dep_ref, adj_refs,
    field, field_t, adjoint, spans, spans_ref, sem,
):
    levels, fine_x, fine_y = sigma_ref.shape
    sources, packed_rows, block = incoming_ref.shape
    deep = packed_rows // 6
    plane = fine_x * fine_y
    chunk = LANES // fine_x
    groups = len(parts_refs)
    share = levels // groups
    rows = levels * fine_x
    me = me_ref[0]
    halves = block // LANES
    column = iota((sources * deep, LANES), 1)
    found = jnp.zeros((sources * deep, LANES), jnp.int32)
    for half in range(halves):
        lanes = slice(half * LANES, (half + 1) * LANES)
        used = incoming_ref[:, 4 * deep:5 * deep, lanes].reshape(sources * deep, LANES) > 0.0
        level = jnp.floor(incoming_ref[:, 5 * deep:, lanes].reshape(sources * deep, LANES) * (1.0 / plane))
        lowest = jnp.min(jnp.where(used, level, float(levels)), 1, keepdims=True).astype(jnp.int32)
        highest = jnp.max(jnp.where(used, level, -1.0), 1, keepdims=True).astype(jnp.int32)
        found = jnp.where((column == 2 * half) & (highest >= 0), lowest, found)
        found = jnp.where((column == 2 * half + 1) & (highest >= 0), highest + 2 - lowest, found)
    spans[...] = found
    fetch = pltpu.make_async_copy(spans, spans_ref, sem)
    fetch.start()
    adjoint[...] = jnp.zeros_like(adjoint)
    dep_ref[...] = jnp.zeros_like(dep_ref)
    field[rows:, :] = jnp.zeros((field.shape[0] - rows, fine_y), jnp.float32)
    for slot, part in enumerate(parts_refs):
        start = lax.rem(me + groups - slot, groups) * share
        static = sigma_ref[pl.ds(start, share)] * static_ref[pl.ds(start, share)]
        where = pl.ds(pl.multiple_of(start * fine_x, LANES), share * fine_x)
        field[where, :] = (part[...] + static).reshape(share * fine_x, fine_y)
    for shift in range(chunk):
        field_t[shift, :, rows:] = jnp.zeros((2 * fine_y, field_t.shape[2] - rows), HALF)
        for g in range(rows // LANES):
            begin = shift * fine_x + g * LANES
            high, low = split_two(field[begin:begin + LANES, :].T)
            field_t[shift, :fine_y, g * LANES:(g + 1) * LANES] = high
            field_t[shift, fine_y:, g * LANES:(g + 1) * LANES] = low

    fetch.wait()

    def block_of(source, at, half):
        def row(p):
            return incoming_ref[source, pl.ds(p * deep + at, 1), :][:, half * LANES:(half + 1) * LANES]

        base = row(5)
        level = jnp.floor(base * (1.0 / plane))
        rest = base - level * plane
        across = jnp.floor(rest * (1.0 / fine_y))
        along = rest - across * fine_y
        frac_x, frac_y, frac_l = row(0), row(1), row(2)
        rows_x = iota((fine_x, LANES), 0).astype(jnp.float32)
        pick_x = jnp.where(rows_x == across, 1.0 - frac_x, 0.0) + jnp.where(rows_x == across + 1.0, frac_x, 0.0)
        rows_y = iota((fine_y, LANES), 0).astype(jnp.float32)
        pick_y = jnp.where(rows_y == along, 1.0 - frac_y, 0.0) + jnp.where(rows_y == along + 1.0, frac_y, 0.0)

        def weights(bottom, reach):
            offset = level - jnp.asarray(bottom, jnp.int32).astype(jnp.float32)
            rows_l = iota((reach, LANES), 0).astype(jnp.float32)
            pick_l = jnp.where(rows_l == offset, 1.0 - frac_l, 0.0) + jnp.where(rows_l == offset + 1.0, frac_l, 0.0)
            picks = [pick_x * pick_l[g:g + 1] for g in range(reach)]
            return jnp.concatenate(split_two(jnp.concatenate(picks, 0)), 1)

        def finish(picked):
            departure = jnp.sum(picked * pick_y, 0, keepdims=True) - row(3)
            turned = jnp.concatenate(split_two((pick_y * (row(4) * departure)).T), 1)
            return departure, jnp.concatenate([turned, turned], 0)

        return weights, finish

    def look(bottom, pick):
        if isinstance(bottom, int):
            seen = dot_nn(field_t[0, :, :pick.shape[0]], pick)
        else:
            lanes = pl.ds(pl.multiple_of((bottom // chunk) * LANES, LANES), pick.shape[0])
            seen = dot_nn(field_t[lax.rem(bottom, chunk), :, lanes], pick)
        return seen[:fine_y, :LANES] + (seen[:fine_y, LANES:] + seen[fine_y:, :LANES])

    def spread(pick, term):
        both = dot_nn(pick, term)
        return both[:, :fine_y] + both[:, fine_y:]

    def rows_at(bottom, reach):
        return pl.ds(pl.multiple_of(bottom * fine_x, fine_x), reach * fine_x)

    def together(blocks, bottoms, reach):
        parts = [block_of(*block) for block in blocks]
        picks = [weights(bottom, reach) for (weights, finish), bottom in zip(parts, bottoms)]
        seen = [look(bottom, pick) for bottom, pick in zip(bottoms, picks)]
        done = [finish(value) for (weights, finish), value in zip(parts, seen)]
        adds = [spread(pick, term) for pick, (departure, term) in zip(picks, done)]
        keep(blocks, [departure for departure, term in done])
        for bottom, add in zip(bottoms, adds):
            adjoint[rows_at(bottom, reach), :] += add

    def keep(blocks, departures):
        for i in range(0, len(blocks), halves):
            source, at, half = blocks[i]
            dep_ref[source, pl.ds(at, 1), :] = jnp.concatenate(departures[i:i + halves], 1)

    step = 2 if deep % 2 == 0 else 1

    def one_step(i, unused):
        source, at = i // (deep // step), lax.rem(i, deep // step) * step
        blocks = [(source, at + r, half) for r in range(step) for half in range(halves)]
        numbers = [(source * deep + at + r, half) for r in range(step) for half in range(halves)]
        bottoms = [spans_ref[row, 2 * half] for row, half in numbers]
        needs = [spans_ref[row, 2 * half + 1] for row, half in numbers]
        most = functools.reduce(jnp.maximum, needs)

        for below, reach in zip((0,) + STEPS, STEPS):
            @pl.when((most > below) & (most <= reach))
            def _():
                together(blocks, [0] * len(blocks) if reach == levels else bottoms, reach)

        return unused

    lax.fori_loop(0, sources * deep // step, one_step, 0)
    for slot, adj_ref in enumerate(adj_refs):
        start = lax.rem(me + slot, groups) * share * fine_x
        adj_ref[...] = adjoint[pl.ds(pl.multiple_of(start, LANES), share * fine_x), :].reshape(share, fine_x, fine_y)


def stencil(parts, incoming, bg_sigma, static_ctrl, me):
    levels, fine_x, fine_y = bg_sigma.shape
    sources, packed_rows, block = incoming.shape
    deep, groups = packed_rows // 6, len(parts)
    rows = levels * fine_x
    padded = rows + STEPS[-2] * fine_x

    def kernel(*refs):
        parts_end = 1 + groups
        stencil_kernel(
            refs[0], refs[1:parts_end], *refs[parts_end:parts_end + 4],
            refs[parts_end + 4:parts_end + 4 + groups], *refs[parts_end + 4 + groups:]
        )

    results = pl.pallas_call(
        kernel,
        out_shape=(jax.ShapeDtypeStruct((sources, deep, block), jnp.float32),)
        + tuple(jax.ShapeDtypeStruct(part.shape, jnp.float32) for part in parts),
        in_specs=[SMEM] + [VMEM] * (groups + 3),
        out_specs=(VMEM,) * (1 + groups),
        scratch_shapes=[
            pltpu.VMEM((padded, fine_y), jnp.float32),
            pltpu.VMEM((LANES // fine_x, 2 * fine_y, padded), HALF),
            pltpu.VMEM((padded, fine_y), jnp.float32),
            pltpu.VMEM((sources * deep, LANES), jnp.int32),
            pltpu.SMEM((sources * deep, LANES), jnp.int32),
            pltpu.SemaphoreType.DMA,
        ],
        compiler_params=room(32),
        cost_estimate=pl.CostEstimate(flops=16 << 30, bytes_accessed=1 << 20, transcendentals=0),
        name="stencil",
    )(me, *parts, bg_sigma, static_ctrl, incoming)
    return results[0], results[1:]


def unpack_kernel(target_ref, table_ref, out_ref):
    slot_rows = table_ref.shape[0]
    high, low = split_two(table_ref[...])
    both = jnp.concatenate([high.astype(jnp.float32), low.astype(jnp.float32)], 0)
    turned = both.T.astype(HALF)
    group = 4

    def some_blocks(g, unused):
        for i in range(group):
            pair = target_ref[pl.ds(2 * (g * group + i), 2), :]
            target = jnp.concatenate([pair[0:1], pair[1:2]], 1)
            rows = jnp.where(iota((slot_rows, BLOCK), 0) == (target >> 8), 1.0, 0.0).astype(HALF)
            lines = dot_nn(turned, jnp.concatenate([rows, rows], 0))
            lane = iota((BLOCK, BLOCK), 0) == (target & (BLOCK - 1))
            found = jnp.sum(jnp.where(lane, lines, 0.0), 0, keepdims=True)
            out_ref[pl.ds(2 * (g * group + i), 2), :] = jnp.concatenate([found[:, :LANES], found[:, LANES:]], 0)
        return unused

    lax.fori_loop(0, target_ref.shape[0] // (2 * group), some_blocks, 0)


def unpack(target, table):
    vmem = pl.BlockSpec(memory_space=pltpu.VMEM)
    return pl.pallas_call(
        unpack_kernel,
        out_shape=jax.ShapeDtypeStruct(target.shape, jnp.float32),
        in_specs=[vmem, vmem],
        out_specs=vmem,
        compiler_params=room(8),
        cost_estimate=pl.CostEstimate(flops=2 << 30, bytes_accessed=1 << 18, transcendentals=0),
        name="unpack",
    )(target, table).reshape(-1)


REACH = NSTEP
EDGE = 8
PAD = 2 * EDGE
SCALE = NU**NSTEP


def interpolation(shape, fine_dim, coarse_dim, shift):
    fine, coarse = iota(shape, fine_dim), iota(shape, coarse_dim) - shift
    frac = (fine % RATIO).astype(jnp.float32) * (1.0 / RATIO)
    low = jnp.where(coarse == fine // RATIO, 1.0 - frac, 0.0)
    return (low + jnp.where(coarse == fine // RATIO + 1, frac, 0.0)).astype(HALF)


def interpolation_rows(fine_x, depth, copies, transposed):
    long, short = EDGE * fine_x, EDGE * depth
    shape = (short, long) if transposed else (long, copies * short)
    fine, coarse = iota(shape, 1 if transposed else 0), iota(shape, 0 if transposed else 1)
    for copy in range(1, copies):
        coarse = jnp.where(coarse >= short, coarse - short, coarse)
    place, target = fine % fine_x, coarse // EDGE
    frac = (place % RATIO).astype(jnp.float32) * (1.0 / RATIO)
    low = jnp.where(target == place // RATIO, 1.0 - frac, 0.0)
    weight = low + jnp.where(target == place // RATIO + 1, frac, 0.0)
    return jnp.where(fine // fine_x == coarse % EDGE, weight, 0.0).astype(HALF)


def mixing(mix_ref):
    levels = mix_ref.shape[0]
    tile = jnp.where(iota((LANES, levels), 0) % levels == iota((LANES, levels), 1), 1.0, 0.0).astype(HALF)
    same = iota((LANES, LANES), 0) // levels == iota((LANES, LANES), 1) // levels
    terms = []
    for term in split_two(mix_ref[...]):
        tiled = dot_nt(dot_nn(tile, term).astype(HALF), tile)
        terms.append(jnp.where(same, tiled, 0.0).astype(HALF))
    return terms


def corner_counts(coarse_x, joined):
    above = [[j, j + 1] for j in range(REACH)]
    below = [[REACH - i, REACH + 1 - i] for i in range(REACH + 1)]
    if not joined:
        return [above, below]
    gap = [[0, 0]] * (coarse_x - REACH)
    high, low = gap + above, below + gap[1:]
    return [[[max(a, b) for a, b in zip(*pair)] for pair in zip(high, low)]]


def neighbours(field):
    width = field.shape[1]
    return pltpu.roll(field, 1, 1) + pltpu.roll(field, width - 1, 1)


def ensemble_kernel(
    coarse_x, coarse_y, offsets,
    me_ref, alpha_ref, above_ref, below_ref,
    left_ref, left_above_ref, left_below_ref, right_ref, right_above_ref, right_below_ref,
    mix_ref, pert_hbm, out_refs, pert_ref, sem, ext, coarse,
):
    members, levels, fine_x, fine_y = pert_ref.shape
    channels = alpha_ref.shape[2]
    fetch = pltpu.make_async_copy(pert_hbm, pert_ref, sem)
    fetch.start()
    ext[:, :EDGE, :] = jnp.zeros((ext.shape[0], EDGE, channels), jnp.float32)
    ext[:, EDGE + coarse_y:, :] = jnp.zeros((ext.shape[0], EDGE, channels), jnp.float32)
    above, below = offsets
    groups = (
        (0, REACH, above, above_ref, left_above_ref, right_above_ref),
        (REACH, coarse_x, 0, alpha_ref, left_ref, right_ref),
        (REACH + coarse_x, REACH + 1, below, below_ref, left_below_ref, right_below_ref),
    )
    for begin, count, offset, middle, left, right in groups:
        ext[begin:begin + count, EDGE:EDGE + coarse_y, :] = middle[offset:offset + count]
        for i in range(count):
            at = offset + i
            ext[begin + i, EDGE - REACH:EDGE, :] = left[at * REACH:(at + 1) * REACH, :]
            ext[begin + i, EDGE + coarse_y:EDGE + coarse_y + REACH + 1, :] = right[
                at * (REACH + 1):(at + 1) * (REACH + 1), :
            ]
    spread_y = interpolation((coarse_y + PAD, fine_y), 1, 0, EDGE)
    spread_y = jnp.concatenate([spread_y, spread_y], 0)
    high, low = mixing(mix_ref)
    mix = jnp.concatenate([high, high, low], 1)

    def one_group(g, unused):
        lanes = pl.ds(pl.multiple_of(g * LANES, LANES), LANES)
        field = ext[:, :, lanes]
        for step in range(NSTEP):
            inner = field[1:-1]
            field = inner + field[2:] + field[:-2] + neighbours(inner)
        high, low = split_two(field * SCALE)
        both = jnp.concatenate([high.astype(jnp.float32), low.astype(jnp.float32)], 1)
        for c in range(coarse_x + 1):
            wide_high, wide_low = split_two(dot_nn(both[c].T.astype(HALF), spread_y))
            coarse[c, lanes, :] = dot_nn(mix, jnp.concatenate([wide_high, wide_low, wide_high], 0))
        return unused

    lax.fori_loop(0, channels // LANES, one_group, 0, unroll=True)
    fetch.wait()
    depth = coarse_x + 2
    spread_x = interpolation_rows(fine_x, depth, 2, False)
    share = levels // len(out_refs)
    unroll = math.gcd(members // 2, 5)

    for slot, out_ref in enumerate(out_refs):
        for sub in range(share // EDGE):
            first = pl.multiple_of(lax.rem(me_ref[0] + slot, len(out_refs)) * share + sub * EDGE, EDGE)

            def stacked(k):
                rows = pl.ds(pl.multiple_of(k * levels + first, EDGE), EDGE)
                parts = [coarse[c, rows, :] for c in range(coarse_x + 1)]
                return jnp.concatenate(parts + [jnp.zeros((EDGE, fine_y), jnp.float32)], 0)

            def perturbation(k):
                return pert_ref[k, pl.ds(first, EDGE)].reshape(EDGE * fine_x, fine_y).astype(jnp.float32)

            def pairs(p, total):
                for i in range(unroll):
                    k = 2 * (unroll * p + i)
                    high, low = split_two(jnp.concatenate([stacked(k), stacked(k + 1)], 1))
                    fine = dot_nn(spread_x, jnp.concatenate([high, low], 0))
                    total = total + (fine[:, :fine_y] * perturbation(k) + fine[:, fine_y:] * perturbation(k + 1))
                return total

            total = lax.fori_loop(
                0, members // (2 * unroll), pairs, jnp.zeros((EDGE * fine_x, fine_y), jnp.float32)
            )
            out_ref[sub * EDGE:(sub + 1) * EDGE] = total.reshape(EDGE, fine_x, fine_y)


def backward_kernel(
    coarse_x, coarse_y, joined, strips,
    me_ref, parts_refs, mix_ref, sigma_ref, static_ref, pert_hbm,
    grad_ref, center_ref, middle_refs, left_refs, right_refs,
    adjoint, coarse, pert_ref, sems,
):
    members, levels, fine_x, fine_y = pert_ref.shape
    channels = members * levels
    unroll = members // sems.shape[0]
    copies = []
    for p in range(sems.shape[0]):
        some = pl.ds(p * unroll, unroll)
        copies.append(pltpu.make_async_copy(pert_hbm.at[some], pert_ref.at[some], sems.at[p]))
        copies[p].start()
    share = levels // len(parts_refs)
    for slot, part in enumerate(parts_refs):
        first = lax.rem(me_ref[0] + len(parts_refs) - slot, len(parts_refs)) * share
        adjoint[pl.ds(first, share)] = part[...]
    grad_ref[...] = static_ref[...] + sigma_ref[...] * adjoint[...]
    depth = coarse_x + 2
    fold_x = interpolation_rows(fine_x, depth, 1, True)

    for p, copy in enumerate(copies):
        copy.wait()

        def one_level_group(group, unused):
            some = pl.ds(group * EDGE, EDGE)
            field = adjoint[some].reshape(EDGE * fine_x, fine_y)
            for k in range(p * unroll, (p + 1) * unroll):
                scaled = pert_ref[k, some].reshape(EDGE * fine_x, fine_y).astype(jnp.float32)
                high, low = split_two(scaled * field)
                both = dot_nn(fold_x, jnp.concatenate([high, low], 1))
                rows = pl.ds(pl.multiple_of(k * levels + group * EDGE, EDGE), EDGE)
                for c in range(coarse_x + 1):
                    piece = both[c * EDGE:(c + 1) * EDGE]
                    coarse[c, rows, :] = piece[:, :fine_y] + piece[:, fine_y:]
            return unused

        lax.fori_loop(0, levels // EDGE, one_level_group, 0)

    fold_y = interpolation((coarse_y + PAD, fine_y), 1, 0, EDGE)
    fold_y = jnp.concatenate([fold_y, fold_y], 1)
    high, low = mixing(mix_ref)
    mix = jnp.concatenate([high, high, low], 0)

    def one_group(g, unused):
        lanes = pl.ds(pl.multiple_of(g * LANES, LANES), LANES)
        rows = []
        for c in range(coarse_x + 1):
            high, low = split_two(coarse[c, lanes, :])
            narrow = dot_nt(fold_y, jnp.concatenate([high, low], 1))
            high, low = split_two(narrow)
            rows.append(dot_nn(jnp.concatenate([high, low, high], 1), mix)[None])
        field = jnp.concatenate(rows, 0) * SCALE
        empty = jnp.zeros((1,) + field.shape[1:], jnp.float32)
        for step in range(NSTEP):
            own = field + neighbours(field)
            field = jnp.concatenate([field, empty, empty], 0) + jnp.concatenate([empty, own, empty], 0) + jnp.concatenate(
                [empty, empty, field], 0
            )
        inside = field[REACH:REACH + coarse_x]
        up, down = field[:REACH], field[REACH + coarse_x:]
        if joined:
            none = jnp.zeros((coarse_x - REACH - 1,) + field.shape[1:], jnp.float32)
            outside = [jnp.concatenate([down, none], 0) + jnp.concatenate([none, empty, up], 0)]
        else:
            outside = [up, down]
        center_ref[:, :, lanes] = inside[:, EDGE:EDGE + coarse_y]
        for ref, value in zip(middle_refs, outside):
            ref[:, :, lanes] = value[:, EDGE:EDGE + coarse_y]
        for left, right, value, counts in zip(left_refs, right_refs, [inside] + outside, strips):
            at_left, at_right = 0, 0
            for i, (to_left, to_right) in enumerate(counts):
                if to_left:
                    left[at_left:at_left + to_left, lanes] = value[i, EDGE - to_left:EDGE]
                if to_right:
                    right[at_right:at_right + to_right, lanes] = value[i, EDGE + coarse_y:EDGE + coarse_y + to_right]
                at_left, at_right = at_left + to_left, at_right + to_right
        return unused

    lax.fori_loop(0, channels // LANES, one_group, 0, unroll=True)


def fold_kernel(places, alpha_ref, center_ref, *refs):
    part_refs, out_ref = refs[:-1], refs[-1]
    coarse_y = out_ref.shape[1]
    out_ref[...] = alpha_ref[...] + center_ref[...]
    for (row, counts, at_end), ref in zip(places, part_refs):
        if at_end is None:
            out_ref[row:row + counts] += ref[...]
            continue
        at = 0
        for i, count in enumerate(counts):
            if count:
                begin = coarse_y - count if at_end else 0
                out_ref[row + i, begin:begin + count, :] += ref[at:at + count, :]
            at += count


def shifted(value, by_x, by_y):
    count_x, count_y = lax.axis_size("tx"), lax.axis_size("ty")
    pairs = [
        (x * count_y + y, (x + by_x) % count_x * count_y + (y + by_y) % count_y)
        for x in range(count_x)
        for y in range(count_y)
    ]
    return lax.ppermute(value, ("tx", "ty"), pairs)


def ensemble(alpha, mix, ens_pert, me, beside):
    coarse_x, coarse_y, channels = alpha.shape
    members, levels, fine_x, fine_y = ens_pert.shape
    joined = lax.axis_size("tx") == 2
    ends = alpha[:, coarse_y - REACH:]
    starts = alpha[:, :REACH + 1]

    def flat(strip):
        return strip.reshape(-1, channels)

    if joined:
        other = shifted(alpha, 1, 0)
        above = below = other
        left_above = left_below = shifted(flat(ends), 1, 1)
        right_above = right_below = shifted(flat(starts), 1, -1)
        offsets = (coarse_x - REACH, 0)
    else:
        last = slice(coarse_x - REACH, coarse_x)
        first = slice(0, REACH + 1)
        above, below = shifted(alpha[last], 1, 0), shifted(alpha[first], -1, 0)
        left_above, left_below = shifted(flat(ends[last]), 1, 1), shifted(flat(ends[first]), -1, 1)
        right_above, right_below = shifted(flat(starts[last]), 1, -1), shifted(flat(starts[first]), -1, -1)
        offsets = (0, 0)
    left, right = shifted(flat(ends), 0, 1), shifted(flat(starts), 0, -1)
    left, beside = lax.optimization_barrier((left, beside))
    groups = lax.axis_size("mem")

    def kernel(*refs):
        ensemble_kernel(coarse_x, coarse_y, offsets, *refs[:12], refs[12:12 + groups], *refs[12 + groups:])

    parts = pl.pallas_call(
        kernel,
        out_shape=tuple(jax.ShapeDtypeStruct((levels // groups, fine_x, fine_y), jnp.float32) for _ in range(groups)),
        in_specs=[SMEM] + [VMEM] * 10 + [HBM],
        out_specs=(VMEM,) * groups,
        scratch_shapes=[
            pltpu.VMEM(ens_pert.shape, ens_pert.dtype),
            pltpu.SemaphoreType.DMA,
            pltpu.VMEM((coarse_x + 2 * REACH + 1, coarse_y + PAD, channels), jnp.float32),
            pltpu.VMEM((coarse_x + 1, channels, fine_y), jnp.float32),
        ],
        compiler_params=room(50),
        cost_estimate=pl.CostEstimate(flops=8 << 30, bytes_accessed=8 << 20, transcendentals=0),
        name="ensemble",
    )(me, alpha, above, below, left, left_above, left_below, right, right_above, right_below, mix, ens_pert)
    return parts, beside


def backward(alpha, adjoint_parts, mix, bg_sigma, static_ctrl, ens_pert, me, beside):
    coarse_x, coarse_y, channels = alpha.shape
    members, levels, fine_x, fine_y = ens_pert.shape
    joined = lax.axis_size("tx") == 2
    groups = len(adjoint_parts)
    outside = [coarse_x] if joined else [REACH, REACH + 1]
    strips = [[[REACH, REACH + 1]] * coarse_x] + corner_counts(coarse_x, joined)
    shapes = [bg_sigma.shape, alpha.shape]
    shapes += [(rows, coarse_y, channels) for rows in outside]
    shapes += [(sum(count[side] for count in counts), channels) for side in range(2) for counts in strips]
    n_in, n_mid, n_strip = 5 + groups, len(outside), len(strips)

    def kernel(*refs):
        me_ref, parts, rest = refs[0], refs[1:1 + groups], refs[1 + groups:n_in]
        outs = refs[n_in:n_in + len(shapes)]
        middle = outs[2:2 + n_mid]
        left = outs[2 + n_mid:2 + n_mid + n_strip]
        right = outs[2 + n_mid + n_strip:]
        backward_kernel(
            coarse_x, coarse_y, joined, strips, me_ref, parts, *rest,
            outs[0], outs[1], middle, left, right, *refs[n_in + len(shapes):]
        )

    results = pl.pallas_call(
        kernel,
        out_shape=tuple(jax.ShapeDtypeStruct(shape, jnp.float32) for shape in shapes),
        in_specs=[SMEM] + [VMEM] * (groups + 3) + [HBM],
        out_specs=(VMEM,) * len(shapes),
        scratch_shapes=[
            pltpu.VMEM(bg_sigma.shape, jnp.float32),
            pltpu.VMEM((coarse_x + 1, channels, fine_y), jnp.float32),
            pltpu.VMEM(ens_pert.shape, ens_pert.dtype),
            pltpu.SemaphoreType.DMA((members // math.gcd(members, 5),)),
        ],
        compiler_params=room(50),
        cost_estimate=pl.CostEstimate(flops=8 << 30, bytes_accessed=8 << 20, transcendentals=0),
        name="backward",
    )(me, *adjoint_parts, mix, bg_sigma, static_ctrl, ens_pert)
    results, beside = lax.optimization_barrier((results, beside))
    grad_static, center = results[:2]
    middle = results[2:2 + n_mid]
    left, right = results[2 + n_mid:2 + n_mid + n_strip], results[2 + n_mid + n_strip:]
    moves = [(1, 0)] if joined else [(-1, coarse_x - REACH), (1, 0)]
    places, parts = [], []
    for (by, row), value in zip(moves, middle):
        parts.append(shifted(value, by, 0))
        places.append((row, value.shape[0], None))
    for (by, row), counts, to_left, to_right in zip([(0, 0)] + moves, strips, left, right):
        parts += [shifted(to_left, by, -1), shifted(to_right, by, 1)]
        places += [(row, [count[0] for count in counts], True), (row, [count[1] for count in counts], False)]
    grad_alpha = pl.pallas_call(
        functools.partial(fold_kernel, places),
        out_shape=jax.ShapeDtypeStruct(alpha.shape, jnp.float32),
        in_specs=[VMEM] * (2 + len(parts)),
        out_specs=VMEM,
        compiler_params=room(8),
        cost_estimate=pl.CostEstimate(flops=1 << 20, bytes_accessed=2 << 20, transcendentals=0),
        name="fold",
    )(alpha, center, *parts)
    return grad_alpha, grad_static, beside


def owned_sum(parts):
    count = len(parts)
    total = parts[0]
    for d in range(1, count):
        total = total + lax.ppermute(parts[d], "mem", [(i, (i + d) % count) for i in range(count)])
    return total


def gathered(own):
    count = lax.axis_size("mem")
    return [own] + [lax.ppermute(own, "mem", [(i, (i + d) % count) for i in range(count)]) for d in range(1, count)]


def per_device(
    alpha,
    lv_sqrt,
    ens_pert,
    bg_sigma,
    static_ctrl,
    obs_owner,
    obs_column,
    obs_level,
    obs_frac,
    innovation,
    obs_rinv,
    obs_count,
):
    levels, fine_x, fine_y = bg_sigma.shape
    tiles = lax.axis_size("tx") * lax.axis_size("ty")
    capacity = 2 * obs_owner.shape[0] // tiles
    me = lax.axis_index("mem").astype(jnp.int32).reshape(1)
    rows = obs_owner.shape[0] // LANES
    ints = jnp.concatenate([obs_owner[:, 0], obs_level, obs_column]).reshape(3 * rows, LANES)
    floats = jnp.concatenate([innovation, obs_rinv]).reshape(2 * rows, LANES)
    target = ranked(tiles, levels, capacity, obs_count, ints)
    partial, target = ensemble(alpha, lv_sqrt, ens_pert, me, target)
    partial, target = lax.optimization_barrier((partial, target))
    outgoing = pack(tiles, fine_x * fine_y, capacity, target, ints, floats, obs_frac)
    incoming = lax.all_to_all(outgoing, ("tx", "ty"), split_axis=0, concat_axis=0, tiled=True)
    increment = owned_sum(partial)
    departure, adjoint = stencil(gathered(increment), incoming, bg_sigma, static_ctrl, me)
    parts, departure = lax.optimization_barrier((gathered(owned_sum(adjoint)), departure))
    returned = lax.all_to_all(departure, ("tx", "ty"), split_axis=0, concat_axis=0, tiled=True)
    grad_alpha, grad_static, returned = backward(
        alpha, parts, lv_sqrt, bg_sigma, static_ctrl, ens_pert, me, returned
    )
    departures = unpack(target, returned.reshape(-1, BLOCK))
    return (grad_alpha, grad_static, departures)


def solution(mesh):
    placed = (
        P("tx", "ty", "mem"),
        P(),
        P("mem", None, "tx", "ty"),
        P(None, "tx", "ty"),
        P(None, "tx", "ty"),
        P(("tx", "ty", "mem"), None),
        P(("tx", "ty", "mem")),
        P(("tx", "ty", "mem")),
        P(None, ("tx", "ty", "mem")),
        P(("tx", "ty", "mem")),
        P(("tx", "ty", "mem")),
        P(("tx", "ty", "mem")),
    )
    return jax.shard_map(
        per_device,
        mesh=mesh,
        in_specs=placed,
        out_specs=(P("tx", "ty", "mem"), P(None, "tx", "ty"), P(("tx", "ty", "mem"))),
        check_vma=False,
    )
```

```python
import functools
import math

import jax
import jax.numpy as jnp
from jax import lax
from jax.experimental import pallas as pl
from jax.experimental.pallas import tpu as pltpu
from jax.sharding import PartitionSpec as P

RATIO = 4
NSTEP = 4
NU = 0.2
VMEM = pl.BlockSpec(memory_space=pltpu.VMEM)
SMEM = pl.BlockSpec(memory_space=pltpu.SMEM)
HBM = pl.BlockSpec(memory_space=pltpu.HBM)


def room(mebibytes):
    return pltpu.CompilerParams(vmem_limit_bytes=mebibytes << 20)

BLOCK = 256
LANES = 128
STEPS = (8, 12, 16, 32)
HALF = jnp.bfloat16


def split_two(value):
    high = value.astype(HALF)
    return high, (value - high.astype(jnp.float32)).astype(HALF)


def dot_nt(a, b):
    return lax.dot_general(a, b, (((1,), (1,)), ((), ())), preferred_element_type=jnp.float32)


def dot_nn(a, b):
    return jnp.dot(a, b, preferred_element_type=jnp.float32)


def iota(shape, dim):
    return lax.broadcasted_iota(jnp.int32, shape, dim)


def row_of(ref, j):
    pair = ref[pl.ds(2 * j, 2), :]
    return jnp.concatenate([pair[0:1], pair[1:2]], 1)


def rank_kernel(tiles, levels, capacity, count_ref, ints_ref, target_ref, carry, total):
    size = target_ref.shape[0]
    owner_ref, level_ref = [ints_ref.at[pl.ds(i * size, size)] for i in range(2)]
    blocks = size * LANES // BLOCK
    keys = tiles * levels
    count = count_ref[0]

    def onehot(j):
        live = iota((1, BLOCK), 1) + j * BLOCK < count
        key = jnp.where(live, row_of(owner_ref, j) * levels + row_of(level_ref, j), -1)
        return live, iota((keys, BLOCK), 0) == key

    ones = jnp.ones((BLOCK, LANES), HALF)
    total[...] = jnp.zeros_like(total)

    many = math.gcd(blocks, 8)

    def count_group(g, unused):
        masks = [onehot(g * many + i)[1] for i in range(many)]
        counted = jnp.concatenate([jnp.where(mask, 1.0, 0.0).astype(HALF) for mask in masks], 1)
        total[...] += dot_nn(counted, jnp.concatenate([ones] * many, 0))
        return unused

    lax.fori_loop(0, blocks // many, count_group, 0)
    high = jnp.floor(total[...] * (1.0 / LANES))
    low = total[...] - high * LANES
    row_key, col_key = iota((keys, keys), 0), iota((keys, keys), 1)
    before = jnp.where((col_key < row_key) & (col_key // levels == row_key // levels), 1.0, 0.0).astype(HALF)
    start = dot_nn(before, high.astype(HALF)) * LANES + dot_nn(before, low.astype(HALF))
    carry[...] = start + ((iota((keys, LANES), 0) // levels) * capacity).astype(jnp.float32)

    earlier = jnp.where(iota((BLOCK, BLOCK), 0) < iota((BLOCK, BLOCK), 1), 1.0, 0.0).astype(HALF)
    prefix = jnp.concatenate([earlier, ones], 1)

    def rank_group(g, unused):
        now = carry[...]
        seen = [onehot(g * many + i) for i in range(many)]
        ranks = [dot_nn(jnp.where(mask, 1.0, 0.0).astype(HALF), prefix) for live, mask in seen]
        for i, ((live, mask), rank) in enumerate(zip(seen, ranks)):
            here = rank[:, :BLOCK] + jnp.concatenate([now] * (BLOCK // LANES), 1)
            now = now + rank[:, BLOCK:]
            slot = jnp.sum(jnp.where(mask, here, 0.0), 0, keepdims=True)
            target = jnp.where(live, slot.astype(jnp.int32), -1)
            target_ref[pl.ds(2 * (g * many + i), 2), :] = jnp.concatenate([target[:, :LANES], target[:, LANES:]], 0)
        carry[...] = now
        return unused

    lax.fori_loop(0, blocks // many, rank_group, 0)


def ranked(tiles, levels, capacity, count, ints):
    return pl.pallas_call(
        functools.partial(rank_kernel, tiles, levels, capacity),
        out_shape=jax.ShapeDtypeStruct((ints.shape[0] // 3, LANES), jnp.int32),
        in_specs=[SMEM, VMEM],
        out_specs=VMEM,
        scratch_shapes=[
            pltpu.VMEM((tiles * levels, LANES), jnp.float32),
            pltpu.VMEM((tiles * levels, LANES), jnp.float32),
        ],
        compiler_params=room(16),
        cost_estimate=pl.CostEstimate(flops=1 << 20, bytes_accessed=1 << 17, transcendentals=0),
        name="rank",
    )(count, ints)


def pack_kernel(tiles, plane, capacity, target_ref, ints_ref, floats_ref, frac_ref, out_ref, *scratch):
    gathered, left_a, right_a, left_b, right_b = scratch
    size = target_ref.shape[0]
    level_ref, column_ref = [ints_ref.at[pl.ds(i * size, size)] for i in (1, 2)]
    innov_ref, rinv_ref = [floats_ref.at[pl.ds(i * size, size)] for i in range(2)]
    blocks = size * LANES // BLOCK
    deep = capacity // BLOCK
    slot_rows = tiles * deep
    group = 4
    gathered[...] = jnp.zeros_like(gathered)

    def place(j):
        target = row_of(target_ref, j)
        rows = jnp.where(iota((slot_rows, BLOCK), 0) == (target >> 8), 1.0, 0.0).astype(HALF)
        lanes = jnp.where(iota((BLOCK, BLOCK), 0) == (target & (BLOCK - 1)), 1.0, 0.0).astype(HALF)
        column = row_of(column_ref, j)
        frac = frac_ref[:, pl.ds(pl.multiple_of(j * BLOCK, BLOCK), BLOCK)]
        terms = []
        for value in (frac[0:1], frac[1:2], frac[2:3], row_of(innov_ref, j), row_of(rinv_ref, j)):
            terms.extend(split_two(jnp.broadcast_to(value, (16, BLOCK))))
        for value in (row_of(level_ref, j), column >> 7, column & (LANES - 1)):
            terms.append(jnp.broadcast_to(value.astype(jnp.float32), (16, BLOCK)).astype(HALF))
        spread = [rows * jnp.concatenate([term] * (slot_rows // 16), 0) for term in terms]
        return jnp.concatenate(spread, 0), lanes

    def build(g, left, right):
        for i in range(group):
            lanes = slice(i * BLOCK, (i + 1) * BLOCK)
            left[:, lanes], right[:, lanes] = place(g * group + i)

    def multiply(left, right):
        gathered[...] += dot_nt(left[...], right[...])

    def scatter_pair(g, unused):
        build(2 * g + 1, left_b, right_b)
        multiply(left_a, right_a)
        build(jnp.minimum(2 * g + 2, blocks // group - 1), left_a, right_a)
        multiply(left_b, right_b)
        return unused

    build(0, left_a, right_a)
    lax.fori_loop(0, blocks // (2 * group), scatter_pair, 0)

    def part(index, tile):
        begin = index * slot_rows + tile * deep
        return gathered[begin:begin + deep, :]

    for tile in range(tiles):
        for p in range(5):
            out_ref[tile, p * deep:(p + 1) * deep, :] = part(2 * p, tile) + part(2 * p + 1, tile)
        base = part(10, tile) * plane + part(11, tile) * LANES + part(12, tile)
        out_ref[tile, 5 * deep:6 * deep, :] = base


def pack(tiles, plane, capacity, target, ints, floats, frac):
    deep = capacity // BLOCK
    rows = 13 * tiles * deep
    return pl.pallas_call(
        functools.partial(pack_kernel, tiles, plane, capacity),
        out_shape=jax.ShapeDtypeStruct((tiles, 6 * deep, BLOCK), jnp.float32),
        in_specs=[VMEM] * 4,
        out_specs=VMEM,
        scratch_shapes=[pltpu.VMEM((rows, BLOCK), jnp.float32)]
        + [pltpu.VMEM((count, 4 * BLOCK), HALF) for count in (rows, BLOCK) * 2],
        compiler_params=room(16),
        cost_estimate=pl.CostEstimate(flops=8 << 30, bytes_accessed=1 << 20, transcendentals=0),
        name="pack",
    )(target, ints, floats, frac)


def stencil_kernel(
    me_ref, parts_refs, sigma_ref, static_ref, incoming_ref,
    dep_ref, adj_refs,
    field, field_t, adjoint, spans, spans_ref, sem,
):
    levels, fine_x, fine_y = sigma_ref.shape
    sources, packed_rows, block = incoming_ref.shape
    deep = packed_rows // 6
    plane = fine_x * fine_y
    chunk = LANES // fine_x
    groups = len(parts_refs)
    share = levels // groups
    rows = levels * fine_x
    me = me_ref[0]
    halves = block // LANES
    column = iota((sources * deep, LANES), 1)
    found = jnp.zeros((sources * deep, LANES), jnp.int32)
    for half in range(halves):
        lanes = slice(half * LANES, (half + 1) * LANES)
        used = incoming_ref[:, 4 * deep:5 * deep, lanes].reshape(sources * deep, LANES) > 0.0
        level = jnp.floor(incoming_ref[:, 5 * deep:, lanes].reshape(sources * deep, LANES) * (1.0 / plane))
        lowest = jnp.min(jnp.where(used, level, float(levels)), 1, keepdims=True).astype(jnp.int32)
        highest = jnp.max(jnp.where(used, level, -1.0), 1, keepdims=True).astype(jnp.int32)
        found = jnp.where((column == 2 * half) & (highest >= 0), lowest, found)
        found = jnp.where((column == 2 * half + 1) & (highest >= 0), highest + 2 - lowest, found)
    spans[...] = found
    fetch = pltpu.make_async_copy(spans, spans_ref, sem)
    fetch.start()
    adjoint[...] = jnp.zeros_like(adjoint)
    dep_ref[...] = jnp.zeros_like(dep_ref)
    field[rows:, :] = jnp.zeros((field.shape[0] - rows, fine_y), jnp.float32)
    for slot, part in enumerate(parts_refs):
        start = lax.rem(me + groups - slot, groups) * share
        static = sigma_ref[pl.ds(start, share)] * static_ref[pl.ds(start, share)]
        where = pl.ds(pl.multiple_of(start * fine_x, LANES), share * fine_x)
        field[where, :] = (part[...] + static).reshape(share * fine_x, fine_y)
    for shift in range(chunk):
        field_t[shift, :, rows:] = jnp.zeros((2 * fine_y, field_t.shape[2] - rows), HALF)
    after = jnp.zeros((fine_y, LANES), jnp.float32)
    lane = iota((fine_y, LANES), 1)
    for g in reversed(range(rows // LANES)):
        now = field[g * LANES:(g + 1) * LANES, :].T
        for shift in range(chunk):
            value, move = now, LANES - shift * fine_x
            if shift:
                value = jnp.where(lane < move, pltpu.roll(now, move, 1), pltpu.roll(after, move, 1))
            high, low = split_two(value)
            field_t[shift, :fine_y, g * LANES:(g + 1) * LANES] = high
            field_t[shift, fine_y:, g * LANES:(g + 1) * LANES] = low
        after = now

    fetch.wait()

    def block_of(source, at, half):
        def row(p):
            return incoming_ref[source, pl.ds(p * deep + at, 1), :][:, half * LANES:(half + 1) * LANES]

        base = row(5)
        level = jnp.floor(base * (1.0 / plane))
        rest = base - level * plane
        across = jnp.floor(rest * (1.0 / fine_y))
        along = rest - across * fine_y
        frac_x, frac_y, frac_l = row(0), row(1), row(2)
        rows_x = iota((fine_x, LANES), 0).astype(jnp.float32)
        pick_x = jnp.where(rows_x == across, 1.0 - frac_x, 0.0) + jnp.where(rows_x == across + 1.0, frac_x, 0.0)
        rows_y = iota((fine_y, LANES), 0).astype(jnp.float32)
        pick_y = jnp.where(rows_y == along, 1.0 - frac_y, 0.0) + jnp.where(rows_y == along + 1.0, frac_y, 0.0)

        def weights(bottom, reach):
            offset = level - jnp.asarray(bottom, jnp.int32).astype(jnp.float32)
            rows_l = iota((reach, LANES), 0).astype(jnp.float32)
            pick_l = jnp.where(rows_l == offset, 1.0 - frac_l, 0.0) + jnp.where(rows_l == offset + 1.0, frac_l, 0.0)
            picks = [pick_x * pick_l[g:g + 1] for g in range(reach)]
            return jnp.concatenate(split_two(jnp.concatenate(picks, 0)), 1)

        def finish(picked):
            departure = jnp.sum(picked * pick_y, 0, keepdims=True) - row(3)
            turned = jnp.concatenate(split_two((pick_y * (row(4) * departure)).T), 1)
            return departure, jnp.concatenate([turned, turned], 0)

        return weights, finish

    def look(bottom, pick):
        if isinstance(bottom, int):
            seen = dot_nn(field_t[0, :, :pick.shape[0]], pick)
        else:
            lanes = pl.ds(pl.multiple_of((bottom // chunk) * LANES, LANES), pick.shape[0])
            seen = dot_nn(field_t[lax.rem(bottom, chunk), :, lanes], pick)
        return seen[:fine_y, :LANES] + (seen[:fine_y, LANES:] + seen[fine_y:, :LANES])

    def spread(pick, term):
        both = dot_nn(pick, term)
        return both[:, :fine_y] + both[:, fine_y:]

    def rows_at(bottom, reach):
        return pl.ds(pl.multiple_of(bottom * fine_x, fine_x), reach * fine_x)

    def together(blocks, bottoms, reach):
        parts = [block_of(*block) for block in blocks]
        picks = [weights(bottom, reach) for (weights, finish), bottom in zip(parts, bottoms)]
        seen = [look(bottom, pick) for bottom, pick in zip(bottoms, picks)]
        done = [finish(value) for (weights, finish), value in zip(parts, seen)]
        adds = [spread(pick, term) for pick, (departure, term) in zip(picks, done)]
        keep(blocks, [departure for departure, term in done])
        for bottom, add in zip(bottoms, adds):
            adjoint[rows_at(bottom, reach), :] += add

    def keep(blocks, departures):
        for i in range(0, len(blocks), halves):
            source, at, half = blocks[i]
            dep_ref[source, pl.ds(at, 1), :] = jnp.concatenate(departures[i:i + halves], 1)

    step = 2 if deep % 2 == 0 else 1

    def one_step(i, unused):
        source, at = i // (deep // step), lax.rem(i, deep // step) * step
        blocks = [(source, at + r, half) for r in range(step) for half in range(halves)]
        numbers = [(source * deep + at + r, half) for r in range(step) for half in range(halves)]
        bottoms = [spans_ref[row, 2 * half] for row, half in numbers]
        needs = [spans_ref[row, 2 * half + 1] for row, half in numbers]
        most = functools.reduce(jnp.maximum, needs)

        for below, reach in zip((0,) + STEPS, STEPS):
            @pl.when((most > below) & (most <= reach))
            def _():
                together(blocks, [0] * len(blocks) if reach == levels else bottoms, reach)

        return unused

    lax.fori_loop(0, sources * deep // step, one_step, 0)
    for slot, adj_ref in enumerate(adj_refs):
        start = lax.rem(me + slot, groups) * share * fine_x
        adj_ref[...] = adjoint[pl.ds(pl.multiple_of(start, LANES), share * fine_x), :].reshape(share, fine_x, fine_y)


def stencil(parts, incoming, bg_sigma, static_ctrl, me):
    levels, fine_x, fine_y = bg_sigma.shape
    sources, packed_rows, block = incoming.shape
    deep, groups = packed_rows // 6, len(parts)
    rows = levels * fine_x
    padded = rows + STEPS[-2] * fine_x

    def kernel(*refs):
        parts_end = 1 + groups
        stencil_kernel(
            refs[0], refs[1:parts_end], *refs[parts_end:parts_end + 4],
            refs[parts_end + 4:parts_end + 4 + groups], *refs[parts_end + 4 + groups:]
        )

    results = pl.pallas_call(
        kernel,
        out_shape=(jax.ShapeDtypeStruct((sources, deep, block), jnp.float32),)
        + tuple(jax.ShapeDtypeStruct(part.shape, jnp.float32) for part in parts),
        in_specs=[SMEM] + [VMEM] * (groups + 3),
        out_specs=(VMEM,) * (1 + groups),
        scratch_shapes=[
            pltpu.VMEM((padded, fine_y), jnp.float32),
            pltpu.VMEM((LANES // fine_x, 2 * fine_y, padded), HALF),
            pltpu.VMEM((padded, fine_y), jnp.float32),
            pltpu.VMEM((sources * deep, LANES), jnp.int32),
            pltpu.SMEM((sources * deep, LANES), jnp.int32),
            pltpu.SemaphoreType.DMA,
        ],
        compiler_params=room(32),
        cost_estimate=pl.CostEstimate(flops=16 << 30, bytes_accessed=1 << 20, transcendentals=0),
        name="stencil",
    )(me, *parts, bg_sigma, static_ctrl, incoming)
    return results[0], results[1:]


def unpack_kernel(target_ref, table_ref, out_ref):
    slot_rows = table_ref.shape[0]
    high, low = split_two(table_ref[...])
    both = jnp.concatenate([high.astype(jnp.float32), low.astype(jnp.float32)], 0)
    turned = both.T.astype(HALF)
    group = 4

    def some_blocks(g, unused):
        for i in range(group):
            pair = target_ref[pl.ds(2 * (g * group + i), 2), :]
            target = jnp.concatenate([pair[0:1], pair[1:2]], 1)
            rows = jnp.where(iota((slot_rows, BLOCK), 0) == (target >> 8), 1.0, 0.0).astype(HALF)
            lines = dot_nn(turned, jnp.concatenate([rows, rows], 0))
            lane = iota((BLOCK, BLOCK), 0) == (target & (BLOCK - 1))
            found = jnp.sum(jnp.where(lane, lines, 0.0), 0, keepdims=True)
            out_ref[pl.ds(2 * (g * group + i), 2), :] = jnp.concatenate([found[:, :LANES], found[:, LANES:]], 0)
        return unused

    lax.fori_loop(0, target_ref.shape[0] // (2 * group), some_blocks, 0)


def unpack(target, table):
    vmem = pl.BlockSpec(memory_space=pltpu.VMEM)
    return pl.pallas_call(
        unpack_kernel,
        out_shape=jax.ShapeDtypeStruct(target.shape, jnp.float32),
        in_specs=[vmem, vmem],
        out_specs=vmem,
        compiler_params=room(8),
        cost_estimate=pl.CostEstimate(flops=2 << 30, bytes_accessed=1 << 18, transcendentals=0),
        name="unpack",
    )(target, table).reshape(-1)


REACH = NSTEP
EDGE = 8
PAD = 2 * EDGE
SCALE = NU**NSTEP


def interpolation(shape, fine_dim, coarse_dim, shift):
    fine, coarse = iota(shape, fine_dim), iota(shape, coarse_dim) - shift
    frac = (fine % RATIO).astype(jnp.float32) * (1.0 / RATIO)
    low = jnp.where(coarse == fine // RATIO, 1.0 - frac, 0.0)
    return (low + jnp.where(coarse == fine // RATIO + 1, frac, 0.0)).astype(HALF)


def interpolation_rows(fine_x, depth, copies, transposed):
    long, short = EDGE * fine_x, EDGE * depth
    shape = (short, long) if transposed else (long, copies * short)
    fine, coarse = iota(shape, 1 if transposed else 0), iota(shape, 0 if transposed else 1)
    for copy in range(1, copies):
        coarse = jnp.where(coarse >= short, coarse - short, coarse)
    place, target = fine % fine_x, coarse // EDGE
    frac = (place % RATIO).astype(jnp.float32) * (1.0 / RATIO)
    low = jnp.where(target == place // RATIO, 1.0 - frac, 0.0)
    weight = low + jnp.where(target == place // RATIO + 1, frac, 0.0)
    return jnp.where(fine // fine_x == coarse % EDGE, weight, 0.0).astype(HALF)


def mixing(mix_ref):
    levels = mix_ref.shape[0]
    tile = jnp.where(iota((LANES, levels), 0) % levels == iota((LANES, levels), 1), 1.0, 0.0).astype(HALF)
    same = iota((LANES, LANES), 0) // levels == iota((LANES, LANES), 1) // levels
    terms = []
    for term in split_two(mix_ref[...]):
        tiled = dot_nt(dot_nn(tile, term).astype(HALF), tile)
        terms.append(jnp.where(same, tiled, 0.0).astype(HALF))
    return terms


def corner_counts(coarse_x, joined):
    above = [[j, j + 1] for j in range(REACH)]
    below = [[REACH - i, REACH + 1 - i] for i in range(REACH + 1)]
    if not joined:
        return [above, below]
    gap = [[0, 0]] * (coarse_x - REACH)
    high, low = gap + above, below + gap[1:]
    return [[[max(a, b) for a, b in zip(*pair)] for pair in zip(high, low)]]


def neighbours(field):
    width = field.shape[1]
    return pltpu.roll(field, 1, 1) + pltpu.roll(field, width - 1, 1)


def edges_kernel(strips, rows, alpha_ref, mix_ref, alpha_out, mix_out, *outs):
    coarse_y = alpha_ref.shape[1]
    alpha_out[...] = alpha_ref[...]
    mix_out[...] = mix_ref[...]
    for (begin, counts), left, right in zip(zip(rows, strips), outs[:len(strips)], outs[len(strips):]):
        at_left, at_right = 0, 0
        for i, (to_left, to_right) in enumerate(counts):
            if to_left:
                left[at_left:at_left + to_left, :] = alpha_ref[begin + i, coarse_y - to_left:, :]
            if to_right:
                right[at_right:at_right + to_right, :] = alpha_ref[begin + i, :to_right, :]
            at_left, at_right = at_left + to_left, at_right + to_right


def ensemble_kernel(
    coarse_x, coarse_y, offsets, strips,
    me_ref, alpha_ref, above_ref, below_ref,
    left_ref, left_above_ref, left_below_ref, right_ref, right_above_ref, right_below_ref,
    mix_ref, pert_hbm, out_refs, pert_ref, sem, ext, coarse,
):
    members, levels, fine_x, fine_y = pert_ref.shape
    channels = alpha_ref.shape[2]
    fetch = pltpu.make_async_copy(pert_hbm, pert_ref, sem)
    fetch.start()
    ext[:, :EDGE, :] = jnp.zeros((ext.shape[0], EDGE, channels), jnp.float32)
    ext[:, EDGE + coarse_y:, :] = jnp.zeros((ext.shape[0], EDGE, channels), jnp.float32)
    above, below = offsets
    groups = (
        (0, REACH, above, strips[1], above_ref, left_above_ref, right_above_ref),
        (REACH, coarse_x, 0, strips[0], alpha_ref, left_ref, right_ref),
        (REACH + coarse_x, REACH + 1, below, strips[-1], below_ref, left_below_ref, right_below_ref),
    )
    for begin, count, offset, counts, middle, left, right in groups:
        ext[begin:begin + count, EDGE:EDGE + coarse_y, :] = middle[offset:offset + count]
        for i in range(count):
            at_left, at_right = [sum(row[side] for row in counts[:offset + i]) for side in range(2)]
            n_left, n_right = counts[offset + i]
            if n_left:
                ext[begin + i, EDGE - n_left:EDGE, :] = left[at_left:at_left + n_left, :]
            if n_right:
                ext[begin + i, EDGE + coarse_y:EDGE + coarse_y + n_right, :] = right[at_right:at_right + n_right, :]
    spread_y = interpolation((coarse_y + PAD, fine_y), 1, 0, EDGE)
    spread_y = jnp.concatenate([spread_y, spread_y], 0)
    high, low = mixing(mix_ref)
    mix = jnp.concatenate([high, high, low], 1)

    def one_group(g, unused):
        lanes = pl.ds(pl.multiple_of(g * LANES, LANES), LANES)
        field = ext[:, :, lanes]
        for step in range(NSTEP):
            inner = field[1:-1]
            field = inner + field[2:] + field[:-2] + neighbours(inner)
        high, low = split_two(field * SCALE)
        both = jnp.concatenate([high.astype(jnp.float32), low.astype(jnp.float32)], 1)
        for c in range(coarse_x + 1):
            wide_high, wide_low = split_two(dot_nn(both[c].T.astype(HALF), spread_y))
            coarse[c, lanes, :] = dot_nn(mix, jnp.concatenate([wide_high, wide_low, wide_high], 0))
        return unused

    lax.fori_loop(0, channels // LANES, one_group, 0, unroll=True)
    fetch.wait()
    depth = coarse_x + 2
    spread_x = interpolation_rows(fine_x, depth, 2, False)
    share = levels // len(out_refs)
    unroll = math.gcd(members // 2, 5)

    for slot, out_ref in enumerate(out_refs):
        for sub in range(share // EDGE):
            first = pl.multiple_of(lax.rem(me_ref[0] + slot, len(out_refs)) * share + sub * EDGE, EDGE)

            def stacked(k):
                rows = pl.ds(pl.multiple_of(k * levels + first, EDGE), EDGE)
                parts = [coarse[c, rows, :] for c in range(coarse_x + 1)]
                return jnp.concatenate(parts + [jnp.zeros((EDGE, fine_y), jnp.float32)], 0)

            def perturbation(k):
                return pert_ref[k, pl.ds(first, EDGE)].reshape(EDGE * fine_x, fine_y).astype(jnp.float32)

            def pairs(p, total):
                for i in range(unroll):
                    k = 2 * (unroll * p + i)
                    high, low = split_two(jnp.concatenate([stacked(k), stacked(k + 1)], 1))
                    fine = dot_nn(spread_x, jnp.concatenate([high, low], 0))
                    total = total + (fine[:, :fine_y] * perturbation(k) + fine[:, fine_y:] * perturbation(k + 1))
                return total

            total = lax.fori_loop(
                0, members // (2 * unroll), pairs, jnp.zeros((EDGE * fine_x, fine_y), jnp.float32)
            )
            out_ref[sub * EDGE:(sub + 1) * EDGE] = total.reshape(EDGE, fine_x, fine_y)


def backward_kernel(
    coarse_x, coarse_y, joined, strips,
    me_ref, parts_refs, mix_ref, sigma_ref, static_ref, pert_hbm,
    grad_ref, center_ref, middle_refs, left_refs, right_refs,
    adjoint, coarse, pert_ref, sems,
):
    members, levels, fine_x, fine_y = pert_ref.shape
    channels = members * levels
    unroll = members // sems.shape[0]
    copies = []
    for p in range(sems.shape[0]):
        some = pl.ds(p * unroll, unroll)
        copies.append(pltpu.make_async_copy(pert_hbm.at[some], pert_ref.at[some], sems.at[p]))
        copies[p].start()
    share = levels // len(parts_refs)
    for slot, part in enumerate(parts_refs):
        first = lax.rem(me_ref[0] + len(parts_refs) - slot, len(parts_refs)) * share
        adjoint[pl.ds(first, share)] = part[...]
    grad_ref[...] = static_ref[...] + sigma_ref[...] * adjoint[...]
    depth = coarse_x + 2
    fold_x = interpolation_rows(fine_x, depth, 1, True)

    for p, copy in enumerate(copies):
        copy.wait()

        def one_level_group(group, unused):
            some = pl.ds(group * EDGE, EDGE)
            field = adjoint[some].reshape(EDGE * fine_x, fine_y)
            for k in range(p * unroll, (p + 1) * unroll):
                scaled = pert_ref[k, some].reshape(EDGE * fine_x, fine_y).astype(jnp.float32)
                high, low = split_two(scaled * field)
                both = dot_nn(fold_x, jnp.concatenate([high, low], 1))
                rows = pl.ds(pl.multiple_of(k * levels + group * EDGE, EDGE), EDGE)
                for c in range(coarse_x + 1):
                    piece = both[c * EDGE:(c + 1) * EDGE]
                    coarse[c, rows, :] = piece[:, :fine_y] + piece[:, fine_y:]
            return unused

        lax.fori_loop(0, levels // EDGE, one_level_group, 0)

    fold_y = interpolation((coarse_y + PAD, fine_y), 1, 0, EDGE)
    fold_y = jnp.concatenate([fold_y, fold_y], 1)
    high, low = mixing(mix_ref)
    mix = jnp.concatenate([high, high, low], 0)

    def one_group(g, unused):
        lanes = pl.ds(pl.multiple_of(g * LANES, LANES), LANES)
        rows = []
        for c in range(coarse_x + 1):
            high, low = split_two(coarse[c, lanes, :])
            narrow = dot_nt(fold_y, jnp.concatenate([high, low], 1))
            high, low = split_two(narrow)
            rows.append(dot_nn(jnp.concatenate([high, low, high], 1), mix)[None])
        field = jnp.concatenate(rows, 0) * SCALE
        empty = jnp.zeros((1,) + field.shape[1:], jnp.float32)
        for step in range(NSTEP):
            own = field + neighbours(field)
            field = jnp.concatenate([field, empty, empty], 0) + jnp.concatenate([empty, own, empty], 0) + jnp.concatenate(
                [empty, empty, field], 0
            )
        inside = field[REACH:REACH + coarse_x]
        up, down = field[:REACH], field[REACH + coarse_x:]
        if joined:
            none = jnp.zeros((coarse_x - REACH - 1,) + field.shape[1:], jnp.float32)
            outside = [jnp.concatenate([down, none], 0) + jnp.concatenate([none, empty, up], 0)]
        else:
            outside = [up, down]
        center_ref[:, :, lanes] = inside[:, EDGE:EDGE + coarse_y]
        for ref, value in zip(middle_refs, outside):
            ref[:, :, lanes] = value[:, EDGE:EDGE + coarse_y]
        for left, right, value, counts in zip(left_refs, right_refs, [inside] + outside, strips):
            at_left, at_right = 0, 0
            for i, (to_left, to_right) in enumerate(counts):
                if to_left:
                    left[at_left:at_left + to_left, lanes] = value[i, EDGE - to_left:EDGE]
                if to_right:
                    right[at_right:at_right + to_right, lanes] = value[i, EDGE + coarse_y:EDGE + coarse_y + to_right]
                at_left, at_right = at_left + to_left, at_right + to_right
        return unused

    lax.fori_loop(0, channels // LANES, one_group, 0, unroll=True)


def fold_kernel(places, alpha_ref, center_ref, *refs):
    part_refs, out_ref = refs[:-1], refs[-1]
    coarse_y = out_ref.shape[1]
    out_ref[...] = alpha_ref[...] + center_ref[...]
    for (row, counts, at_end), ref in zip(places, part_refs):
        if at_end is None:
            out_ref[row:row + counts] += ref[...]
            continue
        at = 0
        for i, count in enumerate(counts):
            if count:
                begin = coarse_y - count if at_end else 0
                out_ref[row + i, begin:begin + count, :] += ref[at:at + count, :]
            at += count


def shifted(value, by_x, by_y):
    count_x, count_y = lax.axis_size("tx"), lax.axis_size("ty")
    pairs = [
        (x * count_y + y, (x + by_x) % count_x * count_y + (y + by_y) % count_y)
        for x in range(count_x)
        for y in range(count_y)
    ]
    return lax.ppermute(value, ("tx", "ty"), pairs)


def ensemble(alpha, mix, ens_pert, me, beside):
    coarse_x, coarse_y, channels = alpha.shape
    members, levels, fine_x, fine_y = ens_pert.shape
    joined = lax.axis_size("tx") == 2
    strips = [[[REACH, REACH + 1]] * coarse_x] + corner_counts(coarse_x, joined)
    rows = [0, 0] if joined else [0, coarse_x - REACH, 0]
    shapes = [alpha.shape, mix.shape]
    shapes += [(sum(count[side] for count in counts), channels) for side in range(2) for counts in strips]
    held, mix, *sides = pl.pallas_call(
        functools.partial(edges_kernel, strips, rows),
        out_shape=tuple(jax.ShapeDtypeStruct(shape, jnp.float32) for shape in shapes),
        in_specs=[VMEM] * 2,
        out_specs=(VMEM,) * len(shapes),
        compiler_params=room(8),
        cost_estimate=pl.CostEstimate(flops=1 << 10, bytes_accessed=1 << 10, transcendentals=0),
        name="edges",
    )(alpha, mix)
    ends, starts = sides[:len(strips)], sides[len(strips):]
    if joined:
        above = below = shifted(alpha, 1, 0)
        left_above = left_below = shifted(ends[1], 1, 1)
        right_above = right_below = shifted(starts[1], 1, -1)
        offsets = (coarse_x - REACH, 0)
    else:
        above, below = shifted(alpha[coarse_x - REACH:], 1, 0), shifted(alpha[:REACH + 1], -1, 0)
        left_above, left_below = shifted(ends[1], 1, 1), shifted(ends[2], -1, 1)
        right_above, right_below = shifted(starts[1], 1, -1), shifted(starts[2], -1, -1)
        offsets = (0, 0)
    left, right = shifted(ends[0], 0, 1), shifted(starts[0], 0, -1)
    left, beside = lax.optimization_barrier((left, beside))
    groups = lax.axis_size("mem")

    def kernel(*refs):
        ensemble_kernel(coarse_x, coarse_y, offsets, strips, *refs[:12], refs[12:12 + groups], *refs[12 + groups:])

    parts = pl.pallas_call(
        kernel,
        out_shape=tuple(jax.ShapeDtypeStruct((levels // groups, fine_x, fine_y), jnp.float32) for _ in range(groups)),
        in_specs=[SMEM] + [VMEM] * 10 + [HBM],
        out_specs=(VMEM,) * groups,
        scratch_shapes=[
            pltpu.VMEM(ens_pert.shape, ens_pert.dtype),
            pltpu.SemaphoreType.DMA,
            pltpu.VMEM((coarse_x + 2 * REACH + 1, coarse_y + PAD, channels), jnp.float32),
            pltpu.VMEM((coarse_x + 1, channels, fine_y), jnp.float32),
        ],
        compiler_params=room(50),
        cost_estimate=pl.CostEstimate(flops=8 << 30, bytes_accessed=8 << 20, transcendentals=0),
        name="ensemble",
    )(me, held, above, below, left, left_above, left_below, right, right_above, right_below, mix, ens_pert)
    return parts, beside


def backward(alpha, adjoint_parts, mix, bg_sigma, static_ctrl, ens_pert, me, beside):
    coarse_x, coarse_y, channels = alpha.shape
    members, levels, fine_x, fine_y = ens_pert.shape
    joined = lax.axis_size("tx") == 2
    groups = len(adjoint_parts)
    outside = [coarse_x] if joined else [REACH, REACH + 1]
    strips = [[[REACH, REACH + 1]] * coarse_x] + corner_counts(coarse_x, joined)
    shapes = [bg_sigma.shape, alpha.shape]
    shapes += [(rows, coarse_y, channels) for rows in outside]
    shapes += [(sum(count[side] for count in counts), channels) for side in range(2) for counts in strips]
    n_in, n_mid, n_strip = 5 + groups, len(outside), len(strips)

    def kernel(*refs):
        me_ref, parts, rest = refs[0], refs[1:1 + groups], refs[1 + groups:n_in]
        outs = refs[n_in:n_in + len(shapes)]
        middle = outs[2:2 + n_mid]
        left = outs[2 + n_mid:2 + n_mid + n_strip]
        right = outs[2 + n_mid + n_strip:]
        backward_kernel(
            coarse_x, coarse_y, joined, strips, me_ref, parts, *rest,
            outs[0], outs[1], middle, left, right, *refs[n_in + len(shapes):]
        )

    results = pl.pallas_call(
        kernel,
        out_shape=tuple(jax.ShapeDtypeStruct(shape, jnp.float32) for shape in shapes),
        in_specs=[SMEM] + [VMEM] * (groups + 3) + [HBM],
        out_specs=(VMEM,) * len(shapes),
        scratch_shapes=[
            pltpu.VMEM(bg_sigma.shape, jnp.float32),
            pltpu.VMEM((coarse_x + 1, channels, fine_y), jnp.float32),
            pltpu.VMEM(ens_pert.shape, ens_pert.dtype),
            pltpu.SemaphoreType.DMA((members // math.gcd(members, 5),)),
        ],
        compiler_params=room(50),
        cost_estimate=pl.CostEstimate(flops=8 << 30, bytes_accessed=8 << 20, transcendentals=0),
        name="backward",
    )(me, *adjoint_parts, mix, bg_sigma, static_ctrl, ens_pert)
    results, beside = lax.optimization_barrier((results, beside))
    grad_static, center = results[:2]
    middle = results[2:2 + n_mid]
    left, right = results[2 + n_mid:2 + n_mid + n_strip], results[2 + n_mid + n_strip:]
    moves = [(1, 0)] if joined else [(-1, coarse_x - REACH), (1, 0)]
    places, parts = [], []
    for (by, row), value in zip(moves, middle):
        parts.append(shifted(value, by, 0))
        places.append((row, value.shape[0], None))
    for (by, row), counts, to_left, to_right in zip([(0, 0)] + moves, strips, left, right):
        parts += [shifted(to_left, by, -1), shifted(to_right, by, 1)]
        places += [(row, [count[0] for count in counts], True), (row, [count[1] for count in counts], False)]
    grad_alpha = pl.pallas_call(
        functools.partial(fold_kernel, places),
        out_shape=jax.ShapeDtypeStruct(alpha.shape, jnp.float32),
        in_specs=[VMEM] * (2 + len(parts)),
        out_specs=VMEM,
        compiler_params=room(8),
        cost_estimate=pl.CostEstimate(flops=1 << 20, bytes_accessed=2 << 20, transcendentals=0),
        name="fold",
    )(alpha, center, *parts)
    return grad_alpha, grad_static, beside


def owned_sum(parts):
    count = len(parts)
    total = parts[0]
    for d in range(1, count):
        total = total + lax.ppermute(parts[d], "mem", [(i, (i + d) % count) for i in range(count)])
    return total


def gathered(own):
    count = lax.axis_size("mem")
    return [own] + [lax.ppermute(own, "mem", [(i, (i + d) % count) for i in range(count)]) for d in range(1, count)]


def per_device(
    alpha,
    lv_sqrt,
    ens_pert,
    bg_sigma,
    static_ctrl,
    obs_owner,
    obs_column,
    obs_level,
    obs_frac,
    innovation,
    obs_rinv,
    obs_count,
):
    levels, fine_x, fine_y = bg_sigma.shape
    tiles = lax.axis_size("tx") * lax.axis_size("ty")
    capacity = 2 * obs_owner.shape[0] // tiles
    me = lax.axis_index("mem").astype(jnp.int32).reshape(1)
    rows = obs_owner.shape[0] // LANES
    ints = jnp.concatenate([obs_owner[:, 0], obs_level, obs_column]).reshape(3 * rows, LANES)
    floats = jnp.concatenate([innovation, obs_rinv]).reshape(2 * rows, LANES)
    target = ranked(tiles, levels, capacity, obs_count, ints)
    partial, target = ensemble(alpha, lv_sqrt, ens_pert, me, target)
    partial, target = lax.optimization_barrier((partial, target))
    outgoing = pack(tiles, fine_x * fine_y, capacity, target, ints, floats, obs_frac)
    incoming = lax.all_to_all(outgoing, ("tx", "ty"), split_axis=0, concat_axis=0, tiled=True)
    increment = owned_sum(partial)
    departure, adjoint = stencil(gathered(increment), incoming, bg_sigma, static_ctrl, me)
    parts, departure = lax.optimization_barrier((gathered(owned_sum(adjoint)), departure))
    returned = lax.all_to_all(departure, ("tx", "ty"), split_axis=0, concat_axis=0, tiled=True)
    grad_alpha, grad_static, returned = backward(
        alpha, parts, lv_sqrt, bg_sigma, static_ctrl, ens_pert, me, returned
    )
    departures = unpack(target, returned.reshape(-1, BLOCK))
    return (grad_alpha, grad_static, departures)


def solution(mesh):
    placed = (
        P("tx", "ty", "mem"),
        P(),
        P("mem", None, "tx", "ty"),
        P(None, "tx", "ty"),
        P(None, "tx", "ty"),
        P(("tx", "ty", "mem"), None),
        P(("tx", "ty", "mem")),
        P(("tx", "ty", "mem")),
        P(None, ("tx", "ty", "mem")),
        P(("tx", "ty", "mem")),
        P(("tx", "ty", "mem")),
        P(("tx", "ty", "mem")),
    )
    return jax.shard_map(
        per_device,
        mesh=mesh,
        in_specs=placed,
        out_specs=(P("tx", "ty", "mem"), P(None, "tx", "ty"), P(("tx", "ty", "mem"))),
        check_vma=False,
    )
```

```python
import functools
import math

import jax
import jax.numpy as jnp
from jax import lax
from jax.experimental import pallas as pl
from jax.experimental.pallas import tpu as pltpu
from jax.sharding import PartitionSpec as P

RATIO = 4
NSTEP = 4
NU = 0.2
VMEM = pl.BlockSpec(memory_space=pltpu.VMEM)
SMEM = pl.BlockSpec(memory_space=pltpu.SMEM)
HBM = pl.BlockSpec(memory_space=pltpu.HBM)


def room(mebibytes):
    return pltpu.CompilerParams(vmem_limit_bytes=mebibytes << 20)

BLOCK = 256
LANES = 128
STEPS = (8, 12, 16, 32)
HALF = jnp.bfloat16


def split_two(value):
    high = value.astype(HALF)
    return high, (value - high.astype(jnp.float32)).astype(HALF)


def dot_nt(a, b):
    return lax.dot_general(a, b, (((1,), (1,)), ((), ())), preferred_element_type=jnp.float32)


def dot_nn(a, b):
    return jnp.dot(a, b, preferred_element_type=jnp.float32)


def iota(shape, dim):
    return lax.broadcasted_iota(jnp.int32, shape, dim)


def row_of(ref, j):
    pair = ref[pl.ds(2 * j, 2), :]
    return jnp.concatenate([pair[0:1], pair[1:2]], 1)


def rank_kernel(tiles, levels, capacity, count_ref, ints_ref, target_ref, carry, total):
    size = target_ref.shape[0]
    owner_ref, level_ref = [ints_ref.at[pl.ds(i * size, size)] for i in range(2)]
    blocks = size * LANES // BLOCK
    keys = tiles * levels
    count = count_ref[0]

    def onehot(j):
        live = iota((1, BLOCK), 1) + j * BLOCK < count
        key = jnp.where(live, row_of(owner_ref, j) * levels + row_of(level_ref, j), -1)
        return live, iota((keys, BLOCK), 0) == key

    ones = jnp.ones((BLOCK, LANES), HALF)
    total[...] = jnp.zeros_like(total)

    many = math.gcd(blocks, 8)

    def count_group(g, unused):
        masks = [onehot(g * many + i)[1] for i in range(many)]
        counted = jnp.concatenate([jnp.where(mask, 1.0, 0.0).astype(HALF) for mask in masks], 1)
        total[...] += dot_nn(counted, jnp.concatenate([ones] * many, 0))
        return unused

    lax.fori_loop(0, blocks // many, count_group, 0)
    high = jnp.floor(total[...] * (1.0 / LANES))
    low = total[...] - high * LANES
    row_key, col_key = iota((keys, keys), 0), iota((keys, keys), 1)
    before = jnp.where((col_key < row_key) & (col_key // levels == row_key // levels), 1.0, 0.0).astype(HALF)
    start = dot_nn(before, high.astype(HALF)) * LANES + dot_nn(before, low.astype(HALF))
    carry[...] = start + ((iota((keys, LANES), 0) // levels) * capacity).astype(jnp.float32)

    earlier = jnp.where(iota((BLOCK, BLOCK), 0) < iota((BLOCK, BLOCK), 1), 1.0, 0.0).astype(HALF)
    prefix = jnp.concatenate([earlier, ones], 1)

    def rank_group(g, unused):
        now = carry[...]
        seen = [onehot(g * many + i) for i in range(many)]
        ranks = [dot_nn(jnp.where(mask, 1.0, 0.0).astype(HALF), prefix) for live, mask in seen]
        for i, ((live, mask), rank) in enumerate(zip(seen, ranks)):
            here = rank[:, :BLOCK] + jnp.concatenate([now] * (BLOCK // LANES), 1)
            now = now + rank[:, BLOCK:]
            slot = jnp.sum(jnp.where(mask, here, 0.0), 0, keepdims=True)
            target = jnp.where(live, slot.astype(jnp.int32), -1)
            target_ref[pl.ds(2 * (g * many + i), 2), :] = jnp.concatenate([target[:, :LANES], target[:, LANES:]], 0)
        carry[...] = now
        return unused

    lax.fori_loop(0, blocks // many, rank_group, 0)


def ranked(tiles, levels, capacity, count, ints):
    return pl.pallas_call(
        functools.partial(rank_kernel, tiles, levels, capacity),
        out_shape=jax.ShapeDtypeStruct((ints.shape[0] // 3, LANES), jnp.int32),
        in_specs=[SMEM, VMEM],
        out_specs=VMEM,
        scratch_shapes=[
            pltpu.VMEM((tiles * levels, LANES), jnp.float32),
            pltpu.VMEM((tiles * levels, LANES), jnp.float32),
        ],
        compiler_params=room(16),
        cost_estimate=pl.CostEstimate(flops=1 << 20, bytes_accessed=1 << 17, transcendentals=0),
        name="rank",
    )(count, ints)


def pack_kernel(tiles, plane, capacity, target_ref, ints_ref, floats_ref, frac_ref, out_ref, *scratch):
    gathered, left_a, right_a, left_b, right_b = scratch
    size = target_ref.shape[0]
    level_ref, column_ref = [ints_ref.at[pl.ds(i * size, size)] for i in (1, 2)]
    innov_ref, rinv_ref = [floats_ref.at[pl.ds(i * size, size)] for i in range(2)]
    blocks = size * LANES // BLOCK
    deep = capacity // BLOCK
    slot_rows = tiles * deep
    group = 4
    gathered[...] = jnp.zeros_like(gathered)

    def place(j):
        target = row_of(target_ref, j)
        rows = jnp.where(iota((slot_rows, BLOCK), 0) == (target >> 8), 1.0, 0.0).astype(HALF)
        lanes = jnp.where(iota((BLOCK, BLOCK), 0) == (target & (BLOCK - 1)), 1.0, 0.0).astype(HALF)
        column = row_of(column_ref, j)
        frac = frac_ref[:, pl.ds(pl.multiple_of(j * BLOCK, BLOCK), BLOCK)]
        terms = []
        for value in (frac[0:1], frac[1:2], frac[2:3], row_of(innov_ref, j), row_of(rinv_ref, j)):
            terms.extend(split_two(jnp.broadcast_to(value, (16, BLOCK))))
        for value in (row_of(level_ref, j), column >> 7, column & (LANES - 1)):
            terms.append(jnp.broadcast_to(value.astype(jnp.float32), (16, BLOCK)).astype(HALF))
        spread = [rows * jnp.concatenate([term] * (slot_rows // 16), 0) for term in terms]
        return jnp.concatenate(spread, 0), lanes

    def build(g, left, right):
        for i in range(group):
            lanes = slice(i * BLOCK, (i + 1) * BLOCK)
            left[:, lanes], right[:, lanes] = place(g * group + i)

    def multiply(left, right):
        gathered[...] += dot_nt(left[...], right[...])

    def scatter_pair(g, unused):
        build(2 * g + 1, left_b, right_b)
        multiply(left_a, right_a)
        build(jnp.minimum(2 * g + 2, blocks // group - 1), left_a, right_a)
        multiply(left_b, right_b)
        return unused

    build(0, left_a, right_a)
    lax.fori_loop(0, blocks // (2 * group), scatter_pair, 0)

    def part(index, tile):
        begin = index * slot_rows + tile * deep
        return gathered[begin:begin + deep, :]

    for tile in range(tiles):
        for p in range(5):
            out_ref[tile, p * deep:(p + 1) * deep, :] = part(2 * p, tile) + part(2 * p + 1, tile)
        base = part(10, tile) * plane + part(11, tile) * LANES + part(12, tile)
        out_ref[tile, 5 * deep:6 * deep, :] = base


def pack(tiles, plane, capacity, target, ints, floats, frac):
    deep = capacity // BLOCK
    rows = 13 * tiles * deep
    return pl.pallas_call(
        functools.partial(pack_kernel, tiles, plane, capacity),
        out_shape=jax.ShapeDtypeStruct((tiles, 6 * deep, BLOCK), jnp.float32),
        in_specs=[VMEM] * 4,
        out_specs=VMEM,
        scratch_shapes=[pltpu.VMEM((rows, BLOCK), jnp.float32)]
        + [pltpu.VMEM((count, 4 * BLOCK), HALF) for count in (rows, BLOCK) * 2],
        compiler_params=room(16),
        cost_estimate=pl.CostEstimate(flops=8 << 30, bytes_accessed=1 << 20, transcendentals=0),
        name="pack",
    )(target, ints, floats, frac)


def stencil_kernel(
    me_ref, parts_refs, sigma_ref, static_ref, incoming_ref,
    dep_ref, adj_refs,
    field, field_t, adjoint, spans, spans_ref, sem,
):
    levels, fine_x, fine_y = sigma_ref.shape
    sources, packed_rows, block = incoming_ref.shape
    deep = packed_rows // 6
    plane = fine_x * fine_y
    chunk = LANES // fine_x
    groups = len(parts_refs)
    share = levels // groups
    rows = levels * fine_x
    me = me_ref[0]
    halves = block // LANES
    column = iota((sources * deep, LANES), 1)
    found = jnp.zeros((sources * deep, LANES), jnp.int32)
    for half in range(halves):
        lanes = slice(half * LANES, (half + 1) * LANES)
        used = incoming_ref[:, 4 * deep:5 * deep, lanes].reshape(sources * deep, LANES) > 0.0
        level = jnp.floor(incoming_ref[:, 5 * deep:, lanes].reshape(sources * deep, LANES) * (1.0 / plane))
        lowest = jnp.min(jnp.where(used, level, float(levels)), 1, keepdims=True).astype(jnp.int32)
        highest = jnp.max(jnp.where(used, level, -1.0), 1, keepdims=True).astype(jnp.int32)
        found = jnp.where((column == 2 * half) & (highest >= 0), lowest, found)
        found = jnp.where((column == 2 * half + 1) & (highest >= 0), highest + 2 - lowest, found)
    spans[...] = found
    fetch = pltpu.make_async_copy(spans, spans_ref, sem)
    fetch.start()
    adjoint[...] = jnp.zeros_like(adjoint)
    dep_ref[...] = jnp.zeros_like(dep_ref)
    field[rows:, :] = jnp.zeros((field.shape[0] - rows, fine_y), jnp.float32)
    for slot, part in enumerate(parts_refs):
        start = lax.rem(me + groups - slot, groups) * share
        static = sigma_ref[pl.ds(start, share)] * static_ref[pl.ds(start, share)]
        where = pl.ds(pl.multiple_of(start * fine_x, LANES), share * fine_x)
        field[where, :] = (part[...] + static).reshape(share * fine_x, fine_y)
    for shift in range(chunk):
        field_t[shift, :, rows:] = jnp.zeros((2 * fine_y, field_t.shape[2] - rows), HALF)
    after = jnp.zeros((fine_y, LANES), jnp.float32)
    lane = iota((fine_y, LANES), 1)
    for g in reversed(range(rows // LANES)):
        now = field[g * LANES:(g + 1) * LANES, :].T
        for shift in range(chunk):
            value, move = now, LANES - shift * fine_x
            if shift:
                value = jnp.where(lane < move, pltpu.roll(now, move, 1), pltpu.roll(after, move, 1))
            high, low = split_two(value)
            field_t[shift, :fine_y, g * LANES:(g + 1) * LANES] = high
            field_t[shift, fine_y:, g * LANES:(g + 1) * LANES] = low
        after = now

    fetch.wait()

    def block_of(source, at, half):
        def row(p):
            return incoming_ref[source, pl.ds(p * deep + at, 1), :][:, half * LANES:(half + 1) * LANES]

        base = row(5)
        level = jnp.floor(base * (1.0 / plane))
        rest = base - level * plane
        across = jnp.floor(rest * (1.0 / fine_y))
        along = rest - across * fine_y
        frac_x, frac_y, frac_l = row(0), row(1), row(2)
        rows_x = iota((fine_x, LANES), 0).astype(jnp.float32)
        pick_x = jnp.where(rows_x == across, 1.0 - frac_x, 0.0) + jnp.where(rows_x == across + 1.0, frac_x, 0.0)
        rows_y = iota((fine_y, LANES), 0).astype(jnp.float32)
        pick_y = jnp.where(rows_y == along, 1.0 - frac_y, 0.0) + jnp.where(rows_y == along + 1.0, frac_y, 0.0)

        def weights(bottom, reach):
            offset = level - jnp.asarray(bottom, jnp.int32).astype(jnp.float32)
            rows_l = iota((reach, LANES), 0).astype(jnp.float32)
            pick_l = jnp.where(rows_l == offset, 1.0 - frac_l, 0.0) + jnp.where(rows_l == offset + 1.0, frac_l, 0.0)
            picks = [pick_x * pick_l[g:g + 1] for g in range(reach)]
            return jnp.concatenate(split_two(jnp.concatenate(picks, 0)), 1)

        def finish(picked):
            departure = jnp.sum(picked * pick_y, 0, keepdims=True) - row(3)
            turned = jnp.concatenate(split_two((pick_y * (row(4) * departure)).T), 1)
            return departure, jnp.concatenate([turned, turned], 0)

        return weights, finish

    def look(bottom, pick):
        if isinstance(bottom, int):
            seen = dot_nn(field_t[0, :, :pick.shape[0]], pick)
        else:
            lanes = pl.ds(pl.multiple_of((bottom // chunk) * LANES, LANES), pick.shape[0])
            seen = dot_nn(field_t[lax.rem(bottom, chunk), :, lanes], pick)
        return seen[:fine_y, :LANES] + (seen[:fine_y, LANES:] + seen[fine_y:, :LANES])

    def spread(pick, term):
        both = dot_nn(pick, term)
        return both[:, :fine_y] + both[:, fine_y:]

    def rows_at(bottom, reach):
        return pl.ds(pl.multiple_of(bottom * fine_x, fine_x), reach * fine_x)

    def together(blocks, bottoms, reach):
        parts = [block_of(*block) for block in blocks]
        picks = [weights(bottom, reach) for (weights, finish), bottom in zip(parts, bottoms)]
        seen = [look(bottom, pick) for bottom, pick in zip(bottoms, picks)]
        done = [finish(value) for (weights, finish), value in zip(parts, seen)]
        adds = [spread(pick, term) for pick, (departure, term) in zip(picks, done)]
        keep(blocks, [departure for departure, term in done])
        for bottom, add in zip(bottoms, adds):
            adjoint[rows_at(bottom, reach), :] += add

    def keep(blocks, departures):
        for i in range(0, len(blocks), halves):
            source, at, half = blocks[i]
            dep_ref[source, pl.ds(at, 1), :] = jnp.concatenate(departures[i:i + halves], 1)

    step = 2 if deep % 2 == 0 else 1

    def group_of(source, at):
        blocks = [(source, at + r, half) for r in range(step) for half in range(halves)]
        numbers = [(source * deep + at + r, half) for r in range(step) for half in range(halves)]
        bottoms = [spans_ref[row, 2 * half] for row, half in numbers]
        needs = [spans_ref[row, 2 * half + 1] for row, half in numbers]
        return blocks, bottoms, functools.reduce(jnp.maximum, needs)

    def one_step(i, unused):
        at = lax.rem(i, deep // step) * step
        groups = [group_of(2 * (i // (deep // step)) + k, at) for k in range(2)]
        most = [group[2] for group in groups]
        low, high = jnp.minimum(*most), jnp.maximum(*most)
        both = (low > 0) & (high <= STEPS[0])

        @pl.when(both)
        def _():
            together(groups[0][0] + groups[1][0], groups[0][1] + groups[1][1], STEPS[0])

        @pl.when((high > 0) & jnp.logical_not(both))
        def _():
            for blocks, bottoms, needed in groups:
                for below, reach in zip((0,) + STEPS, STEPS):
                    @pl.when((needed > below) & (needed <= reach))
                    def _():
                        together(blocks, [0] * len(blocks) if reach == levels else bottoms, reach)

        return unused

    lax.fori_loop(0, sources * deep // (2 * step), one_step, 0)
    for slot, adj_ref in enumerate(adj_refs):
        start = lax.rem(me + slot, groups) * share * fine_x
        adj_ref[...] = adjoint[pl.ds(pl.multiple_of(start, LANES), share * fine_x), :].reshape(share, fine_x, fine_y)


def stencil(parts, incoming, bg_sigma, static_ctrl, me):
    levels, fine_x, fine_y = bg_sigma.shape
    sources, packed_rows, block = incoming.shape
    deep, groups = packed_rows // 6, len(parts)
    rows = levels * fine_x
    padded = rows + STEPS[-2] * fine_x

    def kernel(*refs):
        parts_end = 1 + groups
        stencil_kernel(
            refs[0], refs[1:parts_end], *refs[parts_end:parts_end + 4],
            refs[parts_end + 4:parts_end + 4 + groups], *refs[parts_end + 4 + groups:]
        )

    results = pl.pallas_call(
        kernel,
        out_shape=(jax.ShapeDtypeStruct((sources, deep, block), jnp.float32),)
        + tuple(jax.ShapeDtypeStruct(part.shape, jnp.float32) for part in parts),
        in_specs=[SMEM] + [VMEM] * (groups + 3),
        out_specs=(VMEM,) * (1 + groups),
        scratch_shapes=[
            pltpu.VMEM((padded, fine_y), jnp.float32),
            pltpu.VMEM((LANES // fine_x, 2 * fine_y, padded), HALF),
            pltpu.VMEM((padded, fine_y), jnp.float32),
            pltpu.VMEM((sources * deep, LANES), jnp.int32),
            pltpu.SMEM((sources * deep, LANES), jnp.int32),
            pltpu.SemaphoreType.DMA,
        ],
        compiler_params=room(32),
        cost_estimate=pl.CostEstimate(flops=16 << 30, bytes_accessed=1 << 20, transcendentals=0),
        name="stencil",
    )(me, *parts, bg_sigma, static_ctrl, incoming)
    return results[0], results[1:]


def unpack_kernel(target_ref, table_ref, out_ref):
    slot_rows = table_ref.shape[0]
    high, low = split_two(table_ref[...])
    both = jnp.concatenate([high.astype(jnp.float32), low.astype(jnp.float32)], 0)
    turned = both.T.astype(HALF)
    group = 4

    def some_blocks(g, unused):
        for i in range(group):
            pair = target_ref[pl.ds(2 * (g * group + i), 2), :]
            target = jnp.concatenate([pair[0:1], pair[1:2]], 1)
            rows = jnp.where(iota((slot_rows, BLOCK), 0) == (target >> 8), 1.0, 0.0).astype(HALF)
            lines = dot_nn(turned, jnp.concatenate([rows, rows], 0))
            lane = iota((BLOCK, BLOCK), 0) == (target & (BLOCK - 1))
            found = jnp.sum(jnp.where(lane, lines, 0.0), 0, keepdims=True)
            out_ref[pl.ds(2 * (g * group + i), 2), :] = jnp.concatenate([found[:, :LANES], found[:, LANES:]], 0)
        return unused

    lax.fori_loop(0, target_ref.shape[0] // (2 * group), some_blocks, 0)


def unpack(target, table):
    vmem = pl.BlockSpec(memory_space=pltpu.VMEM)
    return pl.pallas_call(
        unpack_kernel,
        out_shape=jax.ShapeDtypeStruct(target.shape, jnp.float32),
        in_specs=[vmem, vmem],
        out_specs=vmem,
        compiler_params=room(8),
        cost_estimate=pl.CostEstimate(flops=2 << 30, bytes_accessed=1 << 18, transcendentals=0),
        name="unpack",
    )(target, table).reshape(-1)


REACH = NSTEP
EDGE = 8
PAD = 2 * EDGE
SCALE = NU**NSTEP


def interpolation(shape, fine_dim, coarse_dim, shift):
    fine, coarse = iota(shape, fine_dim), iota(shape, coarse_dim) - shift
    frac = (fine % RATIO).astype(jnp.float32) * (1.0 / RATIO)
    low = jnp.where(coarse == fine // RATIO, 1.0 - frac, 0.0)
    return (low + jnp.where(coarse == fine // RATIO + 1, frac, 0.0)).astype(HALF)


def interpolation_rows(fine_x, depth, copies, transposed):
    long, short = EDGE * fine_x, EDGE * depth
    shape = (short, long) if transposed else (long, copies * short)
    fine, coarse = iota(shape, 1 if transposed else 0), iota(shape, 0 if transposed else 1)
    for copy in range(1, copies):
        coarse = jnp.where(coarse >= short, coarse - short, coarse)
    place, target = fine % fine_x, coarse // EDGE
    frac = (place % RATIO).astype(jnp.float32) * (1.0 / RATIO)
    low = jnp.where(target == place // RATIO, 1.0 - frac, 0.0)
    weight = low + jnp.where(target == place // RATIO + 1, frac, 0.0)
    return jnp.where(fine // fine_x == coarse % EDGE, weight, 0.0).astype(HALF)


def mixing(mix_ref):
    levels = mix_ref.shape[0]
    tile = jnp.where(iota((LANES, levels), 0) % levels == iota((LANES, levels), 1), 1.0, 0.0).astype(HALF)
    same = iota((LANES, LANES), 0) // levels == iota((LANES, LANES), 1) // levels
    terms = []
    for term in split_two(mix_ref[...]):
        tiled = dot_nt(dot_nn(tile, term).astype(HALF), tile)
        terms.append(jnp.where(same, tiled, 0.0).astype(HALF))
    return terms


def corner_counts(coarse_x, joined):
    above = [[j, j + 1] for j in range(REACH)]
    below = [[REACH - i, REACH + 1 - i] for i in range(REACH + 1)]
    if not joined:
        return [above, below]
    gap = [[0, 0]] * (coarse_x - REACH)
    high, low = gap + above, below + gap[1:]
    return [[[max(a, b) for a, b in zip(*pair)] for pair in zip(high, low)]]


def neighbours(field):
    width = field.shape[1]
    return pltpu.roll(field, 1, 1) + pltpu.roll(field, width - 1, 1)


def edges_kernel(strips, rows, alpha_ref, mix_ref, alpha_out, mix_out, *outs):
    coarse_y = alpha_ref.shape[1]
    alpha_out[...] = alpha_ref[...]
    mix_out[...] = mix_ref[...]
    for (begin, counts), left, right in zip(zip(rows, strips), outs[:len(strips)], outs[len(strips):]):
        at_left, at_right = 0, 0
        for i, (to_left, to_right) in enumerate(counts):
            if to_left:
                left[at_left:at_left + to_left, :] = alpha_ref[begin + i, coarse_y - to_left:, :]
            if to_right:
                right[at_right:at_right + to_right, :] = alpha_ref[begin + i, :to_right, :]
            at_left, at_right = at_left + to_left, at_right + to_right


def ensemble_kernel(
    coarse_x, coarse_y, offsets, strips,
    me_ref, alpha_ref, above_ref, below_ref,
    left_ref, left_above_ref, left_below_ref, right_ref, right_above_ref, right_below_ref,
    mix_ref, pert_hbm, out_refs, pert_ref, sem, ext, coarse,
):
    members, levels, fine_x, fine_y = pert_ref.shape
    channels = alpha_ref.shape[2]
    fetch = pltpu.make_async_copy(pert_hbm, pert_ref, sem)
    fetch.start()
    ext[:, :EDGE, :] = jnp.zeros((ext.shape[0], EDGE, channels), jnp.float32)
    ext[:, EDGE + coarse_y:, :] = jnp.zeros((ext.shape[0], EDGE, channels), jnp.float32)
    above, below = offsets
    groups = (
        (0, REACH, above, strips[1], above_ref, left_above_ref, right_above_ref),
        (REACH, coarse_x, 0, strips[0], alpha_ref, left_ref, right_ref),
        (REACH + coarse_x, REACH + 1, below, strips[-1], below_ref, left_below_ref, right_below_ref),
    )
    for begin, count, offset, counts, middle, left, right in groups:
        ext[begin:begin + count, EDGE:EDGE + coarse_y, :] = middle[offset:offset + count]
        for i in range(count):
            at_left, at_right = [sum(row[side] for row in counts[:offset + i]) for side in range(2)]
            n_left, n_right = counts[offset + i]
            if n_left:
                ext[begin + i, EDGE - n_left:EDGE, :] = left[at_left:at_left + n_left, :]
            if n_right:
                ext[begin + i, EDGE + coarse_y:EDGE + coarse_y + n_right, :] = right[at_right:at_right + n_right, :]
    spread_y = interpolation((coarse_y + PAD, fine_y), 1, 0, EDGE)
    spread_y = jnp.concatenate([spread_y, spread_y], 0)
    high, low = mixing(mix_ref)
    mix = jnp.concatenate([high, high, low], 1)

    def one_group(g, unused):
        lanes = pl.ds(pl.multiple_of(g * LANES, LANES), LANES)
        field = ext[:, :, lanes]
        for step in range(NSTEP):
            inner = field[1:-1]
            field = inner + field[2:] + field[:-2] + neighbours(inner)
        high, low = split_two(field * SCALE)
        both = jnp.concatenate([high.astype(jnp.float32), low.astype(jnp.float32)], 1)
        for c in range(coarse_x + 1):
            wide_high, wide_low = split_two(dot_nn(both[c].T.astype(HALF), spread_y))
            coarse[c, lanes, :] = dot_nn(mix, jnp.concatenate([wide_high, wide_low, wide_high], 0))
        return unused

    lax.fori_loop(0, channels // LANES, one_group, 0, unroll=True)
    fetch.wait()
    depth = coarse_x + 2
    spread_x = interpolation_rows(fine_x, depth, 2, False)
    share = levels // len(out_refs)
    unroll = math.gcd(members // 2, 10)

    for slot, out_ref in enumerate(out_refs):
        for sub in range(share // EDGE):
            first = pl.multiple_of(lax.rem(me_ref[0] + slot, len(out_refs)) * share + sub * EDGE, EDGE)

            def stacked(k):
                rows = pl.ds(pl.multiple_of(k * levels + first, EDGE), EDGE)
                parts = [coarse[c, rows, :] for c in range(coarse_x + 1)]
                return jnp.concatenate(parts + [jnp.zeros((EDGE, fine_y), jnp.float32)], 0)

            def perturbation(k):
                return pert_ref[k, pl.ds(first, EDGE)].reshape(EDGE * fine_x, fine_y).astype(jnp.float32)

            def pairs(p, total):
                for i in range(unroll):
                    k = 2 * (unroll * p + i)
                    high, low = split_two(jnp.concatenate([stacked(k), stacked(k + 1)], 1))
                    fine = dot_nn(spread_x, jnp.concatenate([high, low], 0))
                    total = total + (fine[:, :fine_y] * perturbation(k) + fine[:, fine_y:] * perturbation(k + 1))
                return total

            total = lax.fori_loop(
                0, members // (2 * unroll), pairs, jnp.zeros((EDGE * fine_x, fine_y), jnp.float32)
            )
            out_ref[sub * EDGE:(sub + 1) * EDGE] = total.reshape(EDGE, fine_x, fine_y)


def backward_kernel(
    coarse_x, coarse_y, joined, strips,
    me_ref, parts_refs, mix_ref, sigma_ref, static_ref, pert_hbm,
    grad_ref, center_ref, middle_refs, left_refs, right_refs,
    adjoint, coarse, pert_ref, sems,
):
    members, levels, fine_x, fine_y = pert_ref.shape
    channels = members * levels
    unroll = members // sems.shape[0]
    copies = []
    for p in range(sems.shape[0]):
        some = pl.ds(p * unroll, unroll)
        copies.append(pltpu.make_async_copy(pert_hbm.at[some], pert_ref.at[some], sems.at[p]))
        copies[p].start()
    share = levels // len(parts_refs)
    for slot, part in enumerate(parts_refs):
        first = lax.rem(me_ref[0] + len(parts_refs) - slot, len(parts_refs)) * share
        adjoint[pl.ds(first, share)] = part[...]
    grad_ref[...] = static_ref[...] + sigma_ref[...] * adjoint[...]
    depth = coarse_x + 2
    fold_x = interpolation_rows(fine_x, depth, 1, True)

    for p, copy in enumerate(copies):
        copy.wait()

        def one_level_group(group, unused):
            some = pl.ds(group * EDGE, EDGE)
            field = adjoint[some].reshape(EDGE * fine_x, fine_y)
            for k in range(p * unroll, (p + 1) * unroll):
                scaled = pert_ref[k, some].reshape(EDGE * fine_x, fine_y).astype(jnp.float32)
                high, low = split_two(scaled * field)
                both = dot_nn(fold_x, jnp.concatenate([high, low], 1))
                rows = pl.ds(pl.multiple_of(k * levels + group * EDGE, EDGE), EDGE)
                for c in range(coarse_x + 1):
                    piece = both[c * EDGE:(c + 1) * EDGE]
                    coarse[c, rows, :] = piece[:, :fine_y] + piece[:, fine_y:]
            return unused

        lax.fori_loop(0, levels // EDGE, one_level_group, 0)

    fold_y = interpolation((coarse_y + PAD, fine_y), 1, 0, EDGE)
    fold_y = jnp.concatenate([fold_y, fold_y], 1)
    high, low = mixing(mix_ref)
    mix = jnp.concatenate([high, high, low], 0)

    def one_group(g, unused):
        lanes = pl.ds(pl.multiple_of(g * LANES, LANES), LANES)
        rows = []
        for c in range(coarse_x + 1):
            high, low = split_two(coarse[c, lanes, :])
            narrow = dot_nt(fold_y, jnp.concatenate([high, low], 1))
            high, low = split_two(narrow)
            rows.append(dot_nn(jnp.concatenate([high, low, high], 1), mix)[None])
        field = jnp.concatenate(rows, 0) * SCALE
        empty = jnp.zeros((1,) + field.shape[1:], jnp.float32)
        for step in range(NSTEP):
            own = field + neighbours(field)
            field = jnp.concatenate([field, empty, empty], 0) + jnp.concatenate([empty, own, empty], 0) + jnp.concatenate(
                [empty, empty, field], 0
            )
        inside = field[REACH:REACH + coarse_x]
        up, down = field[:REACH], field[REACH + coarse_x:]
        if joined:
            none = jnp.zeros((coarse_x - REACH - 1,) + field.shape[1:], jnp.float32)
            outside = [jnp.concatenate([down, none], 0) + jnp.concatenate([none, empty, up], 0)]
        else:
            outside = [up, down]
        center_ref[:, :, lanes] = inside[:, EDGE:EDGE + coarse_y]
        for ref, value in zip(middle_refs, outside):
            ref[:, :, lanes] = value[:, EDGE:EDGE + coarse_y]
        for left, right, value, counts in zip(left_refs, right_refs, [inside] + outside, strips):
            at_left, at_right = 0, 0
            for i, (to_left, to_right) in enumerate(counts):
                if to_left:
                    left[at_left:at_left + to_left, lanes] = value[i, EDGE - to_left:EDGE]
                if to_right:
                    right[at_right:at_right + to_right, lanes] = value[i, EDGE + coarse_y:EDGE + coarse_y + to_right]
                at_left, at_right = at_left + to_left, at_right + to_right
        return unused

    lax.fori_loop(0, channels // LANES, one_group, 0, unroll=True)


def fold_kernel(places, alpha_ref, center_ref, *refs):
    part_refs, out_ref = refs[:-1], refs[-1]
    coarse_y = out_ref.shape[1]
    out_ref[...] = alpha_ref[...] + center_ref[...]
    for (row, counts, at_end), ref in zip(places, part_refs):
        if at_end is None:
            out_ref[row:row + counts] += ref[...]
            continue
        at = 0
        for i, count in enumerate(counts):
            if count:
                begin = coarse_y - count if at_end else 0
                out_ref[row + i, begin:begin + count, :] += ref[at:at + count, :]
            at += count


def shifted(value, by_x, by_y):
    count_x, count_y = lax.axis_size("tx"), lax.axis_size("ty")
    pairs = [
        (x * count_y + y, (x + by_x) % count_x * count_y + (y + by_y) % count_y)
        for x in range(count_x)
        for y in range(count_y)
    ]
    return lax.ppermute(value, ("tx", "ty"), pairs)


def ensemble(alpha, mix, ens_pert, me, beside):
    coarse_x, coarse_y, channels = alpha.shape
    members, levels, fine_x, fine_y = ens_pert.shape
    joined = lax.axis_size("tx") == 2
    strips = [[[REACH, REACH + 1]] * coarse_x] + corner_counts(coarse_x, joined)
    rows = [0, 0] if joined else [0, coarse_x - REACH, 0]
    shapes = [alpha.shape, mix.shape]
    shapes += [(sum(count[side] for count in counts), channels) for side in range(2) for counts in strips]
    held, mix, *sides = pl.pallas_call(
        functools.partial(edges_kernel, strips, rows),
        out_shape=tuple(jax.ShapeDtypeStruct(shape, jnp.float32) for shape in shapes),
        in_specs=[VMEM] * 2,
        out_specs=(VMEM,) * len(shapes),
        compiler_params=room(8),
        cost_estimate=pl.CostEstimate(flops=1 << 10, bytes_accessed=1 << 10, transcendentals=0),
        name="edges",
    )(alpha, mix)
    ends, starts = sides[:len(strips)], sides[len(strips):]
    if joined:
        above = below = shifted(alpha, 1, 0)
        left_above = left_below = shifted(ends[1], 1, 1)
        right_above = right_below = shifted(starts[1], 1, -1)
        offsets = (coarse_x - REACH, 0)
    else:
        above, below = shifted(alpha[coarse_x - REACH:], 1, 0), shifted(alpha[:REACH + 1], -1, 0)
        left_above, left_below = shifted(ends[1], 1, 1), shifted(ends[2], -1, 1)
        right_above, right_below = shifted(starts[1], 1, -1), shifted(starts[2], -1, -1)
        offsets = (0, 0)
    left, right = shifted(ends[0], 0, 1), shifted(starts[0], 0, -1)
    left, beside = lax.optimization_barrier((left, beside))
    groups = lax.axis_size("mem")

    def kernel(*refs):
        ensemble_kernel(coarse_x, coarse_y, offsets, strips, *refs[:12], refs[12:12 + groups], *refs[12 + groups:])

    parts = pl.pallas_call(
        kernel,
        out_shape=tuple(jax.ShapeDtypeStruct((levels // groups, fine_x, fine_y), jnp.float32) for _ in range(groups)),
        in_specs=[SMEM] + [VMEM] * 10 + [HBM],
        out_specs=(VMEM,) * groups,
        scratch_shapes=[
            pltpu.VMEM(ens_pert.shape, ens_pert.dtype),
            pltpu.SemaphoreType.DMA,
            pltpu.VMEM((coarse_x + 2 * REACH + 1, coarse_y + PAD, channels), jnp.float32),
            pltpu.VMEM((coarse_x + 1, channels, fine_y), jnp.float32),
        ],
        compiler_params=room(50),
        cost_estimate=pl.CostEstimate(flops=8 << 30, bytes_accessed=8 << 20, transcendentals=0),
        name="ensemble",
    )(me, held, above, below, left, left_above, left_below, right, right_above, right_below, mix, ens_pert)
    return parts, beside


def backward(alpha, adjoint_parts, mix, bg_sigma, static_ctrl, ens_pert, me, beside):
    coarse_x, coarse_y, channels = alpha.shape
    members, levels, fine_x, fine_y = ens_pert.shape
    joined = lax.axis_size("tx") == 2
    groups = len(adjoint_parts)
    outside = [coarse_x] if joined else [REACH, REACH + 1]
    strips = [[[REACH, REACH + 1]] * coarse_x] + corner_counts(coarse_x, joined)
    shapes = [bg_sigma.shape, alpha.shape]
    shapes += [(rows, coarse_y, channels) for rows in outside]
    shapes += [(sum(count[side] for count in counts), channels) for side in range(2) for counts in strips]
    n_in, n_mid, n_strip = 5 + groups, len(outside), len(strips)

    def kernel(*refs):
        me_ref, parts, rest = refs[0], refs[1:1 + groups], refs[1 + groups:n_in]
        outs = refs[n_in:n_in + len(shapes)]
        middle = outs[2:2 + n_mid]
        left = outs[2 + n_mid:2 + n_mid + n_strip]
        right = outs[2 + n_mid + n_strip:]
        backward_kernel(
            coarse_x, coarse_y, joined, strips, me_ref, parts, *rest,
            outs[0], outs[1], middle, left, right, *refs[n_in + len(shapes):]
        )

    results = pl.pallas_call(
        kernel,
        out_shape=tuple(jax.ShapeDtypeStruct(shape, jnp.float32) for shape in shapes),
        in_specs=[SMEM] + [VMEM] * (groups + 3) + [HBM],
        out_specs=(VMEM,) * len(shapes),
        scratch_shapes=[
            pltpu.VMEM(bg_sigma.shape, jnp.float32),
            pltpu.VMEM((coarse_x + 1, channels, fine_y), jnp.float32),
            pltpu.VMEM(ens_pert.shape, ens_pert.dtype),
            pltpu.SemaphoreType.DMA((members // math.gcd(members, 5),)),
        ],
        compiler_params=room(50),
        cost_estimate=pl.CostEstimate(flops=8 << 30, bytes_accessed=8 << 20, transcendentals=0),
        name="backward",
    )(me, *adjoint_parts, mix, bg_sigma, static_ctrl, ens_pert)
    results, beside = lax.optimization_barrier((results, beside))
    grad_static, center = results[:2]
    middle = results[2:2 + n_mid]
    left, right = results[2 + n_mid:2 + n_mid + n_strip], results[2 + n_mid + n_strip:]
    moves = [(1, 0)] if joined else [(-1, coarse_x - REACH), (1, 0)]
    places, parts = [], []
    for (by, row), value in zip(moves, middle):
        parts.append(shifted(value, by, 0))
        places.append((row, value.shape[0], None))
    for (by, row), counts, to_left, to_right in zip([(0, 0)] + moves, strips, left, right):
        parts += [shifted(to_left, by, -1), shifted(to_right, by, 1)]
        places += [(row, [count[0] for count in counts], True), (row, [count[1] for count in counts], False)]
    grad_alpha = pl.pallas_call(
        functools.partial(fold_kernel, places),
        out_shape=jax.ShapeDtypeStruct(alpha.shape, jnp.float32),
        in_specs=[VMEM] * (2 + len(parts)),
        out_specs=VMEM,
        compiler_params=room(8),
        cost_estimate=pl.CostEstimate(flops=1 << 20, bytes_accessed=2 << 20, transcendentals=0),
        name="fold",
    )(alpha, center, *parts)
    return grad_alpha, grad_static, beside


def owned_sum(parts):
    count = len(parts)
    total = parts[0]
    for d in range(1, count):
        total = total + lax.ppermute(parts[d], "mem", [(i, (i + d) % count) for i in range(count)])
    return total


def gathered(own):
    count = lax.axis_size("mem")
    return [own] + [lax.ppermute(own, "mem", [(i, (i + d) % count) for i in range(count)]) for d in range(1, count)]


def per_device(
    alpha,
    lv_sqrt,
    ens_pert,
    bg_sigma,
    static_ctrl,
    obs_owner,
    obs_column,
    obs_level,
    obs_frac,
    innovation,
    obs_rinv,
    obs_count,
):
    levels, fine_x, fine_y = bg_sigma.shape
    tiles = lax.axis_size("tx") * lax.axis_size("ty")
    capacity = 2 * obs_owner.shape[0] // tiles
    me = lax.axis_index("mem").astype(jnp.int32).reshape(1)
    rows = obs_owner.shape[0] // LANES
    ints = jnp.concatenate([obs_owner[:, 0], obs_level, obs_column]).reshape(3 * rows, LANES)
    floats = jnp.concatenate([innovation, obs_rinv]).reshape(2 * rows, LANES)
    target = ranked(tiles, levels, capacity, obs_count, ints)
    partial, target = ensemble(alpha, lv_sqrt, ens_pert, me, target)
    partial, target = lax.optimization_barrier((partial, target))
    outgoing = pack(tiles, fine_x * fine_y, capacity, target, ints, floats, obs_frac)
    incoming = lax.all_to_all(outgoing, ("tx", "ty"), split_axis=0, concat_axis=0, tiled=True)
    increment = owned_sum(partial)
    departure, adjoint = stencil(gathered(increment), incoming, bg_sigma, static_ctrl, me)
    parts, departure = lax.optimization_barrier((gathered(owned_sum(adjoint)), departure))
    returned = lax.all_to_all(departure, ("tx", "ty"), split_axis=0, concat_axis=0, tiled=True)
    grad_alpha, grad_static, returned = backward(
        alpha, parts, lv_sqrt, bg_sigma, static_ctrl, ens_pert, me, returned
    )
    departures = unpack(target, returned.reshape(-1, BLOCK))
    return (grad_alpha, grad_static, departures)


def solution(mesh):
    placed = (
        P("tx", "ty", "mem"),
        P(),
        P("mem", None, "tx", "ty"),
        P(None, "tx", "ty"),
        P(None, "tx", "ty"),
        P(("tx", "ty", "mem"), None),
        P(("tx", "ty", "mem")),
        P(("tx", "ty", "mem")),
        P(None, ("tx", "ty", "mem")),
        P(("tx", "ty", "mem")),
        P(("tx", "ty", "mem")),
        P(("tx", "ty", "mem")),
    )
    return jax.shard_map(
        per_device,
        mesh=mesh,
        in_specs=placed,
        out_specs=(P("tx", "ty", "mem"), P(None, "tx", "ty"), P(("tx", "ty", "mem"))),
        check_vma=False,
    )
```

```python
import functools
import math

import jax
import jax.numpy as jnp
from jax import lax
from jax.experimental import pallas as pl
from jax.experimental.pallas import tpu as pltpu
from jax.sharding import PartitionSpec as P

RATIO = 4
NSTEP = 4
NU = 0.2
VMEM = pl.BlockSpec(memory_space=pltpu.VMEM)
SMEM = pl.BlockSpec(memory_space=pltpu.SMEM)
HBM = pl.BlockSpec(memory_space=pltpu.HBM)


def room(mebibytes):
    return pltpu.CompilerParams(vmem_limit_bytes=mebibytes << 20)

BLOCK = 256
LANES = 128
STEPS = (8, 12, 16, 32)
HALF = jnp.bfloat16


def split_two(value):
    high = value.astype(HALF)
    return high, (value - high.astype(jnp.float32)).astype(HALF)


def dot_nt(a, b):
    return lax.dot_general(a, b, (((1,), (1,)), ((), ())), preferred_element_type=jnp.float32)


def dot_nn(a, b):
    return jnp.dot(a, b, preferred_element_type=jnp.float32)


def iota(shape, dim):
    return lax.broadcasted_iota(jnp.int32, shape, dim)


def row_of(ref, j):
    pair = ref[pl.ds(2 * j, 2), :]
    return jnp.concatenate([pair[0:1], pair[1:2]], 1)


def rank_kernel(tiles, levels, capacity, count_ref, ints_ref, target_ref, carry, total):
    size = target_ref.shape[0]
    owner_ref, level_ref = [ints_ref.at[pl.ds(i * size, size)] for i in range(2)]
    blocks = size * LANES // BLOCK
    keys = tiles * levels
    count = count_ref[0]

    def onehot(j):
        live = iota((1, BLOCK), 1) + j * BLOCK < count
        key = jnp.where(live, row_of(owner_ref, j) * levels + row_of(level_ref, j), -1)
        return live, iota((keys, BLOCK), 0) == key

    ones = jnp.ones((BLOCK, LANES), HALF)
    total[...] = jnp.zeros_like(total)

    many = math.gcd(blocks, 8)

    def count_group(g, unused):
        masks = [onehot(g * many + i)[1] for i in range(many)]
        counted = jnp.concatenate([jnp.where(mask, 1.0, 0.0).astype(HALF) for mask in masks], 1)
        total[...] += dot_nn(counted, jnp.concatenate([ones] * many, 0))
        return unused

    lax.fori_loop(0, blocks // many, count_group, 0)
    high = jnp.floor(total[...] * (1.0 / LANES))
    low = total[...] - high * LANES
    row_key, col_key = iota((keys, keys), 0), iota((keys, keys), 1)
    before = jnp.where((col_key < row_key) & (col_key // levels == row_key // levels), 1.0, 0.0).astype(HALF)
    start = dot_nn(before, high.astype(HALF)) * LANES + dot_nn(before, low.astype(HALF))
    carry[...] = start + ((iota((keys, LANES), 0) // levels) * capacity).astype(jnp.float32)

    earlier = jnp.where(iota((BLOCK, BLOCK), 0) < iota((BLOCK, BLOCK), 1), 1.0, 0.0).astype(HALF)
    prefix = jnp.concatenate([earlier, ones], 1)

    def rank_group(g, unused):
        now = carry[...]
        seen = [onehot(g * many + i) for i in range(many)]
        ranks = [dot_nn(jnp.where(mask, 1.0, 0.0).astype(HALF), prefix) for live, mask in seen]
        for i, ((live, mask), rank) in enumerate(zip(seen, ranks)):
            here = rank[:, :BLOCK] + jnp.concatenate([now] * (BLOCK // LANES), 1)
            now = now + rank[:, BLOCK:]
            slot = jnp.sum(jnp.where(mask, here, 0.0), 0, keepdims=True)
            target = jnp.where(live, slot.astype(jnp.int32), -1)
            target_ref[pl.ds(2 * (g * many + i), 2), :] = jnp.concatenate([target[:, :LANES], target[:, LANES:]], 0)
        carry[...] = now
        return unused

    lax.fori_loop(0, blocks // many, rank_group, 0)


def ranked(tiles, levels, capacity, count, ints):
    return pl.pallas_call(
        functools.partial(rank_kernel, tiles, levels, capacity),
        out_shape=jax.ShapeDtypeStruct((ints.shape[0] // 3, LANES), jnp.int32),
        in_specs=[SMEM, VMEM],
        out_specs=VMEM,
        scratch_shapes=[
            pltpu.VMEM((tiles * levels, LANES), jnp.float32),
            pltpu.VMEM((tiles * levels, LANES), jnp.float32),
        ],
        compiler_params=room(16),
        cost_estimate=pl.CostEstimate(flops=1 << 20, bytes_accessed=1 << 17, transcendentals=0),
        name="rank",
    )(count, ints)


def pack_kernel(tiles, plane, capacity, target_ref, ints_ref, floats_ref, frac_ref, out_ref, *scratch):
    gathered, left_a, right_a, left_b, right_b = scratch
    size = target_ref.shape[0]
    level_ref, column_ref = [ints_ref.at[pl.ds(i * size, size)] for i in (1, 2)]
    innov_ref, rinv_ref = [floats_ref.at[pl.ds(i * size, size)] for i in range(2)]
    blocks = size * LANES // BLOCK
    deep = capacity // BLOCK
    slot_rows = tiles * deep
    group = 4
    gathered[...] = jnp.zeros_like(gathered)

    def place(j):
        target = row_of(target_ref, j)
        rows = jnp.where(iota((slot_rows, BLOCK), 0) == (target >> 8), 1.0, 0.0).astype(HALF)
        lanes = jnp.where(iota((BLOCK, BLOCK), 0) == (target & (BLOCK - 1)), 1.0, 0.0).astype(HALF)
        column = row_of(column_ref, j)
        frac = frac_ref[:, pl.ds(pl.multiple_of(j * BLOCK, BLOCK), BLOCK)]
        terms = []
        for value in (frac[0:1], frac[1:2], frac[2:3], row_of(innov_ref, j), row_of(rinv_ref, j)):
            terms.extend(split_two(jnp.broadcast_to(value, (16, BLOCK))))
        for value in (row_of(level_ref, j), column >> 7, column & (LANES - 1)):
            terms.append(jnp.broadcast_to(value.astype(jnp.float32), (16, BLOCK)).astype(HALF))
        spread = [rows * jnp.concatenate([term] * (slot_rows // 16), 0) for term in terms]
        return jnp.concatenate(spread, 0), lanes

    def build(g, left, right):
        for i in range(group):
            lanes = slice(i * BLOCK, (i + 1) * BLOCK)
            left[:, lanes], right[:, lanes] = place(g * group + i)

    def multiply(left, right):
        gathered[...] += dot_nt(left[...], right[...])

    def scatter_pair(g, unused):
        build(2 * g + 1, left_b, right_b)
        multiply(left_a, right_a)
        build(jnp.minimum(2 * g + 2, blocks // group - 1), left_a, right_a)
        multiply(left_b, right_b)
        return unused

    build(0, left_a, right_a)
    lax.fori_loop(0, blocks // (2 * group), scatter_pair, 0)

    def part(index, tile):
        begin = index * slot_rows + tile * deep
        return gathered[begin:begin + deep, :]

    for tile in range(tiles):
        for p in range(5):
            out_ref[tile, p * deep:(p + 1) * deep, :] = part(2 * p, tile) + part(2 * p + 1, tile)
        base = part(10, tile) * plane + part(11, tile) * LANES + part(12, tile)
        out_ref[tile, 5 * deep:6 * deep, :] = base


def pack(tiles, plane, capacity, target, ints, floats, frac):
    deep = capacity // BLOCK
    rows = 13 * tiles * deep
    return pl.pallas_call(
        functools.partial(pack_kernel, tiles, plane, capacity),
        out_shape=jax.ShapeDtypeStruct((tiles, 6 * deep, BLOCK), jnp.float32),
        in_specs=[VMEM] * 4,
        out_specs=VMEM,
        scratch_shapes=[pltpu.VMEM((rows, BLOCK), jnp.float32)]
        + [pltpu.VMEM((count, 4 * BLOCK), HALF) for count in (rows, BLOCK) * 2],
        compiler_params=room(16),
        cost_estimate=pl.CostEstimate(flops=8 << 30, bytes_accessed=1 << 20, transcendentals=0),
        name="pack",
    )(target, ints, floats, frac)


def stencil_kernel(
    me_ref, parts_refs, sigma_ref, static_ref, incoming_ref,
    dep_ref, adj_refs,
    field, field_t, adjoint, spans, spans_ref, sem,
):
    levels, fine_x, fine_y = sigma_ref.shape
    sources, packed_rows, block = incoming_ref.shape
    deep = packed_rows // 6
    plane = fine_x * fine_y
    chunk = LANES // fine_x
    groups = len(parts_refs)
    share = levels // groups
    rows = levels * fine_x
    me = me_ref[0]
    halves = block // LANES
    column = iota((sources * deep, LANES), 1)
    found = jnp.zeros((sources * deep, LANES), jnp.int32)
    for half in range(halves):
        lanes = slice(half * LANES, (half + 1) * LANES)
        used = incoming_ref[:, 4 * deep:5 * deep, lanes].reshape(sources * deep, LANES) > 0.0
        level = jnp.floor(incoming_ref[:, 5 * deep:, lanes].reshape(sources * deep, LANES) * (1.0 / plane))
        lowest = jnp.min(jnp.where(used, level, float(levels)), 1, keepdims=True).astype(jnp.int32)
        highest = jnp.max(jnp.where(used, level, -1.0), 1, keepdims=True).astype(jnp.int32)
        found = jnp.where((column == 2 * half) & (highest >= 0), lowest, found)
        found = jnp.where((column == 2 * half + 1) & (highest >= 0), highest + 2 - lowest, found)
    spans[...] = found
    fetch = pltpu.make_async_copy(spans, spans_ref, sem)
    fetch.start()
    adjoint[...] = jnp.zeros_like(adjoint)
    dep_ref[...] = jnp.zeros_like(dep_ref)
    field[rows:, :] = jnp.zeros((field.shape[0] - rows, fine_y), jnp.float32)
    for slot, part in enumerate(parts_refs):
        start = lax.rem(me + groups - slot, groups) * share
        static = sigma_ref[pl.ds(start, share)] * static_ref[pl.ds(start, share)]
        where = pl.ds(pl.multiple_of(start * fine_x, LANES), share * fine_x)
        field[where, :] = (part[...] + static).reshape(share * fine_x, fine_y)
    for shift in range(chunk):
        field_t[shift, :, rows:] = jnp.zeros((2 * fine_y, field_t.shape[2] - rows), HALF)
    after = jnp.zeros((fine_y, LANES), jnp.float32)
    lane = iota((fine_y, LANES), 1)
    for g in reversed(range(rows // LANES)):
        now = field[g * LANES:(g + 1) * LANES, :].T
        for shift in range(chunk):
            value, move = now, LANES - shift * fine_x
            if shift:
                value = jnp.where(lane < move, pltpu.roll(now, move, 1), pltpu.roll(after, move, 1))
            high, low = split_two(value)
            field_t[shift, :fine_y, g * LANES:(g + 1) * LANES] = high
            field_t[shift, fine_y:, g * LANES:(g + 1) * LANES] = low
        after = now

    fetch.wait()

    def block_of(source, at, half):
        def row(p):
            return incoming_ref[source, pl.ds(p * deep + at, 1), :][:, half * LANES:(half + 1) * LANES]

        base = row(5)
        level = jnp.floor(base * (1.0 / plane))
        rest = base - level * plane
        across = jnp.floor(rest * (1.0 / fine_y))
        along = rest - across * fine_y
        frac_x, frac_y, frac_l = row(0), row(1), row(2)
        rows_x = iota((fine_x, LANES), 0).astype(jnp.float32)
        pick_x = jnp.where(rows_x == across, 1.0 - frac_x, 0.0) + jnp.where(rows_x == across + 1.0, frac_x, 0.0)
        rows_y = iota((fine_y, LANES), 0).astype(jnp.float32)
        pick_y = jnp.where(rows_y == along, 1.0 - frac_y, 0.0) + jnp.where(rows_y == along + 1.0, frac_y, 0.0)

        def weights(bottom, reach):
            offset = level - jnp.asarray(bottom, jnp.int32).astype(jnp.float32)
            rows_l = iota((reach, LANES), 0).astype(jnp.float32)
            pick_l = jnp.where(rows_l == offset, 1.0 - frac_l, 0.0) + jnp.where(rows_l == offset + 1.0, frac_l, 0.0)
            picks = [pick_x * pick_l[g:g + 1] for g in range(reach)]
            return jnp.concatenate(split_two(jnp.concatenate(picks, 0)), 1)

        def finish(picked):
            departure = jnp.sum(picked * pick_y, 0, keepdims=True) - row(3)
            turned = jnp.concatenate(split_two((pick_y * (row(4) * departure)).T), 1)
            return departure, jnp.concatenate([turned, turned], 0)

        return weights, finish

    def look(bottom, pick):
        if isinstance(bottom, int):
            seen = dot_nn(field_t[0, :, :pick.shape[0]], pick)
        else:
            lanes = pl.ds(pl.multiple_of((bottom // chunk) * LANES, LANES), pick.shape[0])
            seen = dot_nn(field_t[lax.rem(bottom, chunk), :, lanes], pick)
        return seen[:fine_y, :LANES] + (seen[:fine_y, LANES:] + seen[fine_y:, :LANES])

    def spread(pick, term):
        both = dot_nn(pick, term)
        return both[:, :fine_y] + both[:, fine_y:]

    def rows_at(bottom, reach):
        return pl.ds(pl.multiple_of(bottom * fine_x, fine_x), reach * fine_x)

    def together(blocks, bottoms, reach):
        parts = [block_of(*block) for block in blocks]
        picks = [weights(bottom, reach) for (weights, finish), bottom in zip(parts, bottoms)]
        seen = [look(bottom, pick) for bottom, pick in zip(bottoms, picks)]
        done = [finish(value) for (weights, finish), value in zip(parts, seen)]
        adds = [spread(pick, term) for pick, (departure, term) in zip(picks, done)]
        keep(blocks, [departure for departure, term in done])
        for bottom, add in zip(bottoms, adds):
            adjoint[rows_at(bottom, reach), :] += add

    def keep(blocks, departures):
        for i in range(0, len(blocks), halves):
            source, at, half = blocks[i]
            dep_ref[source, pl.ds(at, 1), :] = jnp.concatenate(departures[i:i + halves], 1)

    step = 2 if deep % 2 == 0 else 1

    def group_of(source, at):
        blocks = [(source, at + r, half) for r in range(step) for half in range(halves)]
        numbers = [(source * deep + at + r, half) for r in range(step) for half in range(halves)]
        bottoms = [spans_ref[row, 2 * half] for row, half in numbers]
        needs = [spans_ref[row, 2 * half + 1] for row, half in numbers]
        return blocks, bottoms, functools.reduce(jnp.maximum, needs)

    def one_step(i, unused):
        at = lax.rem(i, deep // step) * step
        groups = [group_of(2 * (i // (deep // step)) + k, at) for k in range(2)]
        most = [group[2] for group in groups]
        low, high = jnp.minimum(*most), jnp.maximum(*most)
        both = (low > 0) & (high <= STEPS[1])
        for below, reach in zip((0, STEPS[0]), STEPS[:2]):
            @pl.when(both & (high > below) & (high <= reach))
            def _():
                together(groups[0][0] + groups[1][0], groups[0][1] + groups[1][1], reach)

        @pl.when((high > 0) & jnp.logical_not(both))
        def _():
            for blocks, bottoms, needed in groups:
                for below, reach in zip((0,) + STEPS, STEPS):
                    @pl.when((needed > below) & (needed <= reach))
                    def _():
                        together(blocks, [0] * len(blocks) if reach == levels else bottoms, reach)

        return unused

    lax.fori_loop(0, sources * deep // (2 * step), one_step, 0)
    for slot, adj_ref in enumerate(adj_refs):
        start = lax.rem(me + slot, groups) * share * fine_x
        adj_ref[...] = adjoint[pl.ds(pl.multiple_of(start, LANES), share * fine_x), :].reshape(share, fine_x, fine_y)


def stencil(parts, incoming, bg_sigma, static_ctrl, me):
    levels, fine_x, fine_y = bg_sigma.shape
    sources, packed_rows, block = incoming.shape
    deep, groups = packed_rows // 6, len(parts)
    rows = levels * fine_x
    padded = rows + STEPS[-2] * fine_x

    def kernel(*refs):
        parts_end = 1 + groups
        stencil_kernel(
            refs[0], refs[1:parts_end], *refs[parts_end:parts_end + 4],
            refs[parts_end + 4:parts_end + 4 + groups], *refs[parts_end + 4 + groups:]
        )

    results = pl.pallas_call(
        kernel,
        out_shape=(jax.ShapeDtypeStruct((sources, deep, block), jnp.float32),)
        + tuple(jax.ShapeDtypeStruct(part.shape, jnp.float32) for part in parts),
        in_specs=[SMEM] + [VMEM] * (groups + 3),
        out_specs=(VMEM,) * (1 + groups),
        scratch_shapes=[
            pltpu.VMEM((padded, fine_y), jnp.float32),
            pltpu.VMEM((LANES // fine_x, 2 * fine_y, padded), HALF),
            pltpu.VMEM((padded, fine_y), jnp.float32),
            pltpu.VMEM((sources * deep, LANES), jnp.int32),
            pltpu.SMEM((sources * deep, LANES), jnp.int32),
            pltpu.SemaphoreType.DMA,
        ],
        compiler_params=room(32),
        cost_estimate=pl.CostEstimate(flops=16 << 30, bytes_accessed=1 << 20, transcendentals=0),
        name="stencil",
    )(me, *parts, bg_sigma, static_ctrl, incoming)
    return results[0], results[1:]


def unpack_kernel(target_ref, table_ref, out_ref):
    slot_rows = table_ref.shape[0]
    high, low = split_two(table_ref[...])
    both = jnp.concatenate([high.astype(jnp.float32), low.astype(jnp.float32)], 0)
    turned = both.T.astype(HALF)
    group = 4

    def some_blocks(g, unused):
        for i in range(group):
            pair = target_ref[pl.ds(2 * (g * group + i), 2), :]
            target = jnp.concatenate([pair[0:1], pair[1:2]], 1)
            rows = jnp.where(iota((slot_rows, BLOCK), 0) == (target >> 8), 1.0, 0.0).astype(HALF)
            lines = dot_nn(turned, jnp.concatenate([rows, rows], 0))
            lane = iota((BLOCK, BLOCK), 0) == (target & (BLOCK - 1))
            found = jnp.sum(jnp.where(lane, lines, 0.0), 0, keepdims=True)
            out_ref[pl.ds(2 * (g * group + i), 2), :] = jnp.concatenate([found[:, :LANES], found[:, LANES:]], 0)
        return unused

    lax.fori_loop(0, target_ref.shape[0] // (2 * group), some_blocks, 0)


def unpack(target, table):
    vmem = pl.BlockSpec(memory_space=pltpu.VMEM)
    return pl.pallas_call(
        unpack_kernel,
        out_shape=jax.ShapeDtypeStruct(target.shape, jnp.float32),
        in_specs=[vmem, vmem],
        out_specs=vmem,
        compiler_params=room(8),
        cost_estimate=pl.CostEstimate(flops=2 << 30, bytes_accessed=1 << 18, transcendentals=0),
        name="unpack",
    )(target, table).reshape(-1)


REACH = NSTEP
EDGE = 8
PAD = 2 * EDGE
SCALE = NU**NSTEP


def interpolation(shape, fine_dim, coarse_dim, shift):
    fine, coarse = iota(shape, fine_dim), iota(shape, coarse_dim) - shift
    frac = (fine % RATIO).astype(jnp.float32) * (1.0 / RATIO)
    low = jnp.where(coarse == fine // RATIO, 1.0 - frac, 0.0)
    return (low + jnp.where(coarse == fine // RATIO + 1, frac, 0.0)).astype(HALF)


def interpolation_rows(fine_x, depth, copies, transposed):
    long, short = EDGE * fine_x, EDGE * depth
    shape = (short, long) if transposed else (long, copies * short)
    fine, coarse = iota(shape, 1 if transposed else 0), iota(shape, 0 if transposed else 1)
    for copy in range(1, copies):
        coarse = jnp.where(coarse >= short, coarse - short, coarse)
    place, target = fine % fine_x, coarse // EDGE
    frac = (place % RATIO).astype(jnp.float32) * (1.0 / RATIO)
    low = jnp.where(target == place // RATIO, 1.0 - frac, 0.0)
    weight = low + jnp.where(target == place // RATIO + 1, frac, 0.0)
    return jnp.where(fine // fine_x == coarse % EDGE, weight, 0.0).astype(HALF)


def mixing(mix_ref):
    levels = mix_ref.shape[0]
    tile = jnp.where(iota((LANES, levels), 0) % levels == iota((LANES, levels), 1), 1.0, 0.0).astype(HALF)
    same = iota((LANES, LANES), 0) // levels == iota((LANES, LANES), 1) // levels
    terms = []
    for term in split_two(mix_ref[...]):
        tiled = dot_nt(dot_nn(tile, term).astype(HALF), tile)
        terms.append(jnp.where(same, tiled, 0.0).astype(HALF))
    return terms


def corner_counts(coarse_x, joined):
    above = [[j, j + 1] for j in range(REACH)]
    below = [[REACH - i, REACH + 1 - i] for i in range(REACH + 1)]
    if not joined:
        return [above, below]
    gap = [[0, 0]] * (coarse_x - REACH)
    high, low = gap + above, below + gap[1:]
    return [[[max(a, b) for a, b in zip(*pair)] for pair in zip(high, low)]]


def neighbours(field):
    width = field.shape[1]
    return pltpu.roll(field, 1, 1) + pltpu.roll(field, width - 1, 1)


def edges_kernel(strips, rows, alpha_ref, mix_ref, alpha_out, mix_out, *outs):
    coarse_y = alpha_ref.shape[1]
    alpha_out[...] = alpha_ref[...]
    mix_out[...] = mix_ref[...]
    for (begin, counts), left, right in zip(zip(rows, strips), outs[:len(strips)], outs[len(strips):]):
        at_left, at_right = 0, 0
        for i, (to_left, to_right) in enumerate(counts):
            if to_left:
                left[at_left:at_left + to_left, :] = alpha_ref[begin + i, coarse_y - to_left:, :]
            if to_right:
                right[at_right:at_right + to_right, :] = alpha_ref[begin + i, :to_right, :]
            at_left, at_right = at_left + to_left, at_right + to_right


def ensemble_kernel(
    coarse_x, coarse_y, offsets, strips,
    me_ref, alpha_ref, above_ref, below_ref,
    left_ref, left_above_ref, left_below_ref, right_ref, right_above_ref, right_below_ref,
    mix_ref, pert_hbm, out_refs, pert_ref, sem, ext, coarse,
):
    members, levels, fine_x, fine_y = pert_ref.shape
    channels = alpha_ref.shape[2]
    fetch = pltpu.make_async_copy(pert_hbm, pert_ref, sem)
    fetch.start()
    ext[:, :EDGE, :] = jnp.zeros((ext.shape[0], EDGE, channels), jnp.float32)
    ext[:, EDGE + coarse_y:, :] = jnp.zeros((ext.shape[0], EDGE, channels), jnp.float32)
    above, below = offsets
    groups = (
        (0, REACH, above, strips[1], above_ref, left_above_ref, right_above_ref),
        (REACH, coarse_x, 0, strips[0], alpha_ref, left_ref, right_ref),
        (REACH + coarse_x, REACH + 1, below, strips[-1], below_ref, left_below_ref, right_below_ref),
    )
    for begin, count, offset, counts, middle, left, right in groups:
        ext[begin:begin + count, EDGE:EDGE + coarse_y, :] = middle[offset:offset + count]
        for i in range(count):
            at_left, at_right = [sum(row[side] for row in counts[:offset + i]) for side in range(2)]
            n_left, n_right = counts[offset + i]
            if n_left:
                ext[begin + i, EDGE - n_left:EDGE, :] = left[at_left:at_left + n_left, :]
            if n_right:
                ext[begin + i, EDGE + coarse_y:EDGE + coarse_y + n_right, :] = right[at_right:at_right + n_right, :]
    spread_y = interpolation((coarse_y + PAD, fine_y), 1, 0, EDGE)
    spread_y = jnp.concatenate([spread_y, spread_y], 0)
    high, low = mixing(mix_ref)
    mix = jnp.concatenate([high, high, low], 1)

    def one_group(g, unused):
        lanes = pl.ds(pl.multiple_of(g * LANES, LANES), LANES)
        field = ext[:, :, lanes]
        for step in range(NSTEP):
            inner = field[1:-1]
            field = inner + field[2:] + field[:-2] + neighbours(inner)
        high, low = split_two(field * SCALE)
        both = jnp.concatenate([high.astype(jnp.float32), low.astype(jnp.float32)], 1)
        for c in range(coarse_x + 1):
            wide_high, wide_low = split_two(dot_nn(both[c].T.astype(HALF), spread_y))
            coarse[c, lanes, :] = dot_nn(mix, jnp.concatenate([wide_high, wide_low, wide_high], 0))
        return unused

    lax.fori_loop(0, channels // LANES, one_group, 0, unroll=True)
    fetch.wait()
    depth = coarse_x + 2
    spread_x = interpolation_rows(fine_x, depth, 2, False)
    share = levels // len(out_refs)
    unroll = math.gcd(members // 2, 10)

    for slot, out_ref in enumerate(out_refs):
        for sub in range(share // EDGE):
            first = pl.multiple_of(lax.rem(me_ref[0] + slot, len(out_refs)) * share + sub * EDGE, EDGE)

            def stacked(k):
                rows = pl.ds(pl.multiple_of(k * levels + first, EDGE), EDGE)
                parts = [coarse[c, rows, :] for c in range(coarse_x + 1)]
                return jnp.concatenate(parts + [jnp.zeros((EDGE, fine_y), jnp.float32)], 0)

            def perturbation(k):
                return pert_ref[k, pl.ds(first, EDGE)].reshape(EDGE * fine_x, fine_y).astype(jnp.float32)

            def pairs(p, total):
                for i in range(unroll):
                    k = 2 * (unroll * p + i)
                    high, low = split_two(jnp.concatenate([stacked(k), stacked(k + 1)], 1))
                    fine = dot_nn(spread_x, jnp.concatenate([high, low], 0))
                    total = total + (fine[:, :fine_y] * perturbation(k) + fine[:, fine_y:] * perturbation(k + 1))
                return total

            total = lax.fori_loop(
                0, members // (2 * unroll), pairs, jnp.zeros((EDGE * fine_x, fine_y), jnp.float32)
            )
            out_ref[sub * EDGE:(sub + 1) * EDGE] = total.reshape(EDGE, fine_x, fine_y)


def backward_kernel(
    coarse_x, coarse_y, joined, strips,
    me_ref, parts_refs, mix_ref, sigma_ref, static_ref, pert_hbm,
    grad_ref, center_ref, middle_refs, left_refs, right_refs,
    adjoint, coarse, pert_ref, sems,
):
    members, levels, fine_x, fine_y = pert_ref.shape
    channels = members * levels
    unroll = members // sems.shape[0]
    copies = []
    for p in range(sems.shape[0]):
        some = pl.ds(p * unroll, unroll)
        copies.append(pltpu.make_async_copy(pert_hbm.at[some], pert_ref.at[some], sems.at[p]))
        copies[p].start()
    share = levels // len(parts_refs)
    for slot, part in enumerate(parts_refs):
        first = lax.rem(me_ref[0] + len(parts_refs) - slot, len(parts_refs)) * share
        adjoint[pl.ds(first, share)] = part[...]
    grad_ref[...] = static_ref[...] + sigma_ref[...] * adjoint[...]
    depth = coarse_x + 2
    fold_x = interpolation_rows(fine_x, depth, 1, True)

    for p, copy in enumerate(copies):
        copy.wait()

        def one_level_group(group):
            some = pl.ds(group * EDGE, EDGE)
            field = adjoint[some].reshape(EDGE * fine_x, fine_y)
            for k in range(p * unroll, (p + 1) * unroll):
                scaled = pert_ref[k, some].reshape(EDGE * fine_x, fine_y).astype(jnp.float32)
                high, low = split_two(scaled * field)
                both = dot_nn(fold_x, jnp.concatenate([high, low], 1))
                rows = pl.ds(pl.multiple_of(k * levels + group * EDGE, EDGE), EDGE)
                for c in range(coarse_x + 1):
                    piece = both[c * EDGE:(c + 1) * EDGE]
                    coarse[c, rows, :] = piece[:, :fine_y] + piece[:, fine_y:]

        def two_level_groups(i, unused):
            one_level_group(2 * i)
            one_level_group(2 * i + 1)
            return unused

        lax.fori_loop(0, levels // (2 * EDGE), two_level_groups, 0)

    fold_y = interpolation((coarse_y + PAD, fine_y), 1, 0, EDGE)
    fold_y = jnp.concatenate([fold_y, fold_y], 1)
    high, low = mixing(mix_ref)
    mix = jnp.concatenate([high, high, low], 0)

    def one_group(g, unused):
        lanes = pl.ds(pl.multiple_of(g * LANES, LANES), LANES)
        rows = []
        for c in range(coarse_x + 1):
            high, low = split_two(coarse[c, lanes, :])
            narrow = dot_nt(fold_y, jnp.concatenate([high, low], 1))
            high, low = split_two(narrow)
            rows.append(dot_nn(jnp.concatenate([high, low, high], 1), mix)[None])
        field = jnp.concatenate(rows, 0) * SCALE
        empty = jnp.zeros((1,) + field.shape[1:], jnp.float32)
        for step in range(NSTEP):
            own = field + neighbours(field)
            field = jnp.concatenate([field, empty, empty], 0) + jnp.concatenate([empty, own, empty], 0) + jnp.concatenate(
                [empty, empty, field], 0
            )
        inside = field[REACH:REACH + coarse_x]
        up, down = field[:REACH], field[REACH + coarse_x:]
        if joined:
            none = jnp.zeros((coarse_x - REACH - 1,) + field.shape[1:], jnp.float32)
            outside = [jnp.concatenate([down, none], 0) + jnp.concatenate([none, empty, up], 0)]
        else:
            outside = [up, down]
        center_ref[:, :, lanes] = inside[:, EDGE:EDGE + coarse_y]
        for ref, value in zip(middle_refs, outside):
            ref[:, :, lanes] = value[:, EDGE:EDGE + coarse_y]
        for left, right, value, counts in zip(left_refs, right_refs, [inside] + outside, strips):
            at_left, at_right = 0, 0
            for i, (to_left, to_right) in enumerate(counts):
                if to_left:
                    left[at_left:at_left + to_left, lanes] = value[i, EDGE - to_left:EDGE]
                if to_right:
                    right[at_right:at_right + to_right, lanes] = value[i, EDGE + coarse_y:EDGE + coarse_y + to_right]
                at_left, at_right = at_left + to_left, at_right + to_right
        return unused

    lax.fori_loop(0, channels // LANES, one_group, 0, unroll=True)


def fold_kernel(places, alpha_ref, center_ref, *refs):
    part_refs, out_ref = refs[:-1], refs[-1]
    coarse_y = out_ref.shape[1]
    out_ref[...] = alpha_ref[...] + center_ref[...]
    for (row, counts, at_end), ref in zip(places, part_refs):
        if at_end is None:
            out_ref[row:row + counts] += ref[...]
            continue
        at = 0
        for i, count in enumerate(counts):
            if count:
                begin = coarse_y - count if at_end else 0
                out_ref[row + i, begin:begin + count, :] += ref[at:at + count, :]
            at += count


def shifted(value, by_x, by_y):
    count_x, count_y = lax.axis_size("tx"), lax.axis_size("ty")
    pairs = [
        (x * count_y + y, (x + by_x) % count_x * count_y + (y + by_y) % count_y)
        for x in range(count_x)
        for y in range(count_y)
    ]
    return lax.ppermute(value, ("tx", "ty"), pairs)


def ensemble(alpha, mix, ens_pert, me, beside):
    coarse_x, coarse_y, channels = alpha.shape
    members, levels, fine_x, fine_y = ens_pert.shape
    joined = lax.axis_size("tx") == 2
    strips = [[[REACH, REACH + 1]] * coarse_x] + corner_counts(coarse_x, joined)
    rows = [0, 0] if joined else [0, coarse_x - REACH, 0]
    shapes = [alpha.shape, mix.shape]
    shapes += [(sum(count[side] for count in counts), channels) for side in range(2) for counts in strips]
    held, mix, *sides = pl.pallas_call(
        functools.partial(edges_kernel, strips, rows),
        out_shape=tuple(jax.ShapeDtypeStruct(shape, jnp.float32) for shape in shapes),
        in_specs=[VMEM] * 2,
        out_specs=(VMEM,) * len(shapes),
        compiler_params=room(8),
        cost_estimate=pl.CostEstimate(flops=1 << 10, bytes_accessed=1 << 10, transcendentals=0),
        name="edges",
    )(alpha, mix)
    ends, starts = sides[:len(strips)], sides[len(strips):]
    if joined:
        above = below = shifted(alpha, 1, 0)
        left_above = left_below = shifted(ends[1], 1, 1)
        right_above = right_below = shifted(starts[1], 1, -1)
        offsets = (coarse_x - REACH, 0)
    else:
        above, below = shifted(alpha[coarse_x - REACH:], 1, 0), shifted(alpha[:REACH + 1], -1, 0)
        left_above, left_below = shifted(ends[1], 1, 1), shifted(ends[2], -1, 1)
        right_above, right_below = shifted(starts[1], 1, -1), shifted(starts[2], -1, -1)
        offsets = (0, 0)
    left, right = shifted(ends[0], 0, 1), shifted(starts[0], 0, -1)
    left, beside = lax.optimization_barrier((left, beside))
    groups = lax.axis_size("mem")

    def kernel(*refs):
        ensemble_kernel(coarse_x, coarse_y, offsets, strips, *refs[:12], refs[12:12 + groups], *refs[12 + groups:])

    parts = pl.pallas_call(
        kernel,
        out_shape=tuple(jax.ShapeDtypeStruct((levels // groups, fine_x, fine_y), jnp.float32) for _ in range(groups)),
        in_specs=[SMEM] + [VMEM] * 10 + [HBM],
        out_specs=(VMEM,) * groups,
        scratch_shapes=[
            pltpu.VMEM(ens_pert.shape, ens_pert.dtype),
            pltpu.SemaphoreType.DMA,
            pltpu.VMEM((coarse_x + 2 * REACH + 1, coarse_y + PAD, channels), jnp.float32),
            pltpu.VMEM((coarse_x + 1, channels, fine_y), jnp.float32),
        ],
        compiler_params=room(50),
        cost_estimate=pl.CostEstimate(flops=8 << 30, bytes_accessed=8 << 20, transcendentals=0),
        name="ensemble",
    )(me, held, above, below, left, left_above, left_below, right, right_above, right_below, mix, ens_pert)
    return parts, beside


def backward(alpha, adjoint_parts, mix, bg_sigma, static_ctrl, ens_pert, me, beside):
    coarse_x, coarse_y, channels = alpha.shape
    members, levels, fine_x, fine_y = ens_pert.shape
    joined = lax.axis_size("tx") == 2
    groups = len(adjoint_parts)
    outside = [coarse_x] if joined else [REACH, REACH + 1]
    strips = [[[REACH, REACH + 1]] * coarse_x] + corner_counts(coarse_x, joined)
    shapes = [bg_sigma.shape, alpha.shape]
    shapes += [(rows, coarse_y, channels) for rows in outside]
    shapes += [(sum(count[side] for count in counts), channels) for side in range(2) for counts in strips]
    n_in, n_mid, n_strip = 5 + groups, len(outside), len(strips)

    def kernel(*refs):
        me_ref, parts, rest = refs[0], refs[1:1 + groups], refs[1 + groups:n_in]
        outs = refs[n_in:n_in + len(shapes)]
        middle = outs[2:2 + n_mid]
        left = outs[2 + n_mid:2 + n_mid + n_strip]
        right = outs[2 + n_mid + n_strip:]
        backward_kernel(
            coarse_x, coarse_y, joined, strips, me_ref, parts, *rest,
            outs[0], outs[1], middle, left, right, *refs[n_in + len(shapes):]
        )

    results = pl.pallas_call(
        kernel,
        out_shape=tuple(jax.ShapeDtypeStruct(shape, jnp.float32) for shape in shapes),
        in_specs=[SMEM] + [VMEM] * (groups + 3) + [HBM],
        out_specs=(VMEM,) * len(shapes),
        scratch_shapes=[
            pltpu.VMEM(bg_sigma.shape, jnp.float32),
            pltpu.VMEM((coarse_x + 1, channels, fine_y), jnp.float32),
            pltpu.VMEM(ens_pert.shape, ens_pert.dtype),
            pltpu.SemaphoreType.DMA((members // math.gcd(members, 5),)),
        ],
        compiler_params=room(50),
        cost_estimate=pl.CostEstimate(flops=8 << 30, bytes_accessed=8 << 20, transcendentals=0),
        name="backward",
    )(me, *adjoint_parts, mix, bg_sigma, static_ctrl, ens_pert)
    results, beside = lax.optimization_barrier((results, beside))
    grad_static, center = results[:2]
    middle = results[2:2 + n_mid]
    left, right = results[2 + n_mid:2 + n_mid + n_strip], results[2 + n_mid + n_strip:]
    moves = [(1, 0)] if joined else [(-1, coarse_x - REACH), (1, 0)]
    places, parts = [], []
    for (by, row), value in zip(moves, middle):
        parts.append(shifted(value, by, 0))
        places.append((row, value.shape[0], None))
    for (by, row), counts, to_left, to_right in zip([(0, 0)] + moves, strips, left, right):
        parts += [shifted(to_left, by, -1), shifted(to_right, by, 1)]
        places += [(row, [count[0] for count in counts], True), (row, [count[1] for count in counts], False)]
    grad_alpha = pl.pallas_call(
        functools.partial(fold_kernel, places),
        out_shape=jax.ShapeDtypeStruct(alpha.shape, jnp.float32),
        in_specs=[VMEM] * (2 + len(parts)),
        out_specs=VMEM,
        compiler_params=room(8),
        cost_estimate=pl.CostEstimate(flops=1 << 20, bytes_accessed=2 << 20, transcendentals=0),
        name="fold",
    )(alpha, center, *parts)
    return grad_alpha, grad_static, beside


def owned_sum(parts):
    count = len(parts)
    total = parts[0]
    for d in range(1, count):
        total = total + lax.ppermute(parts[d], "mem", [(i, (i + d) % count) for i in range(count)])
    return total


def gathered(own):
    count = lax.axis_size("mem")
    return [own] + [lax.ppermute(own, "mem", [(i, (i + d) % count) for i in range(count)]) for d in range(1, count)]


def per_device(
    alpha,
    lv_sqrt,
    ens_pert,
    bg_sigma,
    static_ctrl,
    obs_owner,
    obs_column,
    obs_level,
    obs_frac,
    innovation,
    obs_rinv,
    obs_count,
):
    levels, fine_x, fine_y = bg_sigma.shape
    tiles = lax.axis_size("tx") * lax.axis_size("ty")
    capacity = 2 * obs_owner.shape[0] // tiles
    me = lax.axis_index("mem").astype(jnp.int32).reshape(1)
    rows = obs_owner.shape[0] // LANES
    ints = jnp.concatenate([obs_owner[:, 0], obs_level, obs_column]).reshape(3 * rows, LANES)
    floats = jnp.concatenate([innovation, obs_rinv]).reshape(2 * rows, LANES)
    target = ranked(tiles, levels, capacity, obs_count, ints)
    partial, target = ensemble(alpha, lv_sqrt, ens_pert, me, target)
    partial, target = lax.optimization_barrier((partial, target))
    outgoing = pack(tiles, fine_x * fine_y, capacity, target, ints, floats, obs_frac)
    incoming = lax.all_to_all(outgoing, ("tx", "ty"), split_axis=0, concat_axis=0, tiled=True)
    increment = owned_sum(partial)
    departure, adjoint = stencil(gathered(increment), incoming, bg_sigma, static_ctrl, me)
    parts, departure = lax.optimization_barrier((gathered(owned_sum(adjoint)), departure))
    returned = lax.all_to_all(departure, ("tx", "ty"), split_axis=0, concat_axis=0, tiled=True)
    grad_alpha, grad_static, returned = backward(
        alpha, parts, lv_sqrt, bg_sigma, static_ctrl, ens_pert, me, returned
    )
    departures = unpack(target, returned.reshape(-1, BLOCK))
    return (grad_alpha, grad_static, departures)


def solution(mesh):
    placed = (
        P("tx", "ty", "mem"),
        P(),
        P("mem", None, "tx", "ty"),
        P(None, "tx", "ty"),
        P(None, "tx", "ty"),
        P(("tx", "ty", "mem"), None),
        P(("tx", "ty", "mem")),
        P(("tx", "ty", "mem")),
        P(None, ("tx", "ty", "mem")),
        P(("tx", "ty", "mem")),
        P(("tx", "ty", "mem")),
        P(("tx", "ty", "mem")),
    )
    return jax.shard_map(
        per_device,
        mesh=mesh,
        in_specs=placed,
        out_specs=(P("tx", "ty", "mem"), P(None, "tx", "ty"), P(("tx", "ty", "mem"))),
        check_vma=False,
    )
```
